256 devices in a mesh: rep: 4 (over y), seq: 64 (over x, z, core).
Axes of the slice: x: 4, y: 4, z: 8, core: 2. Of those that a mesh axis runs over, the one named last changes fastest.
Arguments:
- coarse_input: bfloat16 [4, 8192, 1536], P('rep', 'seq'), may hold values from -6 to 6
- skip_input: bfloat16 [4, 16384, 1536], P('rep', 'seq'), may hold values from -6 to 6
- depth_kernel: float32 [3, 1536], replicated, may hold values from -3 to 3
- head_weight: bfloat16 [1536, 4096], P(None, 'rep'), may hold values from -0.15625 to 0.15625
- head_bias: float32 [4096], P('rep'), may hold values from 0.5 to 2
- coverage: bfloat16 [4, 16384, 4096], P(None, 'seq', 'rep'), may hold values from 0 to 160, as said below
Outputs:
- loss_value: float32 [], replicated
- weight_grad: float32 [1536, 4096], P('seq', 'rep')
- skip_grad: bfloat16 [4, 16384, 1536], P('rep', 'seq')
The draws below stay inside these ranges and needn't reach their ends.
Inputs may be any that keep to these rules, and one draw needn't show every extreme that they name: Nonnegative coverage.
All inputs are finite; a program needn't handle non-finite values.
Results may differ from the reference program's by a relative error of at most 0.0065.
Values may be sent and summed in bfloat16 or wider, within the bound.
No kernel may reach another device: no remote copies, remote signals or barrier semaphores. Data moves between devices by JAX's collectives and lax.ppermute only.
A program may use at most 128 MiB of HBM per device.

```python
import math
import jax
import jax.numpy as jnp
from jax import lax

C = 1536
TR = 4096
SEQS = 4
BINS = 16384


def draw_coverage(key, part):
    key = jax.random.fold_in(key, 11)
    track_key, rough_key = jax.random.split(key)
    track_scale = jnp.exp(jax.random.uniform(track_key, (TR,), jnp.float32, 0.0, math.log(10.0)))
    position = jnp.arange(BINS, dtype=jnp.float32) / max(BINS - 1, 1)
    ramp = 1.0 + 2.0 * position
    rough = jnp.exp(jax.random.uniform(rough_key, (SEQS, BINS, TR), jnp.float32, math.log(0.25), math.log(4.0)))
    values = track_scale[None, None, :] * ramp[None, :, None] * rough
    return values.astype(jnp.bfloat16)


def levels(own_key, dims, cuts, low, high):
    level = 1.0
    for dim, shards_of in cuts:
        draws = jax.random.uniform(jax.random.fold_in(jax.random.fold_in(own_key, 6), dim), (shards_of,), jnp.float32, low / len(cuts), high / len(cuts))
        level = level * jnp.repeat(jnp.exp(draws), dims[dim] // shards_of).reshape((-1,) + (1,) * (len(dims) - 1 - dim))
    return level


def centred(key, extent, deviation, bound, cuts=(), kind=jnp.bfloat16):
    loudness = levels(key, extent, cuts, -0.22, 0.18) if cuts else 1.0
    drawn = jax.random.normal(key, extent, jnp.float32) * deviation * loudness
    return jnp.minimum(jnp.maximum(drawn, -bound), bound).astype(kind)


def setup_inputs(seed: int = 0) -> dict:
    keys = jax.random.split(jax.random.key(seed), 7)
    return {
        "coarse_input": centred(keys[0], (SEQS, BINS // 2, C), 1.0, 6.0, ((0, 4), (1, 64))),
        "skip_input": centred(keys[1], (SEQS, BINS, C), 1.0, 6.0, ((0, 4), (1, 64))),
        "depth_kernel": centred(keys[2], (3, C), 0.6, 3.0, (), jnp.float32),
        "head_weight": centred(keys[3], (C, TR), C ** -0.5, 0.15625, ((1, 4),)),
        "head_bias": jnp.clip(0.5 + 1.5 * jax.random.uniform(keys[4], (TR,), jnp.float32) ** levels(keys[4], (TR,), ((0, 4),), -0.2, 0.2), 0.5, 2.0),
        "coverage": draw_coverage(jax.random.fold_in(keys[6], 71), 0),
    }


loss_scale = 4194304.0
total_weight = 0.2

def reference(coarse_input, skip_input, depth_kernel, head_weight, head_bias, coverage):
    denominator = SEQS * TR * BINS
    factor = loss_scale / denominator

    def one_sequence(carry, items):
        grad_sum, loss_sum = carry
        coarse, skipped, counts = items
        mixed = (jnp.repeat(coarse.astype(jnp.float32), 2, axis=0) + skipped.astype(jnp.float32)).astype(jnp.bfloat16)
        padded = jnp.pad(mixed.astype(jnp.float32), ((1, 1), (0, 0)))
        hidden_pre = depth_kernel[0] * padded[:-2] + depth_kernel[1] * padded[1:-1] + depth_kernel[2] * padded[2:]
        hidden = jax.nn.gelu(hidden_pre).astype(jnp.bfloat16)
        logits = jnp.dot(hidden, head_weight, preferred_element_type=jnp.float32) + head_bias
        predicted = jax.nn.softplus(logits)
        targets = counts.astype(jnp.float32)
        pred_total = lax.optimization_barrier(jnp.sum(predicted, axis=0))
        target_total = lax.optimization_barrier(jnp.sum(targets, axis=0))
        log_total = jnp.log(pred_total)
        track_terms = total_weight * (pred_total - target_total * log_total) + target_total * log_total
        loss_here = jnp.sum(track_terms) - jnp.sum(targets * jnp.log(predicted))
        ratio = target_total / pred_total
        logit_grad = (factor * (total_weight + (1.0 - total_weight) * ratio - targets / predicted) * jax.nn.sigmoid(logits)).astype(jnp.bfloat16)
        grad_sum = grad_sum + jnp.dot(hidden.T, logit_grad, preferred_element_type=jnp.float32)
        hidden_grad = jnp.dot(logit_grad, head_weight.T, preferred_element_type=jnp.float32)
        _, pullback = jax.vjp(jax.nn.gelu, hidden_pre)
        pre_grad = pullback(hidden_grad)[0]
        padded_grad = jnp.pad(pre_grad, ((1, 1), (0, 0)))
        mixed_grad = depth_kernel[0] * padded_grad[2:] + depth_kernel[1] * padded_grad[1:-1] + depth_kernel[2] * padded_grad[:-2]
        return ((grad_sum, loss_sum + loss_here), mixed_grad.astype(jnp.bfloat16))
    start_carry = (jnp.zeros((C, TR), jnp.float32), jnp.zeros((), jnp.float32))
    (weight_grad, loss_sum), skip_grad = lax.scan(one_sequence, start_carry, (coarse_input, skip_input, coverage))
    return (loss_sum / denominator, weight_grad, skip_grad)
```

```python
import jax
import jax.numpy as jnp
from jax import lax
from jax.sharding import PartitionSpec as P

loss_scale = 4194304.0
total_weight = 0.2
X, Z, CORES, REP = 4, 8, 2, 4


def seq_index(x, z, c):
    return (x * Z + z) * CORES + c


def seq_move(block, to):
    pairs = [
        (seq_index(x, z, c), seq_index(*to(x, z, c)))
        for x in range(X)
        for z in range(Z)
        for c in range(CORES)
    ]
    return lax.ppermute(block, "seq", pairs)


def move_x(block, step):
    return seq_move(block, lambda x, z, c: ((x + step) % X, z, c))


def move_z(block, step):
    return seq_move(block, lambda x, z, c: (x, (z + step) % Z, c))


def move_core(block):
    return seq_move(block, lambda x, z, c: (x, z, 1 - c))


def move_rep(block, step):
    return lax.ppermute(block, "rep", [(i, (i + step) % REP) for i in range(REP)])


def halo(low_row, high_row):
    count = X * Z * CORES
    up = [(i, i + 1) for i in range(count - 1)]
    down = [(target, source) for source, target in up]
    return lax.ppermute(high_row, "seq", up), lax.ppermute(low_row, "seq", down)


def seq_sum(block):
    rounds = (
        (
            lambda x, z, c: (x, z, 1 - c),
            lambda x, z, c: (x, z ^ 1, c),
            lambda x, z, c: (x, z ^ 1, 1 - c),
        ),
        tuple(lambda x, z, c, k=k: ((x + k) % X, z, c) for k in (1, 2, 3)),
        tuple(lambda x, z, c, k=k: (x, (z + 2 * k) % Z, c) for k in (1, 2, 3)),
    )
    for moves in rounds:
        parts = [seq_move(block, to) for to in moves]
        block = (block + parts[0]) + (parts[1] + parts[2])
    return block


def send(block):
    return block.astype(jnp.bfloat16)


def take(block):
    return block.astype(jnp.float32)


def reduce_scatter_seq(part):
    rows, tracks = part.shape
    own = rows // (X * Z * CORES)
    me = lax.axis_index("seq")
    core, z, x = me % CORES, (me // CORES) % Z, me // (CORES * Z)
    by_core = part.reshape(X * Z, CORES, own, tracks)
    mine = lax.dynamic_index_in_dim(by_core, core, 1, keepdims=False)
    other = lax.dynamic_index_in_dim(by_core, 1 - core, 1, keepdims=False)
    mine = mine + take(move_core(send(other)))
    grid = mine.reshape(X, Z, own, tracks)
    grid = jnp.roll(grid, (-x, -z), (0, 1))
    half = tracks // 2
    a = grid[..., :half]
    ring = [a[:, k] for k in range(Z)]
    up, down = ring[4][:2], ring[4][2:]
    up, down = move_z(send(up), 1), move_z(send(down), -1)
    ring[3] = ring[3].at[:2].add(take(up))
    ring[5] = ring[5].at[2:].add(take(down))
    for k in (3, 2, 1):
        up, down = move_z(send(ring[k]), 1), move_z(send(ring[Z - k]), -1)
        if k > 1:
            ring[k - 1] = ring[k - 1] + take(up)
            ring[Z - k + 1] = ring[Z - k + 1] + take(down)
    a = ring[0] + take(up) + take(down)
    a = a[0] + sum(move_x(a[k], k) for k in (1, 2, 3))
    b = grid[..., half:]
    ring = [b[k] for k in range(X)]
    up, down = ring[2][:4], ring[2][4:]
    up, down = move_x(send(up), 1), move_x(send(down), -1)
    ring[1] = ring[1].at[:4].add(take(up))
    ring[3] = ring[3].at[4:].add(take(down))
    up, down = move_x(send(ring[1]), 1), move_x(send(ring[3]), -1)
    b = ring[0] + take(up) + take(down)
    b = b[0] + sum(move_z(b[k], k) for k in range(1, Z))
    return jnp.concatenate([a, b], axis=-1)


def shards(coarse_input, skip_input, depth_kernel, head_weight, head_bias, coverage):
    rep_count, seq_count = REP, X * Z * CORES
    denominator = (
        coverage.shape[0] * (head_weight.shape[1] * rep_count) * (coverage.shape[1] * seq_count)
    )
    factor = loss_scale / denominator
    rep = lax.axis_index("rep")
    bins = skip_input.shape[1]
    mixed = (
        jnp.repeat(coarse_input[0], 2, axis=0).astype(jnp.float32)
        + skip_input[0].astype(jnp.float32)
    ).astype(jnp.bfloat16)
    low, high = halo(mixed[:1], mixed[-1:])
    padded = jnp.concatenate([low, mixed, high], axis=0).astype(jnp.float32)
    hidden_pre = (
        depth_kernel[0] * padded[:-2]
        + depth_kernel[1] * padded[1:-1]
        + depth_kernel[2] * padded[2:]
    )
    hidden = jax.nn.gelu(hidden_pre).astype(jnp.bfloat16)
    below, above = move_rep(hidden, 1), move_rep(hidden, -1)
    cut = bins // 2
    across = jnp.concatenate([move_rep(below[:cut], 1), move_rep(above[cut:], -1)], axis=0)
    hidden_every = jnp.stack([hidden, below, above, across])
    order = (rep + jnp.array([0, REP - 1, 1, 2])) % REP
    targets = coverage[order].astype(jnp.float32)
    logits = (
        jnp.einsum("sbc,ct->sbt", hidden_every, head_weight, preferred_element_type=jnp.float32)
        + head_bias
    )
    predicted = jax.nn.softplus(logits)
    cross = jnp.sum(targets * jnp.log(predicted), axis=(0, 1))
    totals = seq_sum(
        jnp.concatenate(
            [jnp.sum(predicted, axis=1), jnp.sum(targets, axis=1), cross[None]], axis=0
        )
    )
    pred_total, target_total = totals[:4], totals[4:8]
    log_total = jnp.log(pred_total)
    track_terms = total_weight * (pred_total - target_total * log_total) + target_total * log_total
    loss = jnp.sum(track_terms) - jnp.sum(totals[8])
    loss = jnp.broadcast_to(loss, (8, 128))
    loss = loss + move_rep(loss, 1)
    loss = loss + move_rep(loss, 2)
    loss_value = loss[0, 0] / denominator
    ratio = target_total / pred_total
    logit_grad = (
        factor
        * (total_weight + (1.0 - total_weight) * ratio[:, None, :] - targets / predicted)
        * jax.nn.sigmoid(logits)
    ).astype(jnp.bfloat16)
    part = jnp.einsum("sbt,ct->sbc", logit_grad, head_weight, preferred_element_type=jnp.float32)
    up, down = move_rep(send(part[3, :cut]), 1), move_rep(send(part[3, cut:]), -1)
    up_sum = move_rep(send(part[2, :cut] + take(up)), 1)
    up_own = move_rep(send(part[2, cut:]), 1)
    down_sum = move_rep(send(part[1, cut:] + take(down)), -1)
    down_own = move_rep(send(part[1, :cut]), -1)
    hidden_grad = part[0] + jnp.concatenate(
        [take(up_sum) + take(down_own), take(up_own) + take(down_sum)], axis=0
    )
    weight_grad = reduce_scatter_seq(
        jnp.einsum("sbc,sbt->ct", hidden_every, logit_grad, preferred_element_type=jnp.float32)
    )
    _, pullback = jax.vjp(jax.nn.gelu, hidden_pre)
    pre_grad = pullback(hidden_grad)[0]
    low, high = halo(pre_grad[:1], pre_grad[-1:])
    padded_grad = jnp.concatenate([low, pre_grad, high], axis=0)
    mixed_grad = (
        depth_kernel[0] * padded_grad[2:]
        + depth_kernel[1] * padded_grad[1:-1]
        + depth_kernel[2] * padded_grad[:-2]
    )
    return (loss_value, weight_grad, mixed_grad.astype(jnp.bfloat16)[None])


def solution(mesh):
    return jax.shard_map(
        shards,
        mesh=mesh,
        in_specs=(
            P("rep", "seq", None),
            P("rep", "seq", None),
            P(),
            P(None, "rep"),
            P("rep"),
            P(None, "seq", "rep"),
        ),
        out_specs=(P(), P("seq", "rep"), P("rep", "seq", None)),
        check_vma=False,
    )
```

```python
import math

import jax
import jax.numpy as jnp
from jax import lax
from jax.experimental import pallas as pl
from jax.experimental.pallas import tpu as pltpu
from jax.sharding import PartitionSpec as P

loss_scale = 4194304.0
total_weight = 0.2
X, Z, CORES, REP = 4, 8, 2, 4


def seq_index(x, z, c):
    return (x * Z + z) * CORES + c


def seq_move(block, to):
    pairs = [
        (seq_index(x, z, c), seq_index(*to(x, z, c)))
        for x in range(X)
        for z in range(Z)
        for c in range(CORES)
    ]
    return lax.ppermute(block, "seq", pairs)


def move_x(block, step):
    return seq_move(block, lambda x, z, c: ((x + step) % X, z, c))


def move_z(block, step):
    return seq_move(block, lambda x, z, c: (x, (z + step) % Z, c))


def move_core(block):
    return seq_move(block, lambda x, z, c: (x, z, 1 - c))


def move_rep(block, step):
    return lax.ppermute(block, "rep", [(i, (i + step) % REP) for i in range(REP)])


def halo(low_row, high_row):
    count = X * Z * CORES
    up = [(i, i + 1) for i in range(count - 1)]
    down = [(target, source) for source, target in up]
    return lax.ppermute(high_row, "seq", up), lax.ppermute(low_row, "seq", down)


def seq_sum(block):
    rounds = (
        (
            lambda x, z, c: (x, z, 1 - c),
            lambda x, z, c: (x, z ^ 1, c),
            lambda x, z, c: (x, z ^ 1, 1 - c),
        ),
        tuple(lambda x, z, c, k=k: ((x + k) % X, z, c) for k in (1, 2, 3)),
        tuple(lambda x, z, c, k=k: (x, (z + 2 * k) % Z, c) for k in (1, 2, 3)),
    )
    for moves in rounds:
        parts = [seq_move(block, to) for to in moves]
        block = (block + parts[0]) + (parts[1] + parts[2])
    return block


F32, BF16 = jnp.float32, jnp.bfloat16
gelu_scale, gelu_cube = math.sqrt(2.0 / math.pi), 0.044715


def dot(a, b):
    return jnp.dot(a, b, preferred_element_type=F32)


def cost(flops, nbytes, transcendentals=0):
    return pl.CostEstimate(flops=flops, bytes_accessed=nbytes, transcendentals=transcendentals)


def params(mebibytes=40):
    return pltpu.CompilerParams(vmem_limit_bytes=mebibytes << 20)


def struct(rows, columns, dtype=F32):
    return jax.ShapeDtypeStruct((rows, columns), dtype)


def columns_of(rows, width):
    return pl.BlockSpec((rows, width), lambda i, *_: (0, i))


def whole(rows, columns):
    return pl.BlockSpec((rows, columns), lambda i, *_: (0, 0))


def previous(block, edge):
    rows = lax.broadcasted_iota(jnp.int32, block.shape, 0)
    return jnp.where(rows == 0, edge, pltpu.roll(block, 1, 0))


def following(block, edge):
    count = block.shape[0]
    rows = lax.broadcasted_iota(jnp.int32, block.shape, 0)
    return jnp.where(rows == count - 1, edge, pltpu.roll(block, count - 1, 0))


def mix_kernel(coarse, skip, mixed, first, last):
    bins, fine = skip.shape[0], skip.shape[0] // 2
    row = lax.broadcasted_iota(jnp.int32, (bins, fine), 0)
    column = lax.broadcasted_iota(jnp.int32, (bins, fine), 1)
    twice = jnp.where((row == 2 * column) | (row == 2 * column + 1), 1.0, 0.0).astype(BF16)
    out = (dot(twice, coarse[...]) + skip[...].astype(F32)).astype(BF16)
    mixed[...] = out
    first[...] = out[:1]
    last[...] = out[bins - 1 :]


def mix(coarse, skip):
    bins, channels = skip.shape
    width = channels // 3
    return pl.pallas_call(
        mix_kernel,
        grid=(3,),
        in_specs=[columns_of(bins // 2, width), columns_of(bins, width)],
        out_specs=[columns_of(bins, width), columns_of(1, width), columns_of(1, width)],
        out_shape=[struct(bins, channels, BF16)] + [struct(1, channels, BF16)] * 2,
        compiler_params=params(),
        cost_estimate=cost(2 * bins * bins // 2 * channels, 5 * bins * channels),
        name="mix",
    )(coarse, skip)


def before_gelu(mixed, low, high, taps):
    block = mixed[...].astype(F32)
    below = previous(block, low[...].astype(F32))
    above = following(block, high[...].astype(F32))
    return taps[0:1] * below + taps[1:2] * block + taps[2:3] * above


def hidden_kernel(mixed, low, high, taps, lo, hi):
    out = jax.nn.gelu(before_gelu(mixed, low, high, taps)).astype(BF16)
    half = lo.shape[0]
    lo[...] = out[:half]
    hi[...] = out[half:]


def make_hidden(mixed, low, high, taps):
    bins, channels = mixed.shape
    width = channels // 3
    return pl.pallas_call(
        hidden_kernel,
        grid=(3,),
        in_specs=[columns_of(bins, width), columns_of(1, width), columns_of(1, width), columns_of(3, width)],
        out_specs=[columns_of(bins // 2, width)] * 2,
        out_shape=[struct(bins // 2, channels, BF16)] * 2,
        compiler_params=params(),
        cost_estimate=cost(20 * bins * channels, 4 * bins * channels, bins * channels),
        name="hidden",
    )(mixed, low, high, taps)


def log1p(e):
    series = e * (1 + e * (-1 / 2 + e * (1 / 3 + e * (-1 / 4 + e * (1 / 5 - e / 6)))))
    return jnp.where(e < 0.05, series, jnp.log(1 + e))


def head_kernel(order, lo, hi, weight, bias, coverage, sig, lin, stats, turned):
    block = jnp.concatenate([lo[...], hi[...]], axis=0)

    @pl.when(pl.program_id(0) == 0)
    def _():
        turned[...] = block.T

    logits = dot(block, weight[...]) + bias[...]
    e = jnp.exp(-jnp.abs(logits))
    predicted = jnp.maximum(logits, 0.0) + log1p(e)
    sigmoid = jnp.where(logits >= 0, 1.0, e) / (1.0 + e)
    target = coverage[0].astype(F32)
    sig[...] = sigmoid
    lin[...] = (total_weight - target / predicted) * sigmoid
    sums = [predicted, target, target * jnp.log(predicted)]
    rows = [jnp.sum(v, axis=0, keepdims=True) for v in sums]
    stats[...] = jnp.concatenate(rows + [jnp.zeros((5, rows[0].shape[1]), F32)], axis=0)


def head(order, lo, hi, weight, bias, coverage):
    channels, tracks = weight.shape
    bins = coverage.shape[1]
    width = tracks // 4
    return pl.pallas_call(
        head_kernel,
        grid_spec=pltpu.PrefetchScalarGridSpec(
            num_scalar_prefetch=1,
            grid=(4,),
            in_specs=[
                whole(bins // 2, channels),
                whole(bins // 2, channels),
                columns_of(channels, width),
                columns_of(1, width),
                pl.BlockSpec((1, bins, width), lambda i, order: (order[0], 0, i)),
            ],
            out_specs=[
                columns_of(bins, width),
                columns_of(bins, width),
                columns_of(8, width),
                whole(channels, bins),
            ],
        ),
        out_shape=[
            struct(bins, tracks),
            struct(bins, tracks),
            struct(8, tracks),
            struct(channels, bins, BF16),
        ],
        compiler_params=params(),
        cost_estimate=cost(2 * bins * channels * tracks, 8 << 20, 4 * bins * tracks),
        name="head",
    )(order, lo, hi, weight, bias, coverage)


def weight_kernel(place, *refs):
    sigs, lins, turned = refs[:4], refs[4:8], refs[8:12]
    scale, coefficient, grad, mine, other, total = refs[12:]
    parts = []
    for slot in range(4):
        part = scale[0:1] * lins[slot][...] + coefficient[slot : slot + 1] * sigs[slot][...]
        parts.append(part.astype(BF16))
        grad[slot] = parts[-1]
    every = jnp.concatenate(parts, axis=0)
    across = jnp.concatenate([t[...] for t in turned], axis=1)
    total[...] = dot(across, every)
    own = total.shape[0] // (X * Z * CORES)
    core, z, x = place[0], place[1], place[2]

    def rows(c, j):
        k, p, m = j // 8, (j // 4) % 2, j % 4
        to_x = lax.rem(x + k, X)
        to_z = 2 * lax.rem(z // 2 + m, 4) + lax.rem(z + p, 2)
        start = ((to_x * Z + to_z) * CORES + c) * own
        return total[pl.ds(pl.multiple_of(start, 8), own), :]

    for j in range(0, X * Z, 2):
        at = slice(j * own, (j + 2) * own)
        mine[at] = jnp.concatenate([rows(core, j), rows(core, j + 1)], axis=0)
        away = jnp.concatenate([rows(1 - core, j), rows(1 - core, j + 1)], axis=0)
        other[at] = away.astype(BF16)


def weight_parts(place, sigs, lins, turned, scale, coefficient):
    bins, tracks = sigs[0].shape
    channels = turned[0].shape[0]
    width = tracks // 4
    half = channels // CORES
    return pl.pallas_call(
        weight_kernel,
        grid_spec=pltpu.PrefetchScalarGridSpec(
            num_scalar_prefetch=1,
            grid=(4,),
            in_specs=[columns_of(bins, width)] * 8
            + [whole(channels, bins)] * 4
            + [columns_of(1, width), columns_of(4, width)],
            out_specs=[
                pl.BlockSpec((4, bins, width), lambda i, *_: (0, 0, i)),
                columns_of(half, width),
                columns_of(half, width),
            ],
            scratch_shapes=[pltpu.VMEM((channels, width), F32)],
        ),
        out_shape=[
            jax.ShapeDtypeStruct((4, bins, tracks), BF16),
            struct(half, tracks),
            struct(half, tracks, BF16),
        ],
        compiler_params=params(48),
        cost_estimate=cost(2 * 4 * bins * channels * tracks, 18 << 20),
        name="weight_parts",
    )(place, *sigs, *lins, *turned, scale, coefficient)


def back(grad, weight):
    return lax.dot_general(grad, weight, (((1,), (1,)), ((), ())), preferred_element_type=F32)


def across_kernel(grad, weight, lo, hi):
    out = back(grad[0], weight[...]).astype(BF16)
    half = lo.shape[0]
    lo[...] = out[:half]
    hi[...] = out[half:]


def across_part(grad, weight):
    _, bins, tracks = grad.shape
    channels = weight.shape[0]
    width = channels // 3
    return pl.pallas_call(
        across_kernel,
        grid=(3,),
        in_specs=[
            pl.BlockSpec((1, bins, tracks), lambda i: (3, 0, 0)),
            pl.BlockSpec((width, tracks), lambda i: (i, 0)),
        ],
        out_specs=[columns_of(bins // 2, width)] * 2,
        out_shape=[struct(bins // 2, channels, BF16)] * 2,
        compiler_params=params(),
        cost_estimate=cost(2 * bins * channels * tracks, 5 << 20),
        name="across_part",
    )(grad, weight)


def near_kernel(grad, weight, own, below_lo, below_hi, above_lo, above_hi):
    block = weight[...]
    half = below_lo.shape[0]
    out = back(grad[2], block)
    above_lo[...] = out[:half]
    above_hi[...] = out[half:].astype(BF16)
    out = back(grad[1], block)
    below_lo[...] = out[:half].astype(BF16)
    below_hi[...] = out[half:]
    own[...] = back(grad[0], block)


def near_parts(grad, weight):
    _, bins, tracks = grad.shape
    channels = weight.shape[0]
    width = channels // 3
    half = bins // 2
    return pl.pallas_call(
        near_kernel,
        grid=(3,),
        in_specs=[
            pl.BlockSpec((3, bins, tracks), lambda i: (0, 0, 0)),
            pl.BlockSpec((width, tracks), lambda i: (i, 0)),
        ],
        out_specs=[columns_of(bins, width)] + [columns_of(half, width)] * 4,
        out_shape=[
            struct(bins, channels),
            struct(half, channels, BF16),
            struct(half, channels),
            struct(half, channels),
            struct(half, channels, BF16),
        ],
        compiler_params=params(),
        cost_estimate=cost(6 * bins * channels * tracks, 9 << 20),
        name="near_parts",
    )(grad, weight)


def core_sum_kernel(mine, other, keep, one, two, three):
    total = mine[...] + other[...].astype(F32)
    size = keep.shape[0]
    keep[...] = total[:size]
    for k, out in enumerate((one, two, three), 1):
        out[...] = total[k * size : (k + 1) * size].astype(BF16)


def core_sum(mine, other):
    rows, tracks = mine.shape
    size, width = rows // X, tracks // 4
    return pl.pallas_call(
        core_sum_kernel,
        grid=(4,),
        in_specs=[columns_of(rows, width)] * 2,
        out_specs=[columns_of(size, width)] * 4,
        out_shape=[struct(size, tracks)] + [struct(size, tracks, BF16)] * 3,
        compiler_params=params(),
        cost_estimate=cost(rows * tracks, 8 * rows * tracks),
        name="core_sum",
    )(mine, other)


def pre_kernel(own, up_lo, down_lo, up_hi, down_hi, mixed, low, high, taps, pre, first, last):
    half = up_lo.shape[0]
    x = before_gelu(mixed, low, high, taps)
    lo = up_lo[...].astype(F32) + down_lo[...].astype(F32)
    hi = up_hi[...].astype(F32) + down_hi[...].astype(F32)
    grad = own[...] + jnp.concatenate([lo, hi], axis=0)
    square = x * x
    t = jnp.tanh(gelu_scale * (x + gelu_cube * (x * square)))
    slope = gelu_scale * (1.0 + 3.0 * gelu_cube * square)
    out = grad * (0.5 * (1.0 + t) + 0.5 * x * ((1.0 - t * t) * slope))
    pre[...] = out
    first[...] = out[:1]
    last[...] = out[2 * half - 1 :]


def pre_gradient(own, up_lo, down_lo, up_hi, down_hi, mixed, low, high, taps):
    bins, channels = own.shape
    width = channels // 3
    row = columns_of(1, width)
    return pl.pallas_call(
        pre_kernel,
        grid=(3,),
        in_specs=[columns_of(bins, width)]
        + [columns_of(bins // 2, width)] * 4
        + [columns_of(bins, width), row, row, columns_of(3, width)],
        out_specs=[columns_of(bins, width), row, row],
        out_shape=[struct(bins, channels)] + [struct(1, channels)] * 2,
        compiler_params=params(),
        cost_estimate=cost(30 * bins * channels, 14 * bins * channels, bins * channels),
        name="pre_gradient",
    )(own, up_lo, down_lo, up_hi, down_hi, mixed, low, high, taps)


def skip_kernel(pre, low, high, taps, out):
    block = pre[...]
    above, below = following(block, high[...]), previous(block, low[...])
    out[0] = (taps[0:1] * above + taps[1:2] * block + taps[2:3] * below).astype(BF16)


def skip_gradient(pre, low, high, taps):
    bins, channels = pre.shape
    width = channels // 3
    row = columns_of(1, width)
    return pl.pallas_call(
        skip_kernel,
        grid=(3,),
        in_specs=[columns_of(bins, width), row, row, columns_of(3, width)],
        out_specs=pl.BlockSpec((1, bins, width), lambda i: (0, 0, i)),
        out_shape=jax.ShapeDtypeStruct((1, bins, channels), BF16),
        compiler_params=params(),
        cost_estimate=cost(10 * bins * channels, 6 * bins * channels),
        name="skip_gradient",
    )(pre, low, high, taps)


def scatter_weight(mine, other):
    keep, one, two, three = core_sum(mine, move_core(other))
    moved = [move_x(part, k) for k, part in ((1, one), (2, two), (3, three))]
    keep = keep + (moved[0].astype(F32) + moved[1].astype(F32) + moved[2].astype(F32))
    half = keep.shape[0] // 2
    moved = seq_move(keep[half:].astype(BF16), lambda x, z, c: (x, z ^ 1, c))
    keep = keep[:half] + moved.astype(F32)
    own = half // 4
    total = keep[:own]
    for m in (1, 2, 3):
        total = total + move_z(keep[m * own : (m + 1) * own].astype(BF16), 2 * m).astype(F32)
    return total


def shards(coarse_input, skip_input, depth_kernel, head_weight, head_bias, coverage):
    rep_count, seq_count = REP, X * Z * CORES
    denominator = (
        coverage.shape[0] * (head_weight.shape[1] * rep_count) * (coverage.shape[1] * seq_count)
    )
    factor = loss_scale / denominator
    rep, seq = lax.axis_index("rep"), lax.axis_index("seq")
    tracks = head_weight.shape[1]
    mixed, first, last = mix(coarse_input[0], skip_input[0])
    low, high = halo(first, last)
    lo, hi = make_hidden(mixed, low, high, depth_kernel)
    below_lo, above_hi = move_rep(lo, 1), move_rep(hi, -1)
    below_hi, above_lo = move_rep(hi, 1), move_rep(lo, -1)
    across_lo, across_hi = move_rep(below_lo, 1), move_rep(above_hi, -1)
    slots = ((lo, hi), (below_lo, below_hi), (above_lo, above_hi), (across_lo, across_hi))
    bias = head_bias[None]
    sigs, lins, stats, turned = zip(
        *(
            head(((rep + step) % REP)[None], *pair, head_weight, bias, coverage)
            for step, pair in zip((0, REP - 1, 1, 2), slots)
        )
    )
    rows = [s[0] for s in stats] + [s[1] for s in stats]
    rows.append(stats[0][2] + stats[1][2] + stats[2][2] + stats[3][2])
    totals = seq_sum(jnp.stack(rows).reshape(-1, 128)).reshape(9, tracks)
    pred_total, target_total = totals[:4], totals[4:8]
    log_total = jnp.log(pred_total)
    track_terms = total_weight * (pred_total - target_total * log_total) + target_total * log_total
    loss = jnp.sum(track_terms) - jnp.sum(totals[8])
    coefficient = (factor * (1.0 - total_weight)) * (target_total / pred_total)
    scale = jnp.full((1, tracks), factor, F32)
    place = jnp.stack([seq % CORES, (seq // CORES) % Z, seq // (CORES * Z)]).astype(jnp.int32)
    grad, mine, other = weight_parts(place, sigs, lins, turned, scale, coefficient)
    weight_grad = scatter_weight(mine, other)
    part_lo, part_hi = across_part(grad, head_weight)
    up, down = move_rep(part_lo, 1), move_rep(part_hi, -1)
    own, below_lo, below_hi, above_lo, above_hi = near_parts(grad, head_weight)
    up_hi, down_lo = move_rep(above_hi, 1), move_rep(below_lo, -1)
    up_lo = move_rep((above_lo + up.astype(F32)).astype(BF16), 1)
    down_hi = move_rep((below_hi + down.astype(F32)).astype(BF16), -1)
    pre, first, last = pre_gradient(
        own, up_lo, down_lo, up_hi, down_hi, mixed, low, high, depth_kernel
    )
    low, high = halo(first, last)
    skip_grad = skip_gradient(pre, low, high, depth_kernel)
    loss, _ = lax.optimization_barrier((jnp.broadcast_to(loss, (8, 128)), first))
    loss = loss + move_rep(loss, 1) + move_rep(loss, 2) + move_rep(loss, 3)
    return (loss[0, 0] / denominator, weight_grad, skip_grad)


def solution(mesh):
    return jax.shard_map(
        shards,
        mesh=mesh,
        in_specs=(
            P("rep", "seq", None),
            P("rep", "seq", None),
            P(),
            P(None, "rep"),
            P("rep"),
            P(None, "seq", "rep"),
        ),
        out_specs=(P(), P("seq", "rep"), P("rep", "seq", None)),
        check_vma=False,
    )
```

```python
import functools
import math

import jax
import jax.numpy as jnp
from jax import lax
from jax.experimental import pallas as pl
from jax.experimental.pallas import tpu as pltpu
from jax.sharding import PartitionSpec as P

loss_scale = 4194304.0
total_weight = 0.2
X, Z, CORES, REP = 4, 8, 2, 4


def seq_index(x, z, c):
    return (x * Z + z) * CORES + c


def seq_move(block, to):
    pairs = [
        (seq_index(x, z, c), seq_index(*to(x, z, c)))
        for x in range(X)
        for z in range(Z)
        for c in range(CORES)
    ]
    return lax.ppermute(block, "seq", pairs)


def move_x(block, step):
    return seq_move(block, lambda x, z, c: ((x + step) % X, z, c))


def move_z(block, step):
    return seq_move(block, lambda x, z, c: (x, (z + step) % Z, c))


def move_core(block):
    return seq_move(block, lambda x, z, c: (x, z, 1 - c))


def move_rep(block, step):
    return lax.ppermute(block, "rep", [(i, (i + step) % REP) for i in range(REP)])


def halo(low_row, high_row):
    count = X * Z * CORES
    up = [(i, i + 1) for i in range(count - 1)]
    down = [(target, source) for source, target in up]
    return lax.ppermute(high_row, "seq", up), lax.ppermute(low_row, "seq", down)


def seq_sum(block):
    rounds = (
        (
            lambda x, z, c: (x, z, 1 - c),
            lambda x, z, c: (x, z ^ 1, c),
            lambda x, z, c: (x, z ^ 1, 1 - c),
        ),
        tuple(lambda x, z, c, k=k: ((x + k) % X, z, c) for k in (1, 2, 3)),
        tuple(lambda x, z, c, k=k: (x, (z + 2 * k) % Z, c) for k in (1, 2, 3)),
    )
    for moves in rounds:
        parts = [seq_move(block, to) for to in moves]
        block = (block + parts[0]) + (parts[1] + parts[2])
    return block


F32, BF16 = jnp.float32, jnp.bfloat16
gelu_scale, gelu_cube = math.sqrt(2.0 / math.pi), 0.044715
EDGE = 16


def dot(a, b):
    return jnp.dot(a, b, preferred_element_type=F32)


def struct(rows, columns, dtype=F32):
    return jax.ShapeDtypeStruct((rows, columns), dtype)


def call(name, kernel, arrays, outs, flops, scalars=0, scratch=(), transcendentals=0):
    nbytes = sum(math.prod(a.shape) * a.dtype.itemsize for a in (*arrays, *outs))
    smem = pl.BlockSpec(memory_space=pltpu.SMEM)
    vmem = pl.BlockSpec(memory_space=pltpu.VMEM)
    return pl.pallas_call(
        kernel,
        in_specs=[smem] * scalars + [vmem] * (len(arrays) - scalars),
        out_specs=[vmem] * len(outs),
        out_shape=list(outs),
        scratch_shapes=list(scratch),
        compiler_params=pltpu.CompilerParams(vmem_limit_bytes=12 << 20),
        cost_estimate=pl.CostEstimate(
            flops=flops, bytes_accessed=nbytes, transcendentals=transcendentals
        ),
        name=name,
    )(*arrays)


def pinned(rows, columns, dtype=F32):
    return pltpu.VMEM((rows, columns), dtype)


def tiles(extent, width):
    return [slice(start, start + width) for start in range(0, extent, width)]


def previous(block, edge):
    rows = lax.broadcasted_iota(jnp.int32, block.shape, 0)
    return jnp.where(rows == 0, edge, pltpu.roll(block, 1, 0))


def following(block, edge):
    count = block.shape[0]
    rows = lax.broadcasted_iota(jnp.int32, block.shape, 0)
    return jnp.where(rows == count - 1, edge, pltpu.roll(block, count - 1, 0))


def convolve(block, low, high, taps):
    return taps[0:1] * previous(block, low) + taps[1:2] * block + taps[2:3] * following(block, high)


def mix_kernel(coarse, skip, taps, mixed, first, last, a, b):
    bins, fine = skip.shape[0], skip.shape[0] // 2
    row = lax.broadcasted_iota(jnp.int32, (bins, fine), 0)
    column = lax.broadcasted_iota(jnp.int32, (bins, fine), 1)
    twice = jnp.where((row == 2 * column) | (row == 2 * column + 1), 1.0, 0.0).astype(BF16)
    for at in tiles(skip.shape[1], 512):
        out = (dot(twice, coarse[:, at]) + skip[:, at].astype(F32)).astype(BF16)
        mixed[:, at] = out
        first[:, at] = out[:1]
        last[:, at] = out[bins - 1 :]
        block = out.astype(F32)
        hidden = jax.nn.gelu(convolve(block, block[:1], block[:1], taps[:, at])).astype(BF16)
        a[:, at] = hidden[EDGE:fine]
        b[:, at] = hidden[fine : bins - EDGE]


def mix(coarse, skip, taps):
    bins, channels = skip.shape
    inner = struct(bins // 2 - EDGE, channels, BF16)
    row = struct(1, channels, BF16)
    outs = [struct(bins, channels, BF16), row, row, inner, inner]
    flops = bins * bins * channels
    return call("mix", mix_kernel, (coarse, skip, taps), outs, flops, transcendentals=bins * channels)


def edge_kernel(mixed, low, high, taps, a, b, edges, up, down):
    bins, inner = mixed.shape[0], a.shape[0]
    start, end = mixed[: 2 * EDGE].astype(F32), mixed[bins - 2 * EDGE :].astype(F32)
    before = convolve(start, low[...].astype(F32), start[:1], taps)[:EDGE]
    after_ = convolve(end, end[:1], high[...].astype(F32), taps)[EDGE:]
    rows = jax.nn.gelu(jnp.concatenate([before, after_], axis=0)).astype(BF16)
    edges[...] = rows
    up[:inner] = b[...]
    up[inner:] = rows
    down[:inner] = a[...]
    down[inner:] = rows


def edge_rows(mixed, low, high, taps, a, b):
    rows, channels = a.shape
    message = struct(rows + 2 * EDGE, channels, BF16)
    outs = [struct(2 * EDGE, channels, BF16), message, message]
    return call("edges", edge_kernel, (mixed, low, high, taps, a, b), outs, 4000 * channels)


def log1p(e):
    series = e * (1 + e * (-1 / 2 + e * (1 / 3 + e * (-1 / 4 + e * (1 / 5 - e / 6)))))
    return jnp.where(e < 0.05, series, jnp.log(1 + e))


def head_kernel(form, slot, *refs):
    order, parts = refs[0], refs[1 : 1 + len(form)]
    weight, bias, coverage, sums, sig, lin, totals, turned, held = refs[1 + len(form) :]
    pieces = {}
    for names, ref in zip(form, parts):
        start = 0
        for name in names:
            rows = 2 * EDGE if name == "e" else held.shape[0] // 2 - EDGE
            pieces[name] = ref[start : start + rows]
            start += rows
    edges = pieces["e"]
    held[...] = jnp.concatenate([edges[:EDGE], pieces["a"], pieces["b"], edges[EDGE:]], axis=0)
    turned[...] = held[...].T
    totals[...] = sums[...]
    sequence = order[slot]
    for n, at in enumerate(tiles(weight.shape[1], 256)):
        logits = dot(held[...], weight[:, at]) + bias[:, at]
        e = jnp.exp(-jnp.abs(logits))
        predicted = jnp.maximum(logits, 0.0) + log1p(e)
        target = coverage[sequence, :, at].astype(F32)
        common = jnp.where(logits >= 0, 1.0, e) / (predicted * (1.0 + e))
        sigmoid = predicted * common
        sig[:, at] = sigmoid
        lin[:, at] = total_weight * sigmoid - target * common
        values = (predicted, target, target * jnp.log(predicted))
        for where, value in zip((16 * slot, 16 * slot + 8, 64), values):
            total = jnp.sum(value, axis=0, keepdims=True)
            for half in range(2):
                row = slice(where + 2 * n + half, where + 2 * n + half + 1)
                totals[row] = sums[row] + total[:, 128 * half : 128 * (half + 1)]


def head(slot, form, order, parts, weight, bias, coverage, sums):
    channels, tracks = weight.shape
    bins = coverage.shape[1]
    outs = [pinned(bins, tracks), pinned(bins, tracks), struct(72, 128), pinned(channels, bins, BF16)]
    return call(
        "head",
        functools.partial(head_kernel, form, slot),
        (order, *parts, weight, bias, coverage, sums),
        outs,
        2 * bins * channels * tracks,
        scalars=1,
        scratch=[pltpu.VMEM((bins, channels), BF16)],
        transcendentals=4 * bins * tracks,
    )


def weight_kernel(factor, place, *refs):
    sigs, lins, turned = refs[:4], refs[4:8], refs[8:12]
    totals, grad, mine, other, total = refs[12:]
    own = total.shape[0] // (X * Z * CORES)
    core, z, x = place[0], place[1], place[2]

    def rows(c, j):
        k, p, m = j // 8, (j // 4) % 2, j % 4
        to_x = lax.rem(x + k, X)
        to_z = 2 * lax.rem(z // 2 + m, 4) + lax.rem(z + p, 2)
        start = ((to_x * Z + to_z) * CORES + c) * own
        return total[pl.ds(pl.multiple_of(start, 8), own), :]

    for n, at in enumerate(tiles(grad.shape[2], 256)):
        result = None
        for slot in range(4):
            ratio = []
            for row in (16 * slot + 2 * n, 16 * slot + 2 * n + 1):
                ratio.append(totals[row + 8 : row + 9] / totals[row : row + 1])
            ratio = jnp.concatenate(ratio, axis=1)
            part = factor * lins[slot][:, at] + (factor * (1.0 - total_weight) * ratio) * sigs[slot][:, at]
            part = part.astype(BF16)
            grad[slot, :, at] = part
            product = dot(turned[slot][...], part)
            result = product if result is None else result + product
        total[...] = result
        for j in range(0, X * Z, 2):
            to = slice(j * own, (j + 2) * own)
            mine[to, at] = jnp.concatenate([rows(core, j), rows(core, j + 1)], axis=0)
            away = jnp.concatenate([rows(1 - core, j), rows(1 - core, j + 1)], axis=0)
            other[to, at] = away.astype(BF16)


def weight_parts(factor, place, sigs, lins, turned, totals):
    bins, tracks = sigs[0].shape
    channels = turned[0].shape[0]
    half = channels // CORES
    outs = [
        jax.ShapeDtypeStruct((4, bins, tracks), BF16),
        struct(half, tracks),
        struct(half, tracks, BF16),
    ]
    return call(
        "weight_parts",
        functools.partial(weight_kernel, factor),
        (place, *sigs, *lins, *turned, totals),
        outs,
        8 * bins * channels * tracks,
        scalars=1,
        scratch=[pltpu.VMEM((channels, 256), F32)],
    )


def back(grad, weight):
    return lax.dot_general(grad, weight, (((1,), (1,)), ((), ())), preferred_element_type=F32)


def across_kernel(grad, weight, lo, hi):
    half = lo.shape[0]
    for at in tiles(weight.shape[0], 512):
        out = back(grad[3], weight[at]).astype(BF16)
        lo[:, at] = out[:half]
        hi[:, at] = out[half:]


def across_part(grad, weight):
    _, bins, tracks = grad.shape
    channels = weight.shape[0]
    outs = [struct(bins // 2, channels, BF16)] * 2
    return call("across_part", across_kernel, (grad, weight), outs, 2 * bins * channels * tracks)


def near_kernel(grad, weight, *outs):
    for at in tiles(weight.shape[0], 512):
        for slot in (2, 1, 0):
            outs[slot][:, at] = back(grad[slot], weight[at])


def near_parts(grad, weight):
    _, bins, tracks = grad.shape
    channels = weight.shape[0]
    outs = [struct(bins, channels)] * 3
    return call("near_parts", near_kernel, (grad, weight), outs, 6 * bins * channels * tracks)


def join_kernel(below, above, up, down, to_up, to_down):
    half = up.shape[0]
    to_up[:half] = (above[:half] + up[...].astype(F32)).astype(BF16)
    to_up[half:] = above[half:].astype(BF16)
    to_down[:half] = below[:half].astype(BF16)
    to_down[half:] = (below[half:] + down[...].astype(F32)).astype(BF16)


def join(below, above, up, down):
    bins, channels = below.shape
    outs = [struct(bins, channels, BF16)] * 2
    return call("join", join_kernel, (below, above, up, down), outs, bins * channels)


def core_sum_kernel(mine, other, keep, one, two, three):
    size = keep.shape[0]
    for k, out in enumerate((keep, one, two, three)):
        at = slice(k * size, (k + 1) * size)
        out[...] = (mine[at] + other[at].astype(F32)).astype(out.dtype)


def core_sum(mine, other):
    rows, tracks = mine.shape
    size = rows // X
    outs = [struct(size, tracks)] + [struct(size, tracks, BF16)] * 3
    return call("core_sum", core_sum_kernel, (mine, other), outs, rows * tracks)


def pre_kernel(own, up, down, mixed, low, high, taps, pre, first, last):
    bins = own.shape[0]
    for at in tiles(own.shape[1], 512):
        x = convolve(
            mixed[:, at].astype(F32),
            low[:, at].astype(F32),
            high[:, at].astype(F32),
            taps[:, at],
        )
        grad = own[:, at] + (up[:, at].astype(F32) + down[:, at].astype(F32))
        square = x * x
        t = jnp.tanh(gelu_scale * (x + gelu_cube * (x * square)))
        slope = gelu_scale * (1.0 + 3.0 * gelu_cube * square)
        out = grad * (0.5 * (1.0 + t) + 0.5 * x * ((1.0 - t * t) * slope))
        pre[:, at] = out
        first[:, at] = out[:1]
        last[:, at] = out[bins - 1 :]


def pre_gradient(own, up, down, mixed, low, high, taps):
    bins, channels = own.shape
    outs = [struct(bins, channels)] + [struct(1, channels)] * 2
    arrays = (own, up, down, mixed, low, high, taps)
    flops = 30 * bins * channels
    return call("pre_gradient", pre_kernel, arrays, outs, flops, transcendentals=bins * channels)


def skip_kernel(pre, low, high, taps, out):
    for at in tiles(pre.shape[1], 512):
        block = pre[:, at]
        above, below = following(block, high[:, at]), previous(block, low[:, at])
        grad = taps[0:1, at] * above + taps[1:2, at] * block + taps[2:3, at] * below
        out[0, :, at] = grad.astype(BF16)


def skip_gradient(pre, low, high, taps):
    bins, channels = pre.shape
    outs = [jax.ShapeDtypeStruct((1, bins, channels), BF16)]
    return call("skip_gradient", skip_kernel, (pre, low, high, taps), outs, 10 * bins * channels)[0]


def loss_kernel(denominator, totals, out):
    total = jnp.zeros((8, 128), F32)
    for slot in range(4):
        predicted, target = totals[16 * slot : 16 * slot + 8], totals[16 * slot + 8 : 16 * slot + 16]
        log_total = jnp.log(predicted)
        terms = total_weight * (predicted - target * log_total) + target * log_total
        total = total + terms
    total = total - totals[64:]
    out[...] = jnp.broadcast_to(jnp.sum(total, keepdims=True) / denominator, (8, 128))


def loss_part(denominator, totals):
    kernel = functools.partial(loss_kernel, denominator)
    return call("loss_part", kernel, (totals,), [struct(8, 128)], 100 * 4096, transcendentals=4096)[0]


def after(value, *others):
    return lax.optimization_barrier((value, *others))[0]


def shards(coarse_input, skip_input, depth_kernel, head_weight, head_bias, coverage):
    rep_count, seq_count = REP, X * Z * CORES
    denominator = (
        coverage.shape[0] * (head_weight.shape[1] * rep_count) * (coverage.shape[1] * seq_count)
    )
    factor = loss_scale / denominator
    rep, seq = lax.axis_index("rep"), lax.axis_index("seq")
    tracks = head_weight.shape[1]
    bias = head_bias[None]
    sums = jnp.zeros((72, 128), F32)

    order = jnp.stack([rep, (rep + REP - 1) % REP, (rep + 1) % REP, (rep + 2) % REP]).astype(jnp.int32)
    place = jnp.stack([seq % CORES, (seq // CORES) % Z, seq // (CORES * Z)]).astype(jnp.int32)
    coarse, order, place, sums, bias = lax.optimization_barrier(
        (coarse_input[0], order, place, sums, bias)
    )

    def head_of(slot, form, parts, sums):
        return head(slot, form, order, parts, head_weight, bias, coverage, sums)

    mixed, first, last, a, b = mix(coarse, skip_input[0], depth_kernel)
    below_a, above_b = move_rep(a, 1), move_rep(b, -1)
    low, high = halo(first, last)
    edges, up, down = edge_rows(mixed, low, high, depth_kernel, a, b)
    from_below, from_above = move_rep(up, 1), move_rep(down, -1)
    own_head = head_of(0, ("a", "be"), (a, up), sums)
    across_a = move_rep(after(below_a, own_head[2]), 1)
    across_b = move_rep(after(above_b, own_head[2]), -1)
    across_e = move_rep(edges, 2)
    below_head = head_of(1, ("a", "be"), (below_a, from_below), own_head[2])
    above_head = head_of(2, ("b", "ae"), (above_b, from_above), below_head[2])
    across_parts = (across_a, across_b, across_e)
    across_head = head_of(3, ("a", "b", "e"), across_parts, above_head[2])
    heads = (own_head, below_head, above_head, across_head)
    totals = seq_sum(across_head[2])
    sigs, lins, _, turned = zip(*heads)
    grad, mine, other = weight_parts(factor, place, sigs, lins, turned, totals)
    other = move_core(other)
    part_lo, part_hi = across_part(grad, head_weight)
    up, down = move_rep(part_lo, 1), move_rep(part_hi, -1)
    own, below, above = near_parts(after(grad, part_lo), head_weight)
    keep, one, two, three = core_sum(mine, after(other, own))
    moved = [move_x(part, k) for k, part in ((1, one), (2, two), (3, three))]
    to_up, to_down = join(after(below, keep), above, up, down)
    up, down = move_rep(to_up, 1), move_rep(to_down, -1)
    pre, first, last = pre_gradient(own, up, down, mixed, low, high, depth_kernel)
    keep = after(keep, to_up)
    keep = keep + (moved[0].astype(F32) + moved[1].astype(F32) + moved[2].astype(F32))
    half = keep.shape[0] // 2
    flipped = seq_move(keep[half:].astype(BF16), lambda x, z, c: (x, z ^ 1, c))
    low, high = halo(first, last)
    keep = keep[:half] + flipped.astype(F32)
    rows = half // 4
    sent = [keep[m * rows : (m + 1) * rows].astype(BF16) for m in (1, 2, 3)]
    parts = [move_z(part, 2 * m) for m, part in zip((1, 2, 3), sent)]
    skip_grad = skip_gradient(after(pre, sent[0]), low, high, depth_kernel)
    loss = loss_part(denominator, after(totals, low, sent[0]))
    loss = loss + move_rep(loss, 1) + move_rep(loss, 2) + move_rep(loss, 3)
    weight_grad = keep[:rows] + sum(part.astype(F32) for part in parts)
    return (loss[0, 0], weight_grad, skip_grad)


def solution(mesh):
    return jax.shard_map(
        shards,
        mesh=mesh,
        in_specs=(
            P("rep", "seq", None),
            P("rep", "seq", None),
            P(),
            P(None, "rep"),
            P("rep"),
            P(None, "seq", "rep"),
        ),
        out_specs=(P(), P("seq", "rep"), P("rep", "seq", None)),
        check_vma=False,
    )
```

```python
import functools
import math

import jax
import jax.numpy as jnp
from jax import lax
from jax.experimental import pallas as pl
from jax.experimental.pallas import tpu as pltpu
from jax.sharding import PartitionSpec as P

loss_scale = 4194304.0
total_weight = 0.2
X, Z, CORES, REP = 4, 8, 2, 4


def seq_index(x, z, c):
    return (x * Z + z) * CORES + c


def seq_move(block, to):
    pairs = [
        (seq_index(x, z, c), seq_index(*to(x, z, c)))
        for x in range(X)
        for z in range(Z)
        for c in range(CORES)
    ]
    return lax.ppermute(block, "seq", pairs)


def move_x(block, step):
    return seq_move(block, lambda x, z, c: ((x + step) % X, z, c))


def move_z(block, step):
    return seq_move(block, lambda x, z, c: (x, (z + step) % Z, c))


def move_core(block):
    return seq_move(block, lambda x, z, c: (x, z, 1 - c))


def move_rep(block, step):
    return lax.ppermute(block, "rep", [(i, (i + step) % REP) for i in range(REP)])


def halo(low_row, high_row):
    count = X * Z * CORES
    up = [(i, i + 1) for i in range(count - 1)]
    down = [(target, source) for source, target in up]
    return lax.ppermute(high_row, "seq", up), lax.ppermute(low_row, "seq", down)


def seq_sum(block):
    rounds = (
        (
            lambda x, z, c: (x, z, 1 - c),
            lambda x, z, c: (x, z ^ 1, c),
            lambda x, z, c: (x, z ^ 1, 1 - c),
        ),
        tuple(lambda x, z, c, k=k: ((x + k) % X, z, c) for k in (1, 2, 3)),
        tuple(lambda x, z, c, k=k: (x, (z + 2 * k) % Z, c) for k in (1, 2, 3)),
    )
    for moves in rounds:
        parts = [seq_move(block, to) for to in moves]
        block = (block + parts[0]) + (parts[1] + parts[2])
    return block


F32, BF16 = jnp.float32, jnp.bfloat16
gelu_scale, gelu_cube = math.sqrt(2.0 / math.pi), 0.044715
EDGE, SPARE = 16, 64


def dot(a, b):
    return jnp.dot(a, b, preferred_element_type=F32)


def struct(rows, columns, dtype=F32):
    return jax.ShapeDtypeStruct((rows, columns), dtype)


def call(name, kernel, arrays, outs, flops, scalars=0, scratch=(), transcendentals=0):
    nbytes = sum(math.prod(a.shape) * a.dtype.itemsize for a in (*arrays, *outs))
    smem = pl.BlockSpec(memory_space=pltpu.SMEM)
    vmem = pl.BlockSpec(memory_space=pltpu.VMEM)
    return pl.pallas_call(
        kernel,
        in_specs=[smem] * scalars + [vmem] * (len(arrays) - scalars),
        out_specs=[vmem] * len(outs),
        out_shape=list(outs),
        scratch_shapes=list(scratch),
        compiler_params=pltpu.CompilerParams(vmem_limit_bytes=12 << 20),
        cost_estimate=pl.CostEstimate(
            flops=flops, bytes_accessed=nbytes, transcendentals=transcendentals
        ),
        name=name,
    )(*arrays)


def pinned(rows, columns, dtype=F32):
    return pltpu.VMEM((rows, columns), dtype)


def tiles(extent, width):
    return [slice(start, start + width) for start in range(0, extent, width)]


def previous(block, edge):
    rows = lax.broadcasted_iota(jnp.int32, block.shape, 0)
    return jnp.where(rows == 0, edge, pltpu.roll(block, 1, 0))


def following(block, edge):
    count = block.shape[0]
    rows = lax.broadcasted_iota(jnp.int32, block.shape, 0)
    return jnp.where(rows == count - 1, edge, pltpu.roll(block, count - 1, 0))


def convolve(block, low, high, taps):
    return taps[0:1] * previous(block, low) + taps[1:2] * block + taps[2:3] * following(block, high)


def mix_kernel(coarse, skip, taps, mixed, up, down):
    bins, fine = skip.shape[0], skip.shape[0] // 2
    row = lax.broadcasted_iota(jnp.int32, (bins, fine), 0)
    column = lax.broadcasted_iota(jnp.int32, (bins, fine), 1)
    twice = jnp.where((row == 2 * column) | (row == 2 * column + 1), 1.0, 0.0).astype(BF16)
    for at in tiles(skip.shape[1], 512):
        out = (dot(twice, coarse[:, at]) + skip[:, at].astype(F32)).astype(BF16)
        mixed[:, at] = out
        block = out.astype(F32)
        hidden = jax.nn.gelu(convolve(block, block[:1], block[:1], taps[:, at])).astype(BF16)
        up[:, at] = hidden[EDGE : bins - SPARE]
        down[:, at] = hidden[SPARE : bins - EDGE]


def mix(coarse, skip, taps):
    bins, channels = skip.shape
    most = struct(bins - EDGE - SPARE, channels, BF16)
    outs = [struct(bins, channels, BF16), most, most]
    flops = bins * bins * channels
    return call("mix", mix_kernel, (coarse, skip, taps), outs, flops, transcendentals=bins * channels)


def block_of(*rows):
    row = lax.broadcasted_iota(jnp.int32, (EDGE, rows[0].shape[1]), 0)
    out = jnp.zeros(row.shape, F32)
    for n, value in enumerate(rows):
        out = jnp.where(row == n, value, out)
    return out


def pack_kernel(mixed, coverage, first, last):
    bins, channels = mixed.shape
    top, bottom = mixed[:EDGE].astype(F32), mixed[bins - EDGE :].astype(F32)
    pad = jnp.zeros((1, channels - coverage.shape[2]), F32)
    low, high = [top[0:1], top[1:2]], [bottom[EDGE - 1 :], bottom[EDGE - 2 : EDGE - 1]]
    for s in range(coverage.shape[0]):
        row = coverage[s, :EDGE].astype(F32)[:1]
        low.append(jnp.concatenate([row, pad], axis=1))
        row = coverage[s, bins - EDGE :].astype(F32)[EDGE - 1 :]
        high.append(jnp.concatenate([row, pad], axis=1))
    first[...] = block_of(*low).astype(BF16)
    last[...] = block_of(*high).astype(BF16)


def pack(mixed, coverage):
    outs = [struct(EDGE, mixed.shape[1], BF16)] * 2
    return call("pack", pack_kernel, (mixed, coverage), outs, 1000 * mixed.shape[1])


def edge_kernel(mixed, low, high, taps, up, down, edges, more_up, more_down):
    bins, rest = mixed.shape[0], SPARE - EDGE
    start, end = mixed[: 2 * EDGE].astype(F32), mixed[bins - 2 * EDGE :].astype(F32)
    below, above = low[...].astype(F32), high[...].astype(F32)
    before = convolve(start, below[:1], start[:1], taps)[:EDGE]
    after_ = convolve(end, end[:1], above[:1], taps)[EDGE:]
    one = taps[0:1] * below[1:2] + taps[1:2] * below[0:1] + taps[2:3] * start[:1]
    two = taps[0:1] * end[2 * EDGE - 1 :] + taps[1:2] * above[0:1] + taps[2:3] * above[1:2]
    rows = jnp.concatenate([before, after_, block_of(one, two)], axis=0)
    rows = jax.nn.gelu(rows).astype(BF16)
    edges[...] = rows
    more_up[:rest] = down[down.shape[0] - rest :]
    more_up[rest:] = rows
    more_down[:rest] = up[:rest]
    more_down[rest:] = rows


def edge_rows(mixed, low, high, taps, up, down):
    channels = mixed.shape[1]
    more = struct(SPARE + 2 * EDGE, channels, BF16)
    outs = [struct(3 * EDGE, channels, BF16), more, more]
    return call("edges", edge_kernel, (mixed, low, high, taps, up, down), outs, 4000 * channels)


def log1p(e):
    series = e * (1 + e * (-1 / 2 + e * (1 / 3 + e * (-1 / 4 + e * (1 / 5 - e / 6)))))
    return jnp.where(e < 0.05, series, jnp.log(1 + e))


def head_kernel(slot, count, rows, *refs):
    order, parts = refs[0], refs[1 : 1 + count]
    weight, bias, coverage, low, high, sums, sig, lin, totals, turned, held = refs[1 + count :]
    bins = coverage.shape[1]
    nth = lax.broadcasted_iota(jnp.int32, (EDGE, 256), 0)
    held[...] = jnp.concatenate([parts[n][start:stop] for n, start, stop in rows], axis=0)
    turned[...] = held[:bins].T
    totals[...] = sums[...]
    sequence = order[slot]
    for n, at in enumerate(tiles(weight.shape[1], 256)):
        logits = dot(held[...], weight[:, at]) + bias[:, at]
        e = jnp.exp(-jnp.abs(logits))
        predicted = jnp.maximum(logits, 0.0) + log1p(e)
        beside = [
            jnp.sum(jnp.where(nth == 2 + sequence, side[:, at].astype(F32), 0.0), axis=0, keepdims=True)
            for side in (low, high)
        ]
        target = jnp.concatenate([coverage[sequence, :, at].astype(F32), block_of(*beside)], axis=0)
        common = jnp.where(logits >= 0, 1.0, e) / (predicted * (1.0 + e))
        sigmoid = predicted * common
        sig[:, at] = sigmoid
        lin[:, at] = total_weight * sigmoid - target * common
        values = (predicted, target, target * jnp.log(predicted))
        for where, value in zip((16 * slot, 16 * slot + 8, 64), values):
            total = jnp.sum(value[:bins], axis=0, keepdims=True)
            for half in range(2):
                row = slice(where + 2 * n + half, where + 2 * n + half + 1)
                totals[row] = sums[row] + total[:, 128 * half : 128 * (half + 1)]


def head(slot, order, parts, rows, weight, bias, coverage, low, high, sums):
    channels, tracks = weight.shape
    bins = coverage.shape[1]
    terms = pinned(bins + EDGE, tracks)
    outs = [terms, terms, struct(72, 128), pinned(channels, bins, BF16)]
    return call(
        "head",
        functools.partial(head_kernel, slot, len(parts), rows),
        (order, *parts, weight, bias, coverage, low, high, sums),
        outs,
        2 * bins * channels * tracks,
        scalars=1,
        scratch=[pltpu.VMEM((bins + EDGE, channels), BF16)],
        transcendentals=4 * bins * tracks,
    )


def weight_kernel(factor, place, *refs):
    sigs, lins, turned = refs[:4], refs[4:8], refs[8:12]
    totals, grad, mine, other, total = refs[12:]
    own = total.shape[0] // (X * Z * CORES)
    core, z, x = place[0], place[1], place[2]

    def rows(c, j):
        k, p, m = j // 8, (j // 4) % 2, j % 4
        to_x = lax.rem(x + k, X)
        to_z = 2 * lax.rem(z // 2 + m, 4) + lax.rem(z + p, 2)
        start = ((to_x * Z + to_z) * CORES + c) * own
        return total[pl.ds(pl.multiple_of(start, 8), own), :]

    for n, at in enumerate(tiles(grad.shape[2], 256)):
        result = None
        for slot in range(4):
            ratio = []
            for row in (16 * slot + 2 * n, 16 * slot + 2 * n + 1):
                ratio.append(totals[row + 8 : row + 9] / totals[row : row + 1])
            ratio = jnp.concatenate(ratio, axis=1)
            part = factor * lins[slot][:, at] + (factor * (1.0 - total_weight) * ratio) * sigs[slot][:, at]
            part = part.astype(BF16)
            grad[slot, :, at] = part
            product = dot(turned[slot][...], part[: turned[slot].shape[1]])
            result = product if result is None else result + product
        total[...] = result
        for j in range(0, X * Z, 2):
            to = slice(j * own, (j + 2) * own)
            mine[to, at] = jnp.concatenate([rows(core, j), rows(core, j + 1)], axis=0)
            away = jnp.concatenate([rows(1 - core, j), rows(1 - core, j + 1)], axis=0)
            other[to, at] = away.astype(BF16)


def weight_parts(factor, place, sigs, lins, turned, totals):
    bins, tracks = sigs[0].shape
    channels = turned[0].shape[0]
    half = channels // CORES
    outs = [
        jax.ShapeDtypeStruct((4, bins, tracks), BF16),
        struct(half, tracks),
        struct(half, tracks, BF16),
    ]
    return call(
        "weight_parts",
        functools.partial(weight_kernel, factor),
        (place, *sigs, *lins, *turned, totals),
        outs,
        8 * bins * channels * tracks,
        scalars=1,
        scratch=[pltpu.VMEM((channels, 256), F32)],
    )


def back(grad, weight):
    return lax.dot_general(grad, weight, (((1,), (1,)), ((), ())), preferred_element_type=F32)


def loss_terms(totals):
    total = -totals[64:]
    for slot in range(4):
        predicted, target = totals[16 * slot : 16 * slot + 8], totals[16 * slot + 8 : 16 * slot + 16]
        log_total = jnp.log(predicted)
        terms = total_weight * (predicted - target * log_total) + target * log_total
        total = total + terms
    return jnp.sum(total, keepdims=True)


def three_of(value, columns):
    one = value.astype(BF16).astype(F32)
    two = (value - one).astype(BF16).astype(F32)
    return [jnp.broadcast_to(v, (1, columns)) for v in (one, two, (value - one) - two)]


def loss_of(block):
    rows = block[:, :128].astype(F32)
    return rows[2:3] + (rows[3:4] + rows[4:5])


def across_kernel(grad, weight, totals, lo, hi, loss):
    half = lo.shape[0] - EDGE
    bins = 2 * half
    value = loss_terms(totals)
    loss[...] = jnp.broadcast_to(value, loss.shape)
    for at in tiles(weight.shape[0], 512):
        out = back(grad[3], weight[at])
        rows = three_of(value, 512)
        none = jnp.zeros_like(rows[0])
        lo[:half, at] = out[:half].astype(BF16)
        hi[:half, at] = out[half:bins].astype(BF16)
        lo[half:, at] = block_of(out[bins : bins + 1], none, *rows).astype(BF16)
        hi[half:, at] = block_of(none, out[bins + 1 : bins + 2], *rows).astype(BF16)


def across_part(grad, weight, totals):
    _, rows, tracks = grad.shape
    channels = weight.shape[0]
    outs = [struct(rows // 2 + EDGE // 2, channels, BF16)] * 2 + [struct(8, 128)]
    arrays = (grad, weight, totals)
    return call("across_part", across_kernel, arrays, outs, 2 * rows * channels * tracks)


def near_kernel(grad, weight, *outs):
    for at in tiles(weight.shape[0], 512):
        for slot in (2, 1, 0):
            outs[slot][:, at] = back(grad[slot], weight[at])


def near_parts(grad, weight):
    _, rows, tracks = grad.shape
    channels = weight.shape[0]
    outs = [struct(rows, channels)] * 3
    return call("near_parts", near_kernel, (grad, weight), outs, 6 * rows * channels * tracks)


def join_kernel(below, above, up, down, to_up, to_down, loss):
    bins = below.shape[0] - EDGE
    half = bins // 2
    row = lax.broadcasted_iota(jnp.int32, (EDGE, below.shape[1]), 0)
    block = up[half:].astype(F32)
    to_up[:half] = (above[:half] + up[:half].astype(F32)).astype(BF16)
    to_up[half:bins] = above[half:bins].astype(BF16)
    to_up[bins:] = jnp.where(row < 2, above[bins:] + block, block).astype(BF16)
    to_down[:half] = below[:half].astype(BF16)
    to_down[half:bins] = (below[half:bins] + down[:half].astype(F32)).astype(BF16)
    to_down[bins:] = jnp.where(row < 2, below[bins:] + down[half:].astype(F32), 0.0).astype(BF16)
    loss[...] = jnp.broadcast_to(loss_of(up[half:]) + loss_of(down[half:]), loss.shape)


def join(below, above, up, down):
    rows, channels = below.shape
    outs = [struct(rows, channels, BF16)] * 2 + [struct(8, 128)]
    return call("join", join_kernel, (below, above, up, down), outs, rows * channels)


def core_sum_kernel(mine, other, keep, one, two, three):
    size = keep.shape[0]
    for k, out in enumerate((keep, one, two, three)):
        at = slice(k * size, (k + 1) * size)
        out[...] = (mine[at] + other[at].astype(F32)).astype(out.dtype)


def core_sum(mine, other):
    rows, tracks = mine.shape
    size = rows // X
    outs = [struct(size, tracks)] + [struct(size, tracks, BF16)] * 3
    return call("core_sum", core_sum_kernel, (mine, other), outs, rows * tracks)


def skip_kernel(
    denominator, place, own, up, down, mixed, low, high, taps, own_loss, near_loss, out, loss
):
    bins = mixed.shape[0]
    far = jnp.broadcast_to(loss_of(up[bins:]), loss.shape)
    loss[...] = ((own_loss[...] + far) + near_loss[...]) / denominator
    index = (place[2] * Z + place[1]) * CORES + place[0]
    has_low = jnp.where(index == 0, 0.0, 1.0)
    has_high = jnp.where(index == X * Z * CORES - 1, 0.0, 1.0)
    row = lax.broadcasted_iota(jnp.int32, (EDGE, 256), 0)
    for at in tiles(own.shape[1], 256):
        tap = taps[:, at]
        below, above = low[:, at].astype(F32), high[:, at].astype(F32)
        below = jnp.where(row == EDGE - 1, below[0:1], jnp.where(row == EDGE - 2, below[1:2], 0.0))
        above = jnp.where(row < 2, above, 0.0)
        block = jnp.concatenate([below, mixed[:, at].astype(F32), above], axis=0)
        x = convolve(block, block[:1], block[:1], tap)
        grad = own[:, at] + (up[:, at].astype(F32) + down[:, at].astype(F32))
        before = jnp.where(row == EDGE - 1, grad[bins : bins + 1] * has_low, 0.0)
        after_ = jnp.where(row == 0, grad[bins + 1 : bins + 2] * has_high, 0.0)
        grad = jnp.concatenate([before, grad[:bins], after_], axis=0)
        square = x * x
        t = jnp.tanh(gelu_scale * (x + gelu_cube * (x * square)))
        slope = gelu_scale * (1.0 + 3.0 * gelu_cube * square)
        pre = grad * (0.5 * (1.0 + t) + 0.5 * x * ((1.0 - t * t) * slope))
        turned = jnp.concatenate([tap[2:3], tap[1:2], tap[0:1]], axis=0)
        result = convolve(pre, pre[:1], pre[:1], turned)
        out[0, :, at] = result[EDGE : EDGE + bins].astype(BF16)


def skip_gradient(denominator, *arrays):
    bins, channels = arrays[4].shape
    outs = [jax.ShapeDtypeStruct((1, bins, channels), BF16), struct(8, 128)]
    kernel = functools.partial(skip_kernel, denominator)
    flops = 40 * bins * channels
    return call("skip_gradient", kernel, arrays, outs, flops, scalars=1, transcendentals=bins * channels)


def after(value, *others):
    return lax.optimization_barrier((value, *others))[0]


def shards(coarse_input, skip_input, depth_kernel, head_weight, head_bias, coverage):
    rep_count, seq_count = REP, X * Z * CORES
    denominator = (
        coverage.shape[0] * (head_weight.shape[1] * rep_count) * (coverage.shape[1] * seq_count)
    )
    factor = loss_scale / denominator
    rep, seq = lax.axis_index("rep"), lax.axis_index("seq")
    tracks = head_weight.shape[1]
    bias = head_bias[None]
    sums = jnp.zeros((72, 128), F32)

    order = jnp.stack([rep, (rep + REP - 1) % REP, (rep + 1) % REP, (rep + 2) % REP]).astype(jnp.int32)
    place = jnp.stack([seq % CORES, (seq // CORES) % Z, seq // (CORES * Z)]).astype(jnp.int32)
    coarse, order, place, sums, bias = lax.optimization_barrier(
        (coarse_input[0], order, place, sums, bias)
    )

    def head_of(slot, parts, rows, sums):
        return head(slot, order, parts, rows, head_weight, bias, coverage, low, high, sums)

    mixed, up, down = mix(coarse, skip_input[0], depth_kernel)
    bins, most = mixed.shape[0], up.shape[0]
    half, rest = bins // 2 - EDGE, SPARE - EDGE
    one, two, three = (rest + n * EDGE for n in (1, 2, 3))
    below_up, above_down = move_rep(up, 1), move_rep(down, -1)
    low, high = halo(*pack(mixed, coverage))
    edges, more_up, more_down = edge_rows(mixed, low, high, depth_kernel, up, down)
    below_more, above_more = move_rep(more_up, 1), move_rep(more_down, -1)
    tail = ((2, EDGE, 2 * EDGE), (2, 2 * EDGE, 3 * EDGE))
    rows = ((2, 0, EDGE), (0, 0, half), (1, most - half, most), *tail)
    own_head = head_of(0, (up, down, edges), rows, sums)
    ready = (own_head[2], below_more, above_more)
    across_a = move_rep(after(below_up, *ready)[:half], 1)
    across_b = move_rep(after(above_down, *ready)[most - half :], -1)
    across_e = move_rep(edges, 2)
    rows = ((1, rest, one), (0, 0, most), (1, 0, rest), (1, one, two), (1, two, three))
    below_head = head_of(1, (below_up, below_more), rows, own_head[2])
    rows = ((1, rest, one), (1, 0, rest), (0, 0, most), (1, one, two), (1, two, three))
    above_head = head_of(2, (above_down, above_more), rows, below_head[2])
    rows = ((2, 0, EDGE), (0, 0, half), (1, 0, half), *tail)
    across_head = head_of(3, (across_a, across_b, across_e), rows, above_head[2])
    heads = (own_head, below_head, above_head, across_head)
    totals = seq_sum(across_head[2])
    sigs, lins, _, turned = zip(*heads)
    grad, mine, other = weight_parts(factor, place, sigs, lins, turned, totals)
    other = move_core(other)
    part_lo, part_hi, own_loss = across_part(grad, head_weight, totals)
    up, down = move_rep(part_lo, 1), move_rep(part_hi, -1)
    own, below, above = near_parts(after(grad, part_lo), head_weight)
    keep, one, two, three = core_sum(mine, after(other, own))
    moved = [move_x(part, k) for k, part in ((1, one), (2, two), (3, three))]
    to_up, to_down, near_loss = join(after(below, keep), above, up, down)
    up, down = move_rep(to_up, 1), move_rep(to_down, -1)
    keep = after(keep, to_up)
    keep = keep + (moved[0].astype(F32) + moved[1].astype(F32) + moved[2].astype(F32))
    half = keep.shape[0] // 2
    flipped = seq_move(keep[half:].astype(BF16), lambda x, z, c: (x, z ^ 1, c))
    keep = keep[:half] + flipped.astype(F32)
    rows = half // 4
    keep = after(keep, up, down)
    sent = [keep[m * rows : (m + 1) * rows].astype(BF16) for m in (1, 2, 3)]
    parts = [move_z(part, 2 * m) for m, part in zip((1, 2, 3), sent)]
    arrays = (up, down, mixed, low, high, depth_kernel, own_loss, near_loss)
    skip_grad, loss = skip_gradient(denominator, place, after(own, sent[0]), *arrays)
    weight_grad = keep[:rows] + sum(part.astype(F32) for part in parts)
    return (loss[0, 0], weight_grad, skip_grad)


def solution(mesh):
    return jax.shard_map(
        shards,
        mesh=mesh,
        in_specs=(
            P("rep", "seq", None),
            P("rep", "seq", None),
            P(),
            P(None, "rep"),
            P("rep"),
            P(None, "seq", "rep"),
        ),
        out_specs=(P(), P("seq", "rep"), P("rep", "seq", None)),
        check_vma=False,
    )
```

```python
import functools
import math

import jax
import jax.numpy as jnp
from jax import lax
from jax.experimental import pallas as pl
from jax.experimental.pallas import tpu as pltpu
from jax.sharding import PartitionSpec as P

loss_scale = 4194304.0
total_weight = 0.2
X, Z, CORES, REP = 4, 8, 2, 4


def seq_index(x, z, c):
    return (x * Z + z) * CORES + c


def seq_move(block, to):
    pairs = [
        (seq_index(x, z, c), seq_index(*to(x, z, c)))
        for x in range(X)
        for z in range(Z)
        for c in range(CORES)
    ]
    return lax.ppermute(block, "seq", pairs)


def move_x(block, step):
    return seq_move(block, lambda x, z, c: ((x + step) % X, z, c))


def flip_z(block, bits):
    return seq_move(block, lambda x, z, c: (x, z ^ bits, c))


def move_core(block):
    return seq_move(block, lambda x, z, c: (x, z, 1 - c))


def move_rep(block, step):
    return lax.ppermute(block, "rep", [(i, (i + step) % REP) for i in range(REP)])


def halo(low_row, high_row):
    count = X * Z * CORES
    up = [(i, i + 1) for i in range(count - 1)]
    down = [(target, source) for source, target in up]
    return lax.ppermute(high_row, "seq", up), lax.ppermute(low_row, "seq", down)


def seq_sum(block):
    rounds = (
        (
            lambda x, z, c: (x, z, 1 - c),
            lambda x, z, c: (x, z ^ 1, c),
            lambda x, z, c: (x, z ^ 1, 1 - c),
        ),
        tuple(lambda x, z, c, k=k: ((x + k) % X, z, c) for k in (1, 2, 3)),
    )
    for moves in rounds:
        parts = [seq_move(block, to) for to in moves]
        block = (block + parts[0]) + (parts[1] + parts[2])
    for bits in (6, 2):
        block = block + flip_z(block, bits)
    return block


F32, BF16 = jnp.float32, jnp.bfloat16
gelu_scale, gelu_cube = math.sqrt(2.0 / math.pi), 0.044715
EDGE, SPARE = 16, 64


def dot(a, b):
    return jnp.dot(a, b, preferred_element_type=F32)


def struct(rows, columns, dtype=F32):
    return jax.ShapeDtypeStruct((rows, columns), dtype)


def call(name, kernel, arrays, outs, flops, scalars=0, scratch=(), transcendentals=0):
    nbytes = sum(math.prod(a.shape) * a.dtype.itemsize for a in (*arrays, *outs))
    smem = pl.BlockSpec(memory_space=pltpu.SMEM)
    vmem = pl.BlockSpec(memory_space=pltpu.VMEM)
    return pl.pallas_call(
        kernel,
        in_specs=[smem] * scalars + [vmem] * (len(arrays) - scalars),
        out_specs=[vmem] * len(outs),
        out_shape=list(outs),
        scratch_shapes=list(scratch),
        compiler_params=pltpu.CompilerParams(vmem_limit_bytes=12 << 20),
        cost_estimate=pl.CostEstimate(
            flops=flops, bytes_accessed=nbytes, transcendentals=transcendentals
        ),
        name=name,
    )(*arrays)


def pinned(rows, columns, dtype=F32):
    return pltpu.VMEM((rows, columns), dtype)


def tiles(extent, width):
    return [slice(start, start + width) for start in range(0, extent, width)]


def previous(block, edge):
    rows = lax.broadcasted_iota(jnp.int32, block.shape, 0)
    return jnp.where(rows == 0, edge, pltpu.roll(block, 1, 0))


def following(block, edge):
    count = block.shape[0]
    rows = lax.broadcasted_iota(jnp.int32, block.shape, 0)
    return jnp.where(rows == count - 1, edge, pltpu.roll(block, count - 1, 0))


def convolve(block, low, high, taps):
    return taps[0:1] * previous(block, low) + taps[1:2] * block + taps[2:3] * following(block, high)


def mix_kernel(coarse, skip, taps, mixed, up, down):
    bins, fine = skip.shape[0], skip.shape[0] // 2
    row = lax.broadcasted_iota(jnp.int32, (bins, fine), 0)
    column = lax.broadcasted_iota(jnp.int32, (bins, fine), 1)
    twice = jnp.where((row == 2 * column) | (row == 2 * column + 1), 1.0, 0.0).astype(BF16)
    for at in tiles(skip.shape[1], 512):
        out = (dot(twice, coarse[:, at]) + skip[:, at].astype(F32)).astype(BF16)
        mixed[:, at] = out
        block = out.astype(F32)
        hidden = jax.nn.gelu(convolve(block, block[:1], block[:1], taps[:, at])).astype(BF16)
        up[:, at] = hidden[EDGE : bins - SPARE]
        down[:, at] = hidden[SPARE : bins - EDGE]


def mix(coarse, skip, taps):
    bins, channels = skip.shape
    most = struct(bins - EDGE - SPARE, channels, BF16)
    outs = [struct(bins, channels, BF16), most, most]
    flops = bins * bins * channels
    return call("mix", mix_kernel, (coarse, skip, taps), outs, flops, transcendentals=bins * channels)


def block_of(*rows):
    row = lax.broadcasted_iota(jnp.int32, (EDGE, rows[0].shape[1]), 0)
    out = jnp.zeros(row.shape, F32)
    for n, value in enumerate(rows):
        out = jnp.where(row == n, value, out)
    return out


def pack_kernel(mixed, coverage, first, last):
    bins, channels = mixed.shape
    top, bottom = mixed[:EDGE].astype(F32), mixed[bins - EDGE :].astype(F32)
    pad = jnp.zeros((1, channels - coverage.shape[2]), F32)
    low, high = [top[0:1], top[1:2]], [bottom[EDGE - 1 :], bottom[EDGE - 2 : EDGE - 1]]
    for s in range(coverage.shape[0]):
        row = coverage[s, :EDGE].astype(F32)[:1]
        low.append(jnp.concatenate([row, pad], axis=1))
        row = coverage[s, bins - EDGE :].astype(F32)[EDGE - 1 :]
        high.append(jnp.concatenate([row, pad], axis=1))
    first[...] = block_of(*low).astype(BF16)
    last[...] = block_of(*high).astype(BF16)


def pack(mixed, coverage):
    outs = [struct(EDGE, mixed.shape[1], BF16)] * 2
    return call("pack", pack_kernel, (mixed, coverage), outs, 1000 * mixed.shape[1])


def edge_kernel(mixed, low, high, taps, up, down, edges, more_up, more_down):
    bins, rest = mixed.shape[0], SPARE - EDGE
    start, end = mixed[: 2 * EDGE].astype(F32), mixed[bins - 2 * EDGE :].astype(F32)
    below, above = low[...].astype(F32), high[...].astype(F32)
    before = convolve(start, below[:1], start[:1], taps)[:EDGE]
    after_ = convolve(end, end[:1], above[:1], taps)[EDGE:]
    one = taps[0:1] * below[1:2] + taps[1:2] * below[0:1] + taps[2:3] * start[:1]
    two = taps[0:1] * end[2 * EDGE - 1 :] + taps[1:2] * above[0:1] + taps[2:3] * above[1:2]
    rows = jnp.concatenate([before, after_, block_of(one, two)], axis=0)
    rows = jax.nn.gelu(rows).astype(BF16)
    edges[...] = rows
    more_up[:rest] = down[down.shape[0] - rest :]
    more_up[rest:] = rows
    more_down[:rest] = up[:rest]
    more_down[rest:] = rows


def edge_rows(mixed, low, high, taps, up, down):
    channels = mixed.shape[1]
    more = struct(SPARE + 2 * EDGE, channels, BF16)
    outs = [struct(3 * EDGE, channels, BF16), more, more]
    return call("edges", edge_kernel, (mixed, low, high, taps, up, down), outs, 4000 * channels)


def log1p(e):
    series = e * (1 + e * (-1 / 2 + e * (1 / 3 + e * (-1 / 4 + e * (1 / 5 - e / 6)))))
    return jnp.where(e < 0.05, series, jnp.log(1 + e))


def head_kernel(slot, count, rows, *refs):
    order, parts = refs[0], refs[1 : 1 + count]
    weight, bias, coverage, low, high, sums, sig, lin, totals, turned, held = refs[1 + count :]
    bins = coverage.shape[1]
    nth = lax.broadcasted_iota(jnp.int32, (EDGE, 256), 0)
    held[...] = jnp.concatenate([parts[n][start:stop] for n, start, stop in rows], axis=0)
    turned[...] = held[:bins].T
    totals[...] = sums[...]
    sequence = order[slot]
    for n, at in enumerate(tiles(weight.shape[1], 256)):
        logits = dot(held[...], weight[:, at]) + bias[:, at]
        e = jnp.exp(-jnp.abs(logits))
        predicted = jnp.maximum(logits, 0.0) + log1p(e)
        beside = [
            jnp.sum(jnp.where(nth == 2 + sequence, side[:, at].astype(F32), 0.0), axis=0, keepdims=True)
            for side in (low, high)
        ]
        target = jnp.concatenate([coverage[sequence, :, at].astype(F32), block_of(*beside)], axis=0)
        common = jnp.where(logits >= 0, 1.0, e) / (predicted * (1.0 + e))
        sigmoid = predicted * common
        sig[:, at] = sigmoid
        lin[:, at] = total_weight * sigmoid - target * common
        values = (predicted, target, target * jnp.log(predicted))
        for where, value in zip((16 * slot, 16 * slot + 8, 64), values):
            total = jnp.sum(value[:bins], axis=0, keepdims=True)
            for half in range(2):
                row = slice(where + 2 * n + half, where + 2 * n + half + 1)
                totals[row] = sums[row] + total[:, 128 * half : 128 * (half + 1)]


def head(slot, order, parts, rows, weight, bias, coverage, low, high, sums):
    channels, tracks = weight.shape
    bins = coverage.shape[1]
    terms = pinned(bins + EDGE, tracks)
    outs = [terms, terms, struct(72, 128), pinned(channels, bins, BF16)]
    return call(
        "head",
        functools.partial(head_kernel, slot, len(parts), rows),
        (order, *parts, weight, bias, coverage, low, high, sums),
        outs,
        2 * bins * channels * tracks,
        scalars=1,
        scratch=[pltpu.VMEM((bins + EDGE, channels), BF16)],
        transcendentals=4 * bins * tracks,
    )


def weight_kernel(factor, place, *refs):
    sigs, lins, turned = refs[:4], refs[4:8], refs[8:12]
    totals, grad, mine, other, total = refs[12:]
    own = total.shape[0] // (X * Z * CORES)
    core, z, x = place[0], place[1], place[2]

    def rows(c, j):
        k, bits = j // 8, (0, 2, 6, 4, 1, 3, 7, 5)[j % 8]
        to_x = lax.rem(x + k, X)
        to_z = lax.bitwise_xor(z, bits)
        start = ((to_x * Z + to_z) * CORES + c) * own
        return total[pl.ds(pl.multiple_of(start, 8), own), :]

    for n, at in enumerate(tiles(grad.shape[2], 256)):
        result = None
        for slot in range(4):
            ratio = []
            for row in (16 * slot + 2 * n, 16 * slot + 2 * n + 1):
                ratio.append(totals[row + 8 : row + 9] / totals[row : row + 1])
            ratio = jnp.concatenate(ratio, axis=1)
            part = factor * lins[slot][:, at] + (factor * (1.0 - total_weight) * ratio) * sigs[slot][:, at]
            part = part.astype(BF16)
            grad[slot, :, at] = part
            product = dot(turned[slot][...], part[: turned[slot].shape[1]])
            result = product if result is None else result + product
        total[...] = result
        for j in range(0, X * Z, 2):
            to = slice(j * own, (j + 2) * own)
            mine[to, at] = jnp.concatenate([rows(core, j), rows(core, j + 1)], axis=0)
            away = jnp.concatenate([rows(1 - core, j), rows(1 - core, j + 1)], axis=0)
            other[to, at] = away.astype(BF16)


def weight_parts(factor, place, sigs, lins, turned, totals):
    bins, tracks = sigs[0].shape
    channels = turned[0].shape[0]
    half = channels // CORES
    outs = [
        jax.ShapeDtypeStruct((4, bins, tracks), BF16),
        struct(half, tracks),
        struct(half, tracks, BF16),
    ]
    return call(
        "weight_parts",
        functools.partial(weight_kernel, factor),
        (place, *sigs, *lins, *turned, totals),
        outs,
        8 * bins * channels * tracks,
        scalars=1,
        scratch=[pltpu.VMEM((channels, 256), F32)],
    )


def back(grad, weight):
    return lax.dot_general(grad, weight, (((1,), (1,)), ((), ())), preferred_element_type=F32)


def loss_terms(totals):
    total = -totals[64:]
    for slot in range(4):
        predicted, target = totals[16 * slot : 16 * slot + 8], totals[16 * slot + 8 : 16 * slot + 16]
        log_total = jnp.log(predicted)
        terms = total_weight * (predicted - target * log_total) + target * log_total
        total = total + terms
    return jnp.sum(total, keepdims=True)


def three_of(value, columns):
    one = value.astype(BF16).astype(F32)
    two = (value - one).astype(BF16).astype(F32)
    return [jnp.broadcast_to(v, (1, columns)) for v in (one, two, (value - one) - two)]


def loss_of(block):
    rows = block[:, :128].astype(F32)
    return rows[2:3] + (rows[3:4] + rows[4:5])


def across_kernel(grad, weight, totals, lo, hi, loss):
    half = lo.shape[0] - EDGE
    bins = 2 * half
    value = loss_terms(totals)
    loss[...] = jnp.broadcast_to(value, loss.shape)
    for at in tiles(weight.shape[0], 512):
        out = back(grad[3], weight[at])
        rows = three_of(value, 512)
        none = jnp.zeros_like(rows[0])
        lo[:half, at] = out[:half].astype(BF16)
        hi[:half, at] = out[half:bins].astype(BF16)
        lo[half:, at] = block_of(out[bins : bins + 1], none, *rows).astype(BF16)
        hi[half:, at] = block_of(none, out[bins + 1 : bins + 2], *rows).astype(BF16)


def across_part(grad, weight, totals):
    _, rows, tracks = grad.shape
    channels = weight.shape[0]
    outs = [struct(rows // 2 + EDGE // 2, channels, BF16)] * 2 + [struct(8, 128)]
    arrays = (grad, weight, totals)
    return call("across_part", across_kernel, arrays, outs, 2 * rows * channels * tracks)


def near_kernel(grad, weight, *outs):
    for at in tiles(weight.shape[0], 512):
        for slot in (2, 1, 0):
            outs[slot][:, at] = back(grad[slot], weight[at])


def near_parts(grad, weight):
    _, rows, tracks = grad.shape
    channels = weight.shape[0]
    outs = [struct(rows, channels)] * 3
    return call("near_parts", near_kernel, (grad, weight), outs, 6 * rows * channels * tracks)


def join_kernel(below, above, up, down, to_up, to_down, loss):
    bins = below.shape[0] - EDGE
    half = bins // 2
    row = lax.broadcasted_iota(jnp.int32, (EDGE, below.shape[1]), 0)
    block = up[half:].astype(F32)
    to_up[:half] = (above[:half] + up[:half].astype(F32)).astype(BF16)
    to_up[half:bins] = above[half:bins].astype(BF16)
    to_up[bins:] = jnp.where(row < 2, above[bins:] + block, block).astype(BF16)
    to_down[:half] = below[:half].astype(BF16)
    to_down[half:bins] = (below[half:bins] + down[:half].astype(F32)).astype(BF16)
    to_down[bins:] = jnp.where(row < 2, below[bins:] + down[half:].astype(F32), 0.0).astype(BF16)
    loss[...] = jnp.broadcast_to(loss_of(up[half:]) + loss_of(down[half:]), loss.shape)


def join(below, above, up, down):
    rows, channels = below.shape
    outs = [struct(rows, channels, BF16)] * 2 + [struct(8, 128)]
    return call("join", join_kernel, (below, above, up, down), outs, rows * channels)


def core_sum_kernel(mine, other, keep, one, two, three):
    size = keep.shape[0]
    for k, out in enumerate((keep, one, two, three)):
        at = slice(k * size, (k + 1) * size)
        out[...] = (mine[at] + other[at].astype(F32)).astype(out.dtype)


def core_sum(mine, other):
    rows, tracks = mine.shape
    size = rows // X
    outs = [struct(size, tracks)] + [struct(size, tracks, BF16)] * 3
    return call("core_sum", core_sum_kernel, (mine, other), outs, rows * tracks)


def skip_kernel(
    denominator, place, own, up, down, mixed, low, high, taps, own_loss, near_loss, out, loss
):
    bins = mixed.shape[0]
    far = jnp.broadcast_to(loss_of(up[bins:]), loss.shape)
    loss[...] = ((own_loss[...] + far) + near_loss[...]) / denominator
    index = (place[2] * Z + place[1]) * CORES + place[0]
    has_low = jnp.where(index == 0, 0.0, 1.0)
    has_high = jnp.where(index == X * Z * CORES - 1, 0.0, 1.0)
    row = lax.broadcasted_iota(jnp.int32, (EDGE, 256), 0)
    for at in tiles(own.shape[1], 256):
        tap = taps[:, at]
        below, above = low[:, at].astype(F32), high[:, at].astype(F32)
        below = jnp.where(row == EDGE - 1, below[0:1], jnp.where(row == EDGE - 2, below[1:2], 0.0))
        above = jnp.where(row < 2, above, 0.0)
        block = jnp.concatenate([below, mixed[:, at].astype(F32), above], axis=0)
        x = convolve(block, block[:1], block[:1], tap)
        grad = own[:, at] + (up[:, at].astype(F32) + down[:, at].astype(F32))
        before = jnp.where(row == EDGE - 1, grad[bins : bins + 1] * has_low, 0.0)
        after_ = jnp.where(row == 0, grad[bins + 1 : bins + 2] * has_high, 0.0)
        grad = jnp.concatenate([before, grad[:bins], after_], axis=0)
        square = x * x
        t = jnp.tanh(gelu_scale * (x + gelu_cube * (x * square)))
        slope = gelu_scale * (1.0 + 3.0 * gelu_cube * square)
        pre = grad * (0.5 * (1.0 + t) + 0.5 * x * ((1.0 - t * t) * slope))
        turned = jnp.concatenate([tap[2:3], tap[1:2], tap[0:1]], axis=0)
        result = convolve(pre, pre[:1], pre[:1], turned)
        out[0, :, at] = result[EDGE : EDGE + bins].astype(BF16)


def skip_gradient(denominator, *arrays):
    bins, channels = arrays[4].shape
    outs = [jax.ShapeDtypeStruct((1, bins, channels), BF16), struct(8, 128)]
    kernel = functools.partial(skip_kernel, denominator)
    flops = 40 * bins * channels
    return call("skip_gradient", kernel, arrays, outs, flops, scalars=1, transcendentals=bins * channels)


def after(value, *others):
    return lax.optimization_barrier((value, *others))[0]


def shards(coarse_input, skip_input, depth_kernel, head_weight, head_bias, coverage):
    rep_count, seq_count = REP, X * Z * CORES
    denominator = (
        coverage.shape[0] * (head_weight.shape[1] * rep_count) * (coverage.shape[1] * seq_count)
    )
    factor = loss_scale / denominator
    rep, seq = lax.axis_index("rep"), lax.axis_index("seq")
    tracks = head_weight.shape[1]
    bias = head_bias[None]
    sums = jnp.zeros((72, 128), F32)

    order = jnp.stack([rep, (rep + REP - 1) % REP, (rep + 1) % REP, (rep + 2) % REP]).astype(jnp.int32)
    place = jnp.stack([seq % CORES, (seq // CORES) % Z, seq // (CORES * Z)]).astype(jnp.int32)
    coarse, order, place, sums, bias = lax.optimization_barrier(
        (coarse_input[0], order, place, sums, bias)
    )

    def head_of(slot, parts, rows, sums):
        return head(slot, order, parts, rows, head_weight, bias, coverage, low, high, sums)

    mixed, up, down = mix(coarse, skip_input[0], depth_kernel)
    bins, most = mixed.shape[0], up.shape[0]
    half, rest = bins // 2 - EDGE, SPARE - EDGE
    one, two, three = (rest + n * EDGE for n in (1, 2, 3))
    below_up, above_down = move_rep(up, 1), move_rep(down, -1)
    low, high = halo(*pack(mixed, coverage))
    edges, more_up, more_down = edge_rows(mixed, low, high, depth_kernel, up, down)
    below_more, above_more = move_rep(more_up, 1), move_rep(more_down, -1)
    tail = ((2, EDGE, 2 * EDGE), (2, 2 * EDGE, 3 * EDGE))
    rows = ((2, 0, EDGE), (0, 0, half), (1, most - half, most), *tail)
    own_head = head_of(0, (up, down, edges), rows, sums)
    ready = (own_head[2], below_more, above_more)
    across_a = move_rep(after(below_up, own_head[2])[:half], 1)
    across_b = move_rep(after(above_down, own_head[2])[most - half :], -1)
    across_e = move_rep(edges, 2)
    rows = ((1, rest, one), (0, 0, most), (1, 0, rest), (1, one, two), (1, two, three))
    below_head = head_of(1, (below_up, below_more), rows, after(*ready))
    rows = ((1, rest, one), (1, 0, rest), (0, 0, most), (1, one, two), (1, two, three))
    above_head = head_of(2, (above_down, above_more), rows, below_head[2])
    rows = ((2, 0, EDGE), (0, 0, half), (1, 0, half), *tail)
    across_head = head_of(3, (across_a, across_b, across_e), rows, above_head[2])
    heads = (own_head, below_head, above_head, across_head)
    totals = seq_sum(across_head[2])
    sigs, lins, _, turned = zip(*heads)
    grad, mine, other = weight_parts(factor, place, sigs, lins, turned, totals)
    other = move_core(other)
    part_lo, part_hi, own_loss = across_part(grad, head_weight, totals)
    up, down = move_rep(part_lo, 1), move_rep(part_hi, -1)
    keep, one, two, three = core_sum(mine, after(other, part_lo))
    own, below, above = near_parts(after(grad, keep), head_weight)
    moved = [move_x(part, k) for k, part in ((1, one), (2, two), (3, three))]
    to_up, to_down, near_loss = join(after(below, keep), above, up, down)
    up, down = move_rep(to_up, 1), move_rep(to_down, -1)
    keep = after(keep, to_up)
    keep = keep + (moved[0].astype(F32) + moved[1].astype(F32) + moved[2].astype(F32))
    for bits in (1, 6, 2):
        half = keep.shape[0] // 2
        sent = keep[half:].astype(BF16)
        if bits == 2:
            sent = after(sent, up, down)
        keep = keep[:half] + flip_z(sent, bits).astype(F32)
    arrays = (up, down, mixed, low, high, depth_kernel, own_loss, near_loss)
    skip_grad, loss = skip_gradient(denominator, place, after(own, sent), *arrays)
    return (loss[0, 0], keep, skip_grad)


def solution(mesh):
    return jax.shard_map(
        shards,
        mesh=mesh,
        in_specs=(
            P("rep", "seq", None),
            P("rep", "seq", None),
            P(),
            P(None, "rep"),
            P("rep"),
            P(None, "seq", "rep"),
        ),
        out_specs=(P(), P("seq", "rep"), P("rep", "seq", None)),
        check_vma=False,
    )
```

```python
import functools
import math

import jax
import jax.numpy as jnp
from jax import lax
from jax.experimental import pallas as pl
from jax.experimental.pallas import tpu as pltpu
from jax.sharding import PartitionSpec as P

loss_scale = 4194304.0
total_weight = 0.2
X, Z, CORES, REP = 4, 8, 2, 4


def seq_index(x, z, c):
    return (x * Z + z) * CORES + c


def seq_move(block, to):
    pairs = [
        (seq_index(x, z, c), seq_index(*to(x, z, c)))
        for x in range(X)
        for z in range(Z)
        for c in range(CORES)
    ]
    return lax.ppermute(block, "seq", pairs)


def move_x(block, step):
    return seq_move(block, lambda x, z, c: ((x + step) % X, z, c))


def flip_z(block, bits):
    return seq_move(block, lambda x, z, c: (x, z ^ bits, c))


def move_core(block):
    return seq_move(block, lambda x, z, c: (x, z, 1 - c))


def move_rep(block, step):
    return lax.ppermute(block, "rep", [(i, (i + step) % REP) for i in range(REP)])


def halo(low_row, high_row):
    count = X * Z * CORES
    up = [(i, i + 1) for i in range(count - 1)]
    down = [(target, source) for source, target in up]
    return lax.ppermute(high_row, "seq", up), lax.ppermute(low_row, "seq", down)


def seq_sum(block):
    rounds = (
        (
            lambda x, z, c: (x, z, 1 - c),
            lambda x, z, c: (x, z ^ 1, c),
            lambda x, z, c: (x, z ^ 1, 1 - c),
        ),
        tuple(lambda x, z, c, k=k: ((x + k) % X, z, c) for k in (1, 2, 3)),
    )
    for moves in rounds:
        parts = [seq_move(block, to) for to in moves]
        block = (block + parts[0]) + (parts[1] + parts[2])
    for bits in (6, 2):
        block = block + flip_z(block, bits)
    return block


F32, BF16 = jnp.float32, jnp.bfloat16
gelu_scale, gelu_cube = math.sqrt(2.0 / math.pi), 0.044715
EDGE, SPARE = 16, 64


def dot(a, b):
    return jnp.dot(a, b, preferred_element_type=F32)


def struct(rows, columns, dtype=F32):
    return jax.ShapeDtypeStruct((rows, columns), dtype)


def call(name, kernel, arrays, outs, flops, scalars=0, scratch=(), transcendentals=0):
    nbytes = sum(math.prod(a.shape) * a.dtype.itemsize for a in (*arrays, *outs))
    smem = pl.BlockSpec(memory_space=pltpu.SMEM)
    vmem = pl.BlockSpec(memory_space=pltpu.VMEM)
    return pl.pallas_call(
        kernel,
        in_specs=[smem] * scalars + [vmem] * (len(arrays) - scalars),
        out_specs=[vmem] * len(outs),
        out_shape=list(outs),
        scratch_shapes=list(scratch),
        compiler_params=pltpu.CompilerParams(vmem_limit_bytes=12 << 20),
        cost_estimate=pl.CostEstimate(
            flops=flops, bytes_accessed=nbytes, transcendentals=transcendentals
        ),
        name=name,
    )(*arrays)


def pinned(rows, columns, dtype=F32):
    return pltpu.VMEM((rows, columns), dtype)


def tiles(extent, width):
    return [slice(start, start + width) for start in range(0, extent, width)]


def previous(block, edge):
    rows = lax.broadcasted_iota(jnp.int32, block.shape, 0)
    return jnp.where(rows == 0, edge, pltpu.roll(block, 1, 0))


def following(block, edge):
    count = block.shape[0]
    rows = lax.broadcasted_iota(jnp.int32, block.shape, 0)
    return jnp.where(rows == count - 1, edge, pltpu.roll(block, count - 1, 0))


def convolve(block, low, high, taps):
    return taps[0:1] * previous(block, low) + taps[1:2] * block + taps[2:3] * following(block, high)


def mix_kernel(coarse, skip, taps, mixed, up, down):
    bins, fine = skip.shape[0], skip.shape[0] // 2
    row = lax.broadcasted_iota(jnp.int32, (bins, fine), 0)
    column = lax.broadcasted_iota(jnp.int32, (bins, fine), 1)
    twice = jnp.where((row == 2 * column) | (row == 2 * column + 1), 1.0, 0.0).astype(BF16)
    for at in tiles(skip.shape[1], 512):
        out = (dot(twice, coarse[:, at]) + skip[:, at].astype(F32)).astype(BF16)
        mixed[:, at] = out
        block = out.astype(F32)
        hidden = jax.nn.gelu(convolve(block, block[:1], block[:1], taps[:, at])).astype(BF16)
        up[:, at] = hidden[EDGE : bins - SPARE]
        down[:, at] = hidden[SPARE : bins - EDGE]


def mix(coarse, skip, taps):
    bins, channels = skip.shape
    most = struct(bins - EDGE - SPARE, channels, BF16)
    outs = [struct(bins, channels, BF16), most, most]
    flops = bins * bins * channels
    return call("mix", mix_kernel, (coarse, skip, taps), outs, flops, transcendentals=bins * channels)


def block_of(*rows):
    row = lax.broadcasted_iota(jnp.int32, (EDGE, rows[0].shape[1]), 0)
    out = jnp.zeros(row.shape, F32)
    for n, value in enumerate(rows):
        out = jnp.where(row == n, value, out)
    return out


def pack_kernel(mixed, coverage, first, last):
    bins, channels = mixed.shape
    top, bottom = mixed[:EDGE].astype(F32), mixed[bins - EDGE :].astype(F32)
    pad = jnp.zeros((1, channels - coverage.shape[2]), F32)
    low, high = [top[0:1], top[1:2]], [bottom[EDGE - 1 :], bottom[EDGE - 2 : EDGE - 1]]
    for s in range(coverage.shape[0]):
        row = coverage[s, :EDGE].astype(F32)[:1]
        low.append(jnp.concatenate([row, pad], axis=1))
        row = coverage[s, bins - EDGE :].astype(F32)[EDGE - 1 :]
        high.append(jnp.concatenate([row, pad], axis=1))
    first[...] = block_of(*low).astype(BF16)
    last[...] = block_of(*high).astype(BF16)


def pack(mixed, coverage):
    outs = [struct(EDGE, mixed.shape[1], BF16)] * 2
    return call("pack", pack_kernel, (mixed, coverage), outs, 1000 * mixed.shape[1])


def edge_kernel(mixed, low, high, taps, up, down, edges, more_up, more_down):
    bins, rest = mixed.shape[0], SPARE - EDGE
    start, end = mixed[: 2 * EDGE].astype(F32), mixed[bins - 2 * EDGE :].astype(F32)
    below, above = low[...].astype(F32), high[...].astype(F32)
    before = convolve(start, below[:1], start[:1], taps)[:EDGE]
    after_ = convolve(end, end[:1], above[:1], taps)[EDGE:]
    one = taps[0:1] * below[1:2] + taps[1:2] * below[0:1] + taps[2:3] * start[:1]
    two = taps[0:1] * end[2 * EDGE - 1 :] + taps[1:2] * above[0:1] + taps[2:3] * above[1:2]
    rows = jnp.concatenate([before, after_, block_of(one, two)], axis=0)
    rows = jax.nn.gelu(rows).astype(BF16)
    edges[...] = rows
    more_up[:rest] = down[down.shape[0] - rest :]
    more_up[rest:] = rows
    more_down[:rest] = up[:rest]
    more_down[rest:] = rows


def edge_rows(mixed, low, high, taps, up, down):
    channels = mixed.shape[1]
    more = struct(SPARE + 2 * EDGE, channels, BF16)
    outs = [struct(3 * EDGE, channels, BF16), more, more]
    return call("edges", edge_kernel, (mixed, low, high, taps, up, down), outs, 4000 * channels)


def log1p(e):
    series = e * (1 + e * (-1 / 2 + e * (1 / 3 + e * (-1 / 4 + e * (1 / 5 - e / 6)))))
    return jnp.where(e < 0.05, series, jnp.log(1 + e))


def head_kernel(slot, count, rows, *refs):
    order, parts = refs[0], refs[1 : 1 + count]
    weight, bias, coverage, low, high, sums, sig, lin, totals, turned, held = refs[1 + count :]
    bins = coverage.shape[1]
    nth = lax.broadcasted_iota(jnp.int32, (EDGE, 256), 0)
    held[...] = jnp.concatenate([parts[n][start:stop] for n, start, stop in rows], axis=0)
    turned[...] = held[:bins].T
    totals[...] = sums[...]
    sequence = order[slot]
    for n, at in enumerate(tiles(weight.shape[1], 256)):
        logits = dot(held[...], weight[:, at]) + bias[:, at]
        e = jnp.exp(-jnp.abs(logits))
        predicted = jnp.maximum(logits, 0.0) + log1p(e)
        beside = [
            jnp.sum(jnp.where(nth == 2 + sequence, side[:, at].astype(F32), 0.0), axis=0, keepdims=True)
            for side in (low, high)
        ]
        target = jnp.concatenate([coverage[sequence, :, at].astype(F32), block_of(*beside)], axis=0)
        common = jnp.where(logits >= 0, 1.0, e) / (predicted * (1.0 + e))
        sigmoid = predicted * common
        sig[:, at] = sigmoid
        lin[:, at] = total_weight * sigmoid - target * common
        values = (predicted, target, target * jnp.log(predicted))
        for where, value in zip((16 * slot, 16 * slot + 8, 64), values):
            total = jnp.sum(value[:bins], axis=0, keepdims=True)
            for half in range(2):
                row = slice(where + 2 * n + half, where + 2 * n + half + 1)
                totals[row] = sums[row] + total[:, 128 * half : 128 * (half + 1)]


def head(slot, order, parts, rows, weight, bias, coverage, low, high, sums):
    channels, tracks = weight.shape
    bins = coverage.shape[1]
    terms = pinned(bins + EDGE, tracks)
    outs = [terms, terms, struct(72, 128), pinned(channels, bins, BF16)]
    return call(
        "head",
        functools.partial(head_kernel, slot, len(parts), rows),
        (order, *parts, weight, bias, coverage, low, high, sums),
        outs,
        2 * bins * channels * tracks,
        scalars=1,
        scratch=[pltpu.VMEM((bins + EDGE, channels), BF16)],
        transcendentals=4 * bins * tracks,
    )


def weight_kernel(factor, place, *refs):
    sigs, lins, turned = refs[:4], refs[4:8], refs[8:12]
    totals, grad, mine, other, total = refs[12:]
    own = total.shape[0] // (X * Z * CORES)
    core, z, x = place[0], place[1], place[2]

    def rows(c, j):
        k, bits = j // 8, (0, 2, 6, 4, 1, 3, 7, 5)[j % 8]
        to_x = lax.rem(x + k, X)
        to_z = lax.bitwise_xor(z, bits)
        start = ((to_x * Z + to_z) * CORES + c) * own
        return total[pl.ds(pl.multiple_of(start, 8), own), :]

    for n, at in enumerate(tiles(grad.shape[2], 256)):
        result = None
        for slot in range(4):
            ratio = []
            for row in (16 * slot + 2 * n, 16 * slot + 2 * n + 1):
                ratio.append(totals[row + 8 : row + 9] / totals[row : row + 1])
            ratio = jnp.concatenate(ratio, axis=1)
            part = factor * lins[slot][:, at] + (factor * (1.0 - total_weight) * ratio) * sigs[slot][:, at]
            part = part.astype(BF16)
            grad[slot, :, at] = part
            product = dot(turned[slot][...], part[: turned[slot].shape[1]])
            result = product if result is None else result + product
        total[...] = result
        for j in range(0, X * Z, 2):
            to = slice(j * own, (j + 2) * own)
            mine[to, at] = jnp.concatenate([rows(core, j), rows(core, j + 1)], axis=0)
            away = jnp.concatenate([rows(1 - core, j), rows(1 - core, j + 1)], axis=0)
            other[to, at] = away.astype(BF16)


def weight_parts(factor, place, sigs, lins, turned, totals):
    bins, tracks = sigs[0].shape
    channels = turned[0].shape[0]
    half = channels // CORES
    outs = [
        jax.ShapeDtypeStruct((4, bins, tracks), BF16),
        struct(half, tracks),
        struct(half, tracks, BF16),
    ]
    return call(
        "weight_parts",
        functools.partial(weight_kernel, factor),
        (place, *sigs, *lins, *turned, totals),
        outs,
        8 * bins * channels * tracks,
        scalars=1,
        scratch=[pltpu.VMEM((channels, 256), F32)],
    )


def back(grad, weight):
    return lax.dot_general(grad, weight, (((1,), (1,)), ((), ())), preferred_element_type=F32)


def loss_terms(totals):
    total = -totals[64:]
    for slot in range(4):
        predicted, target = totals[16 * slot : 16 * slot + 8], totals[16 * slot + 8 : 16 * slot + 16]
        log_total = jnp.log(predicted)
        terms = total_weight * (predicted - target * log_total) + target * log_total
        total = total + terms
    return jnp.sum(total, keepdims=True)


def three_of(value, columns):
    one = value.astype(BF16).astype(F32)
    two = (value - one).astype(BF16).astype(F32)
    return [jnp.broadcast_to(v, (1, columns)) for v in (one, two, (value - one) - two)]


def loss_of(block):
    rows = block[:, :128].astype(F32)
    return rows[2:3] + (rows[3:4] + rows[4:5])


def across_kernel(grad, weight, totals, lo, hi, loss):
    half = lo.shape[0] - EDGE
    bins = 2 * half
    value = loss_terms(totals)
    loss[...] = jnp.broadcast_to(value, loss.shape)
    for at in tiles(weight.shape[0], 512):
        out = back(grad[3], weight[at])
        rows = three_of(value, 512)
        none = jnp.zeros_like(rows[0])
        lo[:half, at] = out[:half].astype(BF16)
        hi[:half, at] = out[half:bins].astype(BF16)
        lo[half:, at] = block_of(out[bins : bins + 1], none, *rows).astype(BF16)
        hi[half:, at] = block_of(none, out[bins + 1 : bins + 2], *rows).astype(BF16)


def across_part(grad, weight, totals):
    _, rows, tracks = grad.shape
    channels = weight.shape[0]
    outs = [struct(rows // 2 + EDGE // 2, channels, BF16)] * 2 + [struct(8, 128)]
    arrays = (grad, weight, totals)
    return call("across_part", across_kernel, arrays, outs, 2 * rows * channels * tracks)


def near_kernel(grad, weight, own, lo, hi, lo_sum, hi_sum, below_more, above_more):
    half = lo.shape[0]
    bins = 2 * half
    for at in tiles(weight.shape[0], 512):
        out = back(grad[2], weight[at])
        lo_sum[:, at] = out[:half]
        hi[:, at] = out[half:bins].astype(BF16)
        above_more[:, at] = out[bins:]
        out = back(grad[1], weight[at])
        lo[:, at] = out[:half].astype(BF16)
        hi_sum[:, at] = out[half:bins]
        below_more[:, at] = out[bins:]
        own[:, at] = back(grad[0], weight[at])


def near_parts(grad, weight):
    _, rows, tracks = grad.shape
    channels = weight.shape[0]
    half = (rows - EDGE) // 2
    outs = [struct(rows, channels)] + [struct(half, channels, BF16)] * 2
    outs += [struct(half, channels)] * 2 + [struct(EDGE, channels)] * 2
    return call("near_parts", near_kernel, (grad, weight), outs, 6 * rows * channels * tracks)


def join_kernel(lo_sum, hi_sum, below_more, above_more, up, down, to_up, to_down, loss):
    half = lo_sum.shape[0]
    row = lax.broadcasted_iota(jnp.int32, (EDGE, lo_sum.shape[1]), 0)
    block = up[half:].astype(F32)
    to_up[:half] = (lo_sum[...] + up[:half].astype(F32)).astype(BF16)
    to_up[half:] = jnp.where(row < 2, above_more[...] + block, block).astype(BF16)
    to_down[:half] = (hi_sum[...] + down[:half].astype(F32)).astype(BF16)
    to_down[half:] = jnp.where(row < 2, below_more[...] + down[half:].astype(F32), 0.0).astype(BF16)
    loss[...] = jnp.broadcast_to(loss_of(up[half:]) + loss_of(down[half:]), loss.shape)


def join(*arrays):
    rows, channels = arrays[-1].shape
    outs = [struct(rows, channels, BF16)] * 2 + [struct(8, 128)]
    return call("join", join_kernel, arrays, outs, rows * channels)


def core_sum_kernel(mine, other, keep, above, below, lo, hi):
    size, half = keep.shape[0], lo.shape[0]

    def part(start, count):
        return mine[start : start + count] + other[start : start + count].astype(F32)

    keep[...] = part(0, size)
    above[...] = part(size, size)
    lo[...] = part(2 * size, half).astype(BF16)
    hi[...] = part(2 * size + half, half).astype(BF16)
    below[...] = part(3 * size, size)


def core_sum(mine, other):
    rows, tracks = mine.shape
    size = rows // X
    outs = [struct(size, tracks)] * 3 + [struct(size // 2, tracks, BF16)] * 2
    return call("core_sum", core_sum_kernel, (mine, other), outs, rows * tracks)


def pass_kernel(above, below, up, down, to_up, to_down):
    half = up.shape[0]
    to_up[:half] = (above[:half] + up[...].astype(F32)).astype(BF16)
    to_up[half:] = above[half:].astype(BF16)
    to_down[:half] = below[:half].astype(BF16)
    to_down[half:] = (below[half:] + down[...].astype(F32)).astype(BF16)


def pass_on(above, below, up, down):
    outs = [struct(*above.shape, BF16)] * 2
    return call("pass_on", pass_kernel, (above, below, up, down), outs, 2 * math.prod(above.shape))


def skip_kernel(
    denominator, place, own, up, down, hi, lo, mixed, low, high, taps, own_loss, near_loss, out, loss
):
    bins, half = mixed.shape[0], hi.shape[0]
    far = jnp.broadcast_to(loss_of(up[half:]), loss.shape)
    loss[...] = ((own_loss[...] + far) + near_loss[...]) / denominator
    index = (place[2] * Z + place[1]) * CORES + place[0]
    has_low = jnp.where(index == 0, 0.0, 1.0)
    has_high = jnp.where(index == X * Z * CORES - 1, 0.0, 1.0)
    row = lax.broadcasted_iota(jnp.int32, (EDGE, 256), 0)
    for at in tiles(own.shape[1], 256):
        tap = taps[:, at]
        below, above = low[:, at].astype(F32), high[:, at].astype(F32)
        below = jnp.where(row == EDGE - 1, below[0:1], jnp.where(row == EDGE - 2, below[1:2], 0.0))
        above = jnp.where(row < 2, above, 0.0)
        block = jnp.concatenate([below, mixed[:, at].astype(F32), above], axis=0)
        x = convolve(block, block[:1], block[:1], tap)
        first = own[:half, at] + (up[:half, at].astype(F32) + lo[:, at].astype(F32))
        second = own[half:bins, at] + (hi[:, at].astype(F32) + down[:half, at].astype(F32))
        more = own[bins:, at] + (up[half:, at].astype(F32) + down[half:, at].astype(F32))
        before = jnp.where(row == EDGE - 1, more[0:1] * has_low, 0.0)
        after_ = jnp.where(row == 0, more[1:2] * has_high, 0.0)
        grad = jnp.concatenate([before, first, second, after_], axis=0)
        square = x * x
        t = jnp.tanh(gelu_scale * (x + gelu_cube * (x * square)))
        slope = gelu_scale * (1.0 + 3.0 * gelu_cube * square)
        pre = grad * (0.5 * (1.0 + t) + 0.5 * x * ((1.0 - t * t) * slope))
        turned = jnp.concatenate([tap[2:3], tap[1:2], tap[0:1]], axis=0)
        result = convolve(pre, pre[:1], pre[:1], turned)
        out[0, :, at] = result[EDGE : EDGE + bins].astype(BF16)


def skip_gradient(denominator, *arrays):
    bins, channels = arrays[6].shape
    outs = [jax.ShapeDtypeStruct((1, bins, channels), BF16), struct(8, 128)]
    kernel = functools.partial(skip_kernel, denominator)
    flops = 40 * bins * channels
    return call("skip_gradient", kernel, arrays, outs, flops, scalars=1, transcendentals=bins * channels)


def after(value, *others):
    return lax.optimization_barrier((value, *others))[0]


def shards(coarse_input, skip_input, depth_kernel, head_weight, head_bias, coverage):
    rep_count, seq_count = REP, X * Z * CORES
    denominator = (
        coverage.shape[0] * (head_weight.shape[1] * rep_count) * (coverage.shape[1] * seq_count)
    )
    factor = loss_scale / denominator
    rep, seq = lax.axis_index("rep"), lax.axis_index("seq")
    tracks = head_weight.shape[1]
    bias = head_bias[None]
    sums = jnp.zeros((72, 128), F32)

    order = jnp.stack([rep, (rep + REP - 1) % REP, (rep + 1) % REP, (rep + 2) % REP]).astype(jnp.int32)
    place = jnp.stack([seq % CORES, (seq // CORES) % Z, seq // (CORES * Z)]).astype(jnp.int32)
    coarse, order, place, sums, bias = lax.optimization_barrier(
        (coarse_input[0], order, place, sums, bias)
    )

    def head_of(slot, parts, rows, sums):
        return head(slot, order, parts, rows, head_weight, bias, coverage, low, high, sums)

    mixed, up, down = mix(coarse, skip_input[0], depth_kernel)
    bins, most = mixed.shape[0], up.shape[0]
    half, rest = bins // 2 - EDGE, SPARE - EDGE
    one, two, three = (rest + n * EDGE for n in (1, 2, 3))
    below_up, above_down = move_rep(up, 1), move_rep(down, -1)
    low, high = halo(*pack(mixed, coverage))
    edges, more_up, more_down = edge_rows(mixed, low, high, depth_kernel, up, down)
    below_more, above_more = move_rep(more_up, 1), move_rep(more_down, -1)
    tail = ((2, EDGE, 2 * EDGE), (2, 2 * EDGE, 3 * EDGE))
    rows = ((2, 0, EDGE), (0, 0, half), (1, most - half, most), *tail)
    own_head = head_of(0, (up, down, edges), rows, sums)
    ready = (own_head[2], below_more, above_more)
    across_a = move_rep(after(below_up, own_head[2])[:half], 1)
    across_b = move_rep(after(above_down, own_head[2])[most - half :], -1)
    across_e = move_rep(edges, 2)
    rows = ((1, rest, one), (0, 0, most), (1, 0, rest), (1, one, two), (1, two, three))
    below_head = head_of(1, (below_up, below_more), rows, after(*ready))
    rows = ((1, rest, one), (1, 0, rest), (0, 0, most), (1, one, two), (1, two, three))
    above_head = head_of(2, (above_down, above_more), rows, below_head[2])
    rows = ((2, 0, EDGE), (0, 0, half), (1, 0, half), *tail)
    across_head = head_of(3, (across_a, across_b, across_e), rows, above_head[2])
    heads = (own_head, below_head, above_head, across_head)
    totals = seq_sum(across_head[2])
    sigs, lins, _, turned = zip(*heads)
    grad, mine, other = weight_parts(factor, place, sigs, lins, turned, totals)
    other = move_core(other)
    part_lo, part_hi, own_loss = across_part(grad, head_weight, totals)
    up, down = move_rep(part_lo, 1), move_rep(part_hi, -1)
    keep, next_x, last_x, far_lo, far_hi = core_sum(mine, after(other, part_lo))
    far_lo, far_hi = move_x(far_lo, 1), move_x(far_hi, -1)
    own, lo, hi, *sums = near_parts(after(grad, keep), head_weight)
    hi, lo = move_rep(hi, 1), move_rep(lo, -1)
    next_x, last_x = pass_on(after(next_x, own), last_x, far_lo, far_hi)
    from_last, from_next = move_x(next_x, 1), move_x(last_x, -1)
    to_up, to_down, near_loss = join(after(sums[0], next_x), *sums[1:], up, down)
    up, down = move_rep(to_up, 1), move_rep(to_down, -1)
    keep = after(keep, to_up, hi, lo)
    keep = keep + (from_last.astype(F32) + from_next.astype(F32))
    for bits in (1, 6, 2):
        half = keep.shape[0] // 2
        sent = keep[half:].astype(BF16)
        if bits == 2:
            sent = after(sent, up, down)
        keep = keep[:half] + flip_z(sent, bits).astype(F32)
    arrays = (up, down, hi, lo, mixed, low, high, depth_kernel, own_loss, near_loss)
    skip_grad, loss = skip_gradient(denominator, place, after(own, sent), *arrays)
    return (loss[0, 0], keep, skip_grad)


def solution(mesh):
    return jax.shard_map(
        shards,
        mesh=mesh,
        in_specs=(
            P("rep", "seq", None),
            P("rep", "seq", None),
            P(),
            P(None, "rep"),
            P("rep"),
            P(None, "seq", "rep"),
        ),
        out_specs=(P(), P("seq", "rep"), P("rep", "seq", None)),
        check_vma=False,
    )
```

```python
import functools
import math

import jax
import jax.numpy as jnp
from jax import lax
from jax.experimental import pallas as pl
from jax.experimental.pallas import tpu as pltpu
from jax.sharding import PartitionSpec as P

loss_scale = 4194304.0
total_weight = 0.2
X, Z, CORES, REP = 4, 8, 2, 4


def seq_index(x, z, c):
    return (x * Z + z) * CORES + c


def seq_move(block, to):
    pairs = [
        (seq_index(x, z, c), seq_index(*to(x, z, c)))
        for x in range(X)
        for z in range(Z)
        for c in range(CORES)
    ]
    return lax.ppermute(block, "seq", pairs)


def move_x(block, step):
    return seq_move(block, lambda x, z, c: ((x + step) % X, z, c))


def flip_z(block, bits):
    return seq_move(block, lambda x, z, c: (x, z ^ bits, c))


def move_core(block):
    return seq_move(block, lambda x, z, c: (x, z, 1 - c))


def move_rep(block, step):
    return lax.ppermute(block, "rep", [(i, (i + step) % REP) for i in range(REP)])


def halo(low_row, high_row):
    count = X * Z * CORES
    up = [(i, i + 1) for i in range(count - 1)]
    down = [(target, source) for source, target in up]
    return lax.ppermute(high_row, "seq", up), lax.ppermute(low_row, "seq", down)


def seq_sum(block):
    rounds = (
        (
            lambda x, z, c: (x, z, 1 - c),
            lambda x, z, c: (x, z ^ 1, c),
            lambda x, z, c: (x, z ^ 1, 1 - c),
        ),
        tuple(lambda x, z, c, k=k: ((x + k) % X, z, c) for k in (1, 2, 3)),
    )
    for moves in rounds:
        parts = [seq_move(block, to) for to in moves]
        block = (block + parts[0]) + (parts[1] + parts[2])
    for bits in (6, 2):
        block = block + flip_z(block, bits)
    return block


F32, BF16 = jnp.float32, jnp.bfloat16
gelu_scale, gelu_cube = math.sqrt(2.0 / math.pi), 0.044715
EDGE, SPARE = 16, 64


def dot(a, b):
    return jnp.dot(a, b, preferred_element_type=F32)


def struct(rows, columns, dtype=F32):
    return jax.ShapeDtypeStruct((rows, columns), dtype)


def call(name, kernel, arrays, outs, flops, scalars=0, scratch=(), transcendentals=0):
    nbytes = sum(math.prod(a.shape) * a.dtype.itemsize for a in (*arrays, *outs))
    smem = pl.BlockSpec(memory_space=pltpu.SMEM)
    vmem = pl.BlockSpec(memory_space=pltpu.VMEM)
    return pl.pallas_call(
        kernel,
        in_specs=[smem] * scalars + [vmem] * (len(arrays) - scalars),
        out_specs=[vmem] * len(outs),
        out_shape=list(outs),
        scratch_shapes=list(scratch),
        compiler_params=pltpu.CompilerParams(vmem_limit_bytes=12 << 20),
        cost_estimate=pl.CostEstimate(
            flops=flops, bytes_accessed=nbytes, transcendentals=transcendentals
        ),
        name=name,
    )(*arrays)


def pinned(rows, columns, dtype=F32):
    return pltpu.VMEM((rows, columns), dtype)


def tiles(extent, width):
    return [slice(start, start + width) for start in range(0, extent, width)]


def previous(block, edge):
    rows = lax.broadcasted_iota(jnp.int32, block.shape, 0)
    return jnp.where(rows == 0, edge, pltpu.roll(block, 1, 0))


def following(block, edge):
    count = block.shape[0]
    rows = lax.broadcasted_iota(jnp.int32, block.shape, 0)
    return jnp.where(rows == count - 1, edge, pltpu.roll(block, count - 1, 0))


def convolve(block, low, high, taps):
    return taps[0:1] * previous(block, low) + taps[1:2] * block + taps[2:3] * following(block, high)


def mix_kernel(coarse, skip, taps, mixed, up, down):
    bins, fine = skip.shape[0], skip.shape[0] // 2
    row = lax.broadcasted_iota(jnp.int32, (bins, fine), 0)
    column = lax.broadcasted_iota(jnp.int32, (bins, fine), 1)
    twice = jnp.where((row == 2 * column) | (row == 2 * column + 1), 1.0, 0.0).astype(BF16)
    for at in tiles(skip.shape[1], 512):
        out = (dot(twice, coarse[:, at]) + skip[:, at].astype(F32)).astype(BF16)
        mixed[:, at] = out
        block = out.astype(F32)
        hidden = jax.nn.gelu(convolve(block, block[:1], block[:1], taps[:, at])).astype(BF16)
        up[:, at] = hidden[: bins - SPARE]
        down[:, at] = hidden[SPARE:]


def mix(coarse, skip, taps):
    bins, channels = skip.shape
    most = struct(bins - SPARE, channels, BF16)
    outs = [struct(bins, channels, BF16), most, most]
    flops = bins * bins * channels
    return call("mix", mix_kernel, (coarse, skip, taps), outs, flops, transcendentals=bins * channels)


def block_of(*rows):
    row = lax.broadcasted_iota(jnp.int32, (EDGE, rows[0].shape[1]), 0)
    out = jnp.zeros(row.shape, F32)
    for n, value in enumerate(rows):
        out = jnp.where(row == n, value, out)
    return out


def pack_kernel(mixed, coverage, first, last):
    bins, channels = mixed.shape
    top, bottom = mixed[:EDGE].astype(F32), mixed[bins - EDGE :].astype(F32)
    pad = jnp.zeros((1, channels - coverage.shape[2]), F32)
    low, high = [top[0:1], top[1:2]], [bottom[EDGE - 1 :], bottom[EDGE - 2 : EDGE - 1]]
    for s in range(coverage.shape[0]):
        row = coverage[s, :EDGE].astype(F32)[:1]
        low.append(jnp.concatenate([row, pad], axis=1))
        row = coverage[s, bins - EDGE :].astype(F32)[EDGE - 1 :]
        high.append(jnp.concatenate([row, pad], axis=1))
    first[...] = block_of(*low).astype(BF16)
    last[...] = block_of(*high).astype(BF16)


def pack(mixed, coverage):
    outs = [struct(EDGE, mixed.shape[1], BF16)] * 2
    return call("pack", pack_kernel, (mixed, coverage), outs, 1000 * mixed.shape[1])


def edge_kernel(mixed, low, high, taps, up, down, edges, more_up, more_down):
    bins = mixed.shape[0]
    start, end = mixed[:EDGE].astype(F32), mixed[bins - EDGE :].astype(F32)
    below, above = low[...].astype(F32), high[...].astype(F32)
    near = [below[1:2], below[0:1], start[0:1], start[1:2]]
    far = [end[EDGE - 2 : EDGE - 1], end[EDGE - 1 :], above[0:1], above[1:2]]
    rows = [
        taps[0:1] * a + taps[1:2] * b + taps[2:3] * c
        for a, b, c in (near[1:], far[:3], near[:3], far[1:])
    ]
    block = jax.nn.gelu(block_of(*rows)).astype(BF16)
    edges[...] = block
    more_up[:SPARE] = down[down.shape[0] - SPARE :]
    more_up[SPARE:] = block
    more_down[:SPARE] = up[:SPARE]
    more_down[SPARE:] = block


def edge_rows(mixed, low, high, taps, up, down):
    channels = mixed.shape[1]
    more = struct(SPARE + EDGE, channels, BF16)
    outs = [struct(EDGE, channels, BF16), more, more]
    return call("edges", edge_kernel, (mixed, low, high, taps, up, down), outs, 1000 * channels)


def log1p(e):
    series = e * (1 + e * (-1 / 2 + e * (1 / 3 + e * (-1 / 4 + e * (1 / 5 - e / 6)))))
    return jnp.where(e < 0.05, series, jnp.log(1 + e))


def head_kernel(slot, count, rows, *refs):
    order, parts = refs[0], refs[1 : 1 + count]
    weight, bias, coverage, low, high, sums, sig, lin, totals, turned, held = refs[1 + count :]
    bins = coverage.shape[1]
    nth = lax.broadcasted_iota(jnp.int32, (EDGE, 256), 0)
    held[:bins] = jnp.concatenate([parts[n][start:stop] for n, start, stop in rows[:-1]], axis=0)
    n, start, stop = rows[-1]
    edges = parts[n][start:stop].astype(F32)
    line = lax.broadcasted_iota(jnp.int32, edges.shape, 0)
    top, bottom = held[:EDGE].astype(F32), held[bins - EDGE : bins].astype(F32)
    held[:EDGE] = jnp.where(line == 0, edges[0:1], top).astype(BF16)
    held[bins - EDGE : bins] = jnp.where(line == EDGE - 1, edges[1:2], bottom).astype(BF16)
    held[bins:] = block_of(edges[2:3], edges[3:4]).astype(BF16)
    turned[...] = held[:bins].T
    totals[...] = sums[...]
    sequence = order[slot]
    for n, at in enumerate(tiles(weight.shape[1], 256)):
        logits = dot(held[...], weight[:, at]) + bias[:, at]
        e = jnp.exp(-jnp.abs(logits))
        predicted = jnp.maximum(logits, 0.0) + log1p(e)
        beside = [
            jnp.sum(jnp.where(nth == 2 + sequence, side[:, at].astype(F32), 0.0), axis=0, keepdims=True)
            for side in (low, high)
        ]
        target = jnp.concatenate([coverage[sequence, :, at].astype(F32), block_of(*beside)], axis=0)
        common = jnp.where(logits >= 0, 1.0, e) / (predicted * (1.0 + e))
        sigmoid = predicted * common
        sig[:, at] = sigmoid
        lin[:, at] = total_weight * sigmoid - target * common
        values = (predicted, target, target * jnp.log(predicted))
        for where, value in zip((16 * slot, 16 * slot + 8, 64), values):
            total = jnp.sum(value[:bins], axis=0, keepdims=True)
            for half in range(2):
                row = slice(where + 2 * n + half, where + 2 * n + half + 1)
                totals[row] = sums[row] + total[:, 128 * half : 128 * (half + 1)]


def head(slot, order, parts, rows, weight, bias, coverage, low, high, sums):
    channels, tracks = weight.shape
    bins = coverage.shape[1]
    terms = pinned(bins + EDGE, tracks)
    outs = [terms, terms, struct(72, 128), pinned(channels, bins, BF16)]
    return call(
        "head",
        functools.partial(head_kernel, slot, len(parts), rows),
        (order, *parts, weight, bias, coverage, low, high, sums),
        outs,
        2 * bins * channels * tracks,
        scalars=1,
        scratch=[pltpu.VMEM((bins + EDGE, channels), BF16)],
        transcendentals=4 * bins * tracks,
    )


def weight_kernel(factor, place, *refs):
    sigs, lins, turned = refs[:4], refs[4:8], refs[8:12]
    totals, grad, mine, other, total = refs[12:]
    own = total.shape[0] // (X * Z * CORES)
    core, z, x = place[0], place[1], place[2]

    def rows(c, j):
        k, bits = j // 8, (0, 2, 6, 4, 1, 3, 7, 5)[j % 8]
        to_x = lax.rem(x + k, X)
        to_z = lax.bitwise_xor(z, bits)
        start = ((to_x * Z + to_z) * CORES + c) * own
        return total[pl.ds(pl.multiple_of(start, 8), own), :]

    for n, at in enumerate(tiles(grad.shape[2], 256)):
        result = None
        for slot in range(4):
            ratio = []
            for row in (16 * slot + 2 * n, 16 * slot + 2 * n + 1):
                ratio.append(totals[row + 8 : row + 9] / totals[row : row + 1])
            ratio = jnp.concatenate(ratio, axis=1)
            part = factor * lins[slot][:, at] + (factor * (1.0 - total_weight) * ratio) * sigs[slot][:, at]
            part = part.astype(BF16)
            grad[slot, :, at] = part
            product = dot(turned[slot][...], part[: turned[slot].shape[1]])
            result = product if result is None else result + product
        total[...] = result
        for j in range(0, X * Z, 2):
            to = slice(j * own, (j + 2) * own)
            mine[to, at] = jnp.concatenate([rows(core, j), rows(core, j + 1)], axis=0)
            away = jnp.concatenate([rows(1 - core, j), rows(1 - core, j + 1)], axis=0)
            other[to, at] = away.astype(BF16)


def weight_parts(factor, place, sigs, lins, turned, totals):
    bins, tracks = sigs[0].shape
    channels = turned[0].shape[0]
    half = channels // CORES
    outs = [
        jax.ShapeDtypeStruct((4, bins, tracks), BF16),
        struct(half, tracks),
        struct(half, tracks, BF16),
    ]
    return call(
        "weight_parts",
        functools.partial(weight_kernel, factor),
        (place, *sigs, *lins, *turned, totals),
        outs,
        8 * bins * channels * tracks,
        scalars=1,
        scratch=[pltpu.VMEM((channels, 256), F32)],
    )


def back(grad, weight):
    return lax.dot_general(grad, weight, (((1,), (1,)), ((), ())), preferred_element_type=F32)


def loss_terms(totals):
    total = -totals[64:]
    for slot in range(4):
        predicted, target = totals[16 * slot : 16 * slot + 8], totals[16 * slot + 8 : 16 * slot + 16]
        log_total = jnp.log(predicted)
        terms = total_weight * (predicted - target * log_total) + target * log_total
        total = total + terms
    return jnp.sum(total, keepdims=True)


def three_of(value, columns):
    one = value.astype(BF16).astype(F32)
    two = (value - one).astype(BF16).astype(F32)
    return [jnp.broadcast_to(v, (1, columns)) for v in (one, two, (value - one) - two)]


def loss_of(block):
    rows = block[:, :128].astype(F32)
    return rows[2:3] + (rows[3:4] + rows[4:5])


def across_kernel(grad, weight, totals, lo, hi, loss):
    half = lo.shape[0] - EDGE
    bins = 2 * half
    value = loss_terms(totals)
    loss[...] = jnp.broadcast_to(value, loss.shape)
    for at in tiles(weight.shape[0], 512):
        out = back(grad[3], weight[at])
        rows = three_of(value, 512)
        none = jnp.zeros_like(rows[0])
        lo[:half, at] = out[:half].astype(BF16)
        hi[:half, at] = out[half:bins].astype(BF16)
        lo[half:, at] = block_of(out[bins : bins + 1], none, *rows).astype(BF16)
        hi[half:, at] = block_of(none, out[bins + 1 : bins + 2], *rows).astype(BF16)


def across_part(grad, weight, totals):
    _, rows, tracks = grad.shape
    channels = weight.shape[0]
    outs = [struct(rows // 2 + EDGE // 2, channels, BF16)] * 2 + [struct(8, 128)]
    arrays = (grad, weight, totals)
    return call("across_part", across_kernel, arrays, outs, 2 * rows * channels * tracks)


def near_kernel(grad, weight, own, lo, hi, lo_sum, hi_sum, below_more, above_more):
    half = lo.shape[0]
    bins = 2 * half
    for at in tiles(weight.shape[0], 512):
        out = back(grad[2], weight[at])
        lo_sum[:, at] = out[:half]
        hi[:, at] = out[half:bins].astype(BF16)
        above_more[:, at] = out[bins:]
        out = back(grad[1], weight[at])
        lo[:, at] = out[:half].astype(BF16)
        hi_sum[:, at] = out[half:bins]
        below_more[:, at] = out[bins:]
        own[:, at] = back(grad[0], weight[at])


def near_parts(grad, weight):
    _, rows, tracks = grad.shape
    channels = weight.shape[0]
    half = (rows - EDGE) // 2
    outs = [struct(rows, channels)] + [struct(half, channels, BF16)] * 2
    outs += [struct(half, channels)] * 2 + [struct(EDGE, channels)] * 2
    return call("near_parts", near_kernel, (grad, weight), outs, 6 * rows * channels * tracks)


def join_kernel(lo_sum, hi_sum, below_more, above_more, up, down, to_up, to_down, loss):
    half = lo_sum.shape[0]
    row = lax.broadcasted_iota(jnp.int32, (EDGE, lo_sum.shape[1]), 0)
    block = up[half:].astype(F32)
    to_up[:half] = (lo_sum[...] + up[:half].astype(F32)).astype(BF16)
    to_up[half:] = jnp.where(row < 2, above_more[...] + block, block).astype(BF16)
    to_down[:half] = (hi_sum[...] + down[:half].astype(F32)).astype(BF16)
    to_down[half:] = jnp.where(row < 2, below_more[...] + down[half:].astype(F32), 0.0).astype(BF16)
    loss[...] = jnp.broadcast_to(loss_of(up[half:]) + loss_of(down[half:]), loss.shape)


def join(*arrays):
    rows, channels = arrays[-1].shape
    outs = [struct(rows, channels, BF16)] * 2 + [struct(8, 128)]
    return call("join", join_kernel, arrays, outs, rows * channels)


def core_sum_kernel(mine, other, keep, above, below, lo, hi):
    size, half = keep.shape[0], lo.shape[0]

    def part(start, count):
        return mine[start : start + count] + other[start : start + count].astype(F32)

    keep[...] = part(0, size)
    above[...] = part(size, size)
    lo[...] = part(2 * size, half).astype(BF16)
    hi[...] = part(2 * size + half, half).astype(BF16)
    below[...] = part(3 * size, size)


def core_sum(mine, other):
    rows, tracks = mine.shape
    size = rows // X
    outs = [struct(size, tracks)] * 3 + [struct(size // 2, tracks, BF16)] * 2
    return call("core_sum", core_sum_kernel, (mine, other), outs, rows * tracks)


def pass_kernel(above, below, up, down, to_up, to_down):
    half = up.shape[0]
    to_up[:half] = (above[:half] + up[...].astype(F32)).astype(BF16)
    to_up[half:] = above[half:].astype(BF16)
    to_down[:half] = below[:half].astype(BF16)
    to_down[half:] = (below[half:] + down[...].astype(F32)).astype(BF16)


def pass_on(above, below, up, down):
    outs = [struct(*above.shape, BF16)] * 2
    return call("pass_on", pass_kernel, (above, below, up, down), outs, 2 * math.prod(above.shape))


def slope_kernel(mixed, low, high, taps, out):
    row = lax.broadcasted_iota(jnp.int32, (EDGE, 256), 0)
    for at in tiles(mixed.shape[1], 256):
        below, above = low[:, at].astype(F32), high[:, at].astype(F32)
        below = jnp.where(row == EDGE - 1, below[0:1], jnp.where(row == EDGE - 2, below[1:2], 0.0))
        above = jnp.where(row < 2, above, 0.0)
        block = jnp.concatenate([below, mixed[:, at].astype(F32), above], axis=0)
        x = convolve(block, block[:1], block[:1], taps[:, at])
        square = x * x
        t = jnp.tanh(gelu_scale * (x + gelu_cube * (x * square)))
        slope = gelu_scale * (1.0 + 3.0 * gelu_cube * square)
        out[:, at] = 0.5 * (1.0 + t) + 0.5 * x * ((1.0 - t * t) * slope)


def slopes(mixed, low, high, taps):
    bins, channels = mixed.shape
    outs = [struct(bins + 2 * EDGE, channels)]
    flops = 40 * bins * channels
    return call("slopes", slope_kernel, (mixed, low, high, taps), outs, flops, transcendentals=bins * channels)[0]


def skip_kernel(denominator, place, own, up, down, hi, lo, slope, taps, own_loss, near_loss, out, loss):
    half = hi.shape[0]
    bins = 2 * half
    far = jnp.broadcast_to(loss_of(up[half:]), loss.shape)
    loss[...] = ((own_loss[...] + far) + near_loss[...]) / denominator
    index = (place[2] * Z + place[1]) * CORES + place[0]
    has_low = jnp.where(index == 0, 0.0, 1.0)
    has_high = jnp.where(index == X * Z * CORES - 1, 0.0, 1.0)
    row = lax.broadcasted_iota(jnp.int32, (EDGE, 256), 0)
    for at in tiles(own.shape[1], 256):
        tap = taps[:, at]
        first = own[:half, at] + (up[:half, at].astype(F32) + lo[:, at].astype(F32))
        second = own[half:bins, at] + (hi[:, at].astype(F32) + down[:half, at].astype(F32))
        more = own[bins:, at] + (up[half:, at].astype(F32) + down[half:, at].astype(F32))
        before = jnp.where(row == EDGE - 1, more[0:1] * has_low, 0.0)
        after_ = jnp.where(row == 0, more[1:2] * has_high, 0.0)
        pre = jnp.concatenate([before, first, second, after_], axis=0) * slope[:, at]
        turned = jnp.concatenate([tap[2:3], tap[1:2], tap[0:1]], axis=0)
        result = convolve(pre, pre[:1], pre[:1], turned)
        out[0, :, at] = result[EDGE : EDGE + bins].astype(BF16)


def skip_gradient(denominator, *arrays):
    bins, channels = 2 * arrays[4].shape[0], arrays[4].shape[1]
    outs = [jax.ShapeDtypeStruct((1, bins, channels), BF16), struct(8, 128)]
    kernel = functools.partial(skip_kernel, denominator)
    return call("skip_gradient", kernel, arrays, outs, 12 * bins * channels, scalars=1)


def after(value, *others):
    return lax.optimization_barrier((value, *others))[0]


def shards(coarse_input, skip_input, depth_kernel, head_weight, head_bias, coverage):
    rep_count, seq_count = REP, X * Z * CORES
    denominator = (
        coverage.shape[0] * (head_weight.shape[1] * rep_count) * (coverage.shape[1] * seq_count)
    )
    factor = loss_scale / denominator
    rep, seq = lax.axis_index("rep"), lax.axis_index("seq")
    tracks = head_weight.shape[1]
    bias = head_bias[None]
    sums = jnp.zeros((72, 128), F32)

    order = jnp.stack([rep, (rep + REP - 1) % REP, (rep + 1) % REP, (rep + 2) % REP]).astype(jnp.int32)
    place = jnp.stack([seq % CORES, (seq // CORES) % Z, seq // (CORES * Z)]).astype(jnp.int32)
    coarse, order, place, sums, bias = lax.optimization_barrier(
        (coarse_input[0], order, place, sums, bias)
    )

    def head_of(slot, parts, rows, sums):
        return head(slot, order, parts, rows, head_weight, bias, coverage, low, high, sums)

    mixed, up, down = mix(coarse, skip_input[0], depth_kernel)
    bins, most = mixed.shape[0], up.shape[0]
    half, more = bins // 2, SPARE + EDGE
    below_up, above_down = move_rep(up, 1), move_rep(down, -1)
    low, high = halo(*pack(mixed, coverage))
    edges, more_up, more_down = edge_rows(mixed, low, high, depth_kernel, up, down)
    below_more, above_more = move_rep(more_up, 1), move_rep(more_down, -1)
    rows = ((0, 0, half), (1, most - half, most), (2, 0, EDGE))
    own_head = head_of(0, (up, down, edges), rows, sums)
    ready = (own_head[2], below_more, above_more)
    across_a = move_rep(after(below_up, own_head[2])[:half], 1)
    across_b = move_rep(after(above_down, own_head[2])[most - half :], -1)
    across_e = move_rep(edges, 2)
    rows = ((0, 0, most), (1, 0, SPARE), (1, SPARE, more))
    below_head = head_of(1, (below_up, below_more), rows, after(*ready))
    rows = ((1, 0, SPARE), (0, 0, most), (1, SPARE, more))
    above_head = head_of(2, (above_down, above_more), rows, below_head[2])
    rows = ((0, 0, half), (1, 0, half), (2, 0, EDGE))
    across_head = head_of(3, (across_a, across_b, across_e), rows, above_head[2])
    heads = (own_head, below_head, above_head, across_head)
    totals = seq_sum(across_head[2])
    sigs, lins, _, turned = zip(*heads)
    grad, mine, other = weight_parts(factor, place, sigs, lins, turned, totals)
    other = move_core(other)
    part_lo, part_hi, own_loss = across_part(grad, head_weight, totals)
    up, down = move_rep(part_lo, 1), move_rep(part_hi, -1)
    keep, next_x, last_x, far_lo, far_hi = core_sum(mine, after(other, part_lo))
    far_lo, far_hi = move_x(far_lo, 1), move_x(far_hi, -1)
    own, lo, hi, *sums = near_parts(after(grad, keep), head_weight)
    hi, lo = move_rep(hi, 1), move_rep(lo, -1)
    next_x, last_x = pass_on(after(next_x, own), last_x, far_lo, far_hi)
    from_last, from_next = move_x(next_x, 1), move_x(last_x, -1)
    slope = slopes(after(mixed, next_x), low, high, depth_kernel)
    to_up, to_down, near_loss = join(after(sums[0], next_x), *sums[1:], up, down)
    up, down = move_rep(to_up, 1), move_rep(to_down, -1)
    keep = after(keep, to_up, hi, lo, slope)
    keep = keep + (from_last.astype(F32) + from_next.astype(F32))
    for bits in (1, 6, 2):
        half = keep.shape[0] // 2
        sent = keep[half:].astype(BF16)
        if bits == 2:
            sent = after(sent, up, down)
        keep = keep[:half] + flip_z(sent, bits).astype(F32)
    arrays = (up, down, hi, lo, slope, depth_kernel, own_loss, near_loss)
    skip_grad, loss = skip_gradient(denominator, place, after(own, sent), *arrays)
    return (loss[0, 0], keep, skip_grad)


def solution(mesh):
    return jax.shard_map(
        shards,
        mesh=mesh,
        in_specs=(
            P("rep", "seq", None),
            P("rep", "seq", None),
            P(),
            P(None, "rep"),
            P("rep"),
            P(None, "seq", "rep"),
        ),
        out_specs=(P(), P("seq", "rep"), P("rep", "seq", None)),
        check_vma=False,
    )
```

```python
import functools
import math

import jax
import jax.numpy as jnp
from jax import lax
from jax.experimental import pallas as pl
from jax.experimental.pallas import tpu as pltpu
from jax.sharding import PartitionSpec as P

loss_scale = 4194304.0
total_weight = 0.2
X, Z, CORES, REP = 4, 8, 2, 4


def seq_index(x, z, c):
    return (x * Z + z) * CORES + c


def seq_move(block, to):
    pairs = [
        (seq_index(x, z, c), seq_index(*to(x, z, c)))
        for x in range(X)
        for z in range(Z)
        for c in range(CORES)
    ]
    return lax.ppermute(block, "seq", pairs)


def move_x(block, step):
    return seq_move(block, lambda x, z, c: ((x + step) % X, z, c))


def flip_z(block, bits):
    return seq_move(block, lambda x, z, c: (x, z ^ bits, c))


def move_core(block):
    return seq_move(block, lambda x, z, c: (x, z, 1 - c))


def move_rep(block, step):
    return lax.ppermute(block, "rep", [(i, (i + step) % REP) for i in range(REP)])


def halo(low_row, high_row):
    count = X * Z * CORES
    up = [(i, i + 1) for i in range(count - 1)]
    down = [(target, source) for source, target in up]
    return lax.ppermute(high_row, "seq", up), lax.ppermute(low_row, "seq", down)


def seq_sum(block):
    rounds = (
        (
            lambda x, z, c: (x, z, 1 - c),
            lambda x, z, c: (x, z ^ 1, c),
            lambda x, z, c: (x, z ^ 1, 1 - c),
        ),
        tuple(lambda x, z, c, k=k: ((x + k) % X, z, c) for k in (1, 2, 3)),
    )
    for moves in rounds:
        parts = [seq_move(block, to) for to in moves]
        block = (block + parts[0]) + (parts[1] + parts[2])
    for bits in (6, 2):
        block = block + flip_z(block, bits)
    return block


F32, BF16 = jnp.float32, jnp.bfloat16
gelu_scale, gelu_cube = math.sqrt(2.0 / math.pi), 0.044715
EDGE, SPARE = 16, 64


def dot(a, b):
    return jnp.dot(a, b, preferred_element_type=F32)


def struct(rows, columns, dtype=F32):
    return jax.ShapeDtypeStruct((rows, columns), dtype)


def call(name, kernel, arrays, outs, flops, scalars=0, scratch=(), transcendentals=0):
    nbytes = sum(math.prod(a.shape) * a.dtype.itemsize for a in (*arrays, *outs))
    smem = pl.BlockSpec(memory_space=pltpu.SMEM)
    vmem = pl.BlockSpec(memory_space=pltpu.VMEM)
    return pl.pallas_call(
        kernel,
        in_specs=[smem] * scalars + [vmem] * (len(arrays) - scalars),
        out_specs=[vmem] * len(outs),
        out_shape=list(outs),
        scratch_shapes=list(scratch),
        compiler_params=pltpu.CompilerParams(vmem_limit_bytes=14 << 20),
        cost_estimate=pl.CostEstimate(
            flops=flops, bytes_accessed=nbytes, transcendentals=transcendentals
        ),
        name=name,
    )(*arrays)


def pinned(rows, columns, dtype=F32):
    return pltpu.VMEM((rows, columns), dtype)


def tiles(extent, width):
    return [slice(start, start + width) for start in range(0, extent, width)]


def previous(block, edge):
    rows = lax.broadcasted_iota(jnp.int32, block.shape, 0)
    return jnp.where(rows == 0, edge, pltpu.roll(block, 1, 0))


def following(block, edge):
    count = block.shape[0]
    rows = lax.broadcasted_iota(jnp.int32, block.shape, 0)
    return jnp.where(rows == count - 1, edge, pltpu.roll(block, count - 1, 0))


def convolve(block, low, high, taps):
    return taps[0:1] * previous(block, low) + taps[1:2] * block + taps[2:3] * following(block, high)


def mix_kernel(coarse, skip, taps, mixed, up, down):
    bins, fine = skip.shape[0], skip.shape[0] // 2
    row = lax.broadcasted_iota(jnp.int32, (bins, fine), 0)
    column = lax.broadcasted_iota(jnp.int32, (bins, fine), 1)
    twice = jnp.where((row == 2 * column) | (row == 2 * column + 1), 1.0, 0.0).astype(BF16)
    for at in tiles(skip.shape[1], 512):
        out = (dot(twice, coarse[:, at]) + skip[:, at].astype(F32)).astype(BF16)
        mixed[:, at] = out
        block = out.astype(F32)
        hidden = jax.nn.gelu(convolve(block, block[:1], block[:1], taps[:, at])).astype(BF16)
        up[:, at] = hidden[: bins - SPARE]
        down[:, at] = hidden[SPARE:]


def mix(coarse, skip, taps):
    bins, channels = skip.shape
    most = struct(bins - SPARE, channels, BF16)
    outs = [struct(bins, channels, BF16), most, most]
    flops = bins * bins * channels
    return call("mix", mix_kernel, (coarse, skip, taps), outs, flops, transcendentals=bins * channels)


def block_of(*rows):
    row = lax.broadcasted_iota(jnp.int32, (EDGE, rows[0].shape[1]), 0)
    out = jnp.zeros(row.shape, F32)
    for n, value in enumerate(rows):
        out = jnp.where(row == n, value, out)
    return out


def pack_kernel(mixed, coverage, first, last):
    bins, channels = mixed.shape
    top, bottom = mixed[:EDGE].astype(F32), mixed[bins - EDGE :].astype(F32)
    pad = jnp.zeros((1, channels - coverage.shape[2]), F32)
    low, high = [top[0:1], top[1:2]], [bottom[EDGE - 1 :], bottom[EDGE - 2 : EDGE - 1]]
    for s in range(coverage.shape[0]):
        row = coverage[s, :EDGE].astype(F32)[:1]
        low.append(jnp.concatenate([row, pad], axis=1))
        row = coverage[s, bins - EDGE :].astype(F32)[EDGE - 1 :]
        high.append(jnp.concatenate([row, pad], axis=1))
    first[...] = block_of(*low).astype(BF16)
    last[...] = block_of(*high).astype(BF16)


def pack(mixed, coverage):
    outs = [struct(EDGE, mixed.shape[1], BF16)] * 2
    return call("pack", pack_kernel, (mixed, coverage), outs, 1000 * mixed.shape[1])


def edge_kernel(mixed, low, high, taps, up, down, edges, more_up, more_down):
    bins = mixed.shape[0]
    start, end = mixed[:EDGE].astype(F32), mixed[bins - EDGE :].astype(F32)
    below, above = low[...].astype(F32), high[...].astype(F32)
    near = [below[1:2], below[0:1], start[0:1], start[1:2]]
    far = [end[EDGE - 2 : EDGE - 1], end[EDGE - 1 :], above[0:1], above[1:2]]
    rows = [
        taps[0:1] * a + taps[1:2] * b + taps[2:3] * c
        for a, b, c in (near[1:], far[:3], near[:3], far[1:])
    ]
    block = jax.nn.gelu(block_of(*rows)).astype(BF16)
    edges[...] = block
    more_up[:SPARE] = down[down.shape[0] - SPARE :]
    more_up[SPARE:] = block
    more_down[:SPARE] = up[:SPARE]
    more_down[SPARE:] = block


def edge_rows(mixed, low, high, taps, up, down):
    channels = mixed.shape[1]
    more = struct(SPARE + EDGE, channels, BF16)
    outs = [struct(EDGE, channels, BF16), more, more]
    return call("edges", edge_kernel, (mixed, low, high, taps, up, down), outs, 1000 * channels)


def log1p(e):
    series = e * (1 + e * (-1 / 2 + e * (1 / 3 + e * (-1 / 4 + e * (1 / 5 - e / 6)))))
    return jnp.where(e < 0.05, series, jnp.log(1 + e))


def head_kernel(slot, count, rows, *refs):
    order, parts = refs[0], refs[1 : 1 + count]
    weight, bias, coverage, low, high, sums, sig, lin, totals, turned, held = refs[1 + count :]
    bins = coverage.shape[1]
    nth = lax.broadcasted_iota(jnp.int32, (EDGE, 256), 0)
    held[:bins] = jnp.concatenate([parts[n][start:stop] for n, start, stop in rows[:-1]], axis=0)
    n, start, stop = rows[-1]
    edges = parts[n][start:stop].astype(F32)
    line = lax.broadcasted_iota(jnp.int32, edges.shape, 0)
    top, bottom = held[:EDGE].astype(F32), held[bins - EDGE : bins].astype(F32)
    held[:EDGE] = jnp.where(line == 0, edges[0:1], top).astype(BF16)
    held[bins - EDGE : bins] = jnp.where(line == EDGE - 1, edges[1:2], bottom).astype(BF16)
    held[bins:] = block_of(edges[2:3], edges[3:4]).astype(BF16)
    turned[...] = held[:bins].T
    totals[...] = sums[...]
    sequence = order[slot]
    for n, at in enumerate(tiles(weight.shape[1], 256)):
        logits = dot(held[...], weight[:, at]) + bias[:, at]
        e = jnp.exp(-jnp.abs(logits))
        predicted = jnp.maximum(logits, 0.0) + log1p(e)
        beside = [
            jnp.sum(jnp.where(nth == 2 + sequence, side[:, at].astype(F32), 0.0), axis=0, keepdims=True)
            for side in (low, high)
        ]
        target = jnp.concatenate([coverage[sequence, :, at].astype(F32), block_of(*beside)], axis=0)
        common = jnp.where(logits >= 0, 1.0, e) / (predicted * (1.0 + e))
        sigmoid = predicted * common
        sig[:, at] = sigmoid
        lin[:, at] = total_weight * sigmoid - target * common
        values = (predicted, target, target * jnp.log(predicted))
        for where, value in zip((16 * slot, 16 * slot + 8, 64), values):
            total = jnp.sum(value[:bins], axis=0, keepdims=True)
            for half in range(2):
                row = slice(where + 2 * n + half, where + 2 * n + half + 1)
                totals[row] = sums[row] + total[:, 128 * half : 128 * (half + 1)]


def head(slot, order, parts, rows, weight, bias, coverage, low, high, sums):
    channels, tracks = weight.shape
    bins = coverage.shape[1]
    terms = pinned(bins + EDGE, tracks)
    outs = [terms, terms, struct(72, 128), pinned(channels, bins, BF16)]
    return call(
        "head",
        functools.partial(head_kernel, slot, len(parts), rows),
        (order, *parts, weight, bias, coverage, low, high, sums),
        outs,
        2 * bins * channels * tracks,
        scalars=1,
        scratch=[pltpu.VMEM((bins + EDGE, channels), BF16)],
        transcendentals=4 * bins * tracks,
    )


def weight_kernel(factor, place, *refs):
    sigs, lins, turned = refs[:4], refs[4:8], refs[8:12]
    totals, grad, mine, other, total, across = refs[12:]
    own = total.shape[0] // (X * Z * CORES)
    core, z, x = place[0], place[1], place[2]

    def rows(c, j):
        k, bits = j // 8, (0, 2, 6, 4, 1, 3, 7, 5)[j % 8]
        to_x = lax.rem(x + k, X)
        to_z = lax.bitwise_xor(z, bits)
        start = ((to_x * Z + to_z) * CORES + c) * own
        return total[pl.ds(pl.multiple_of(start, 8), own), :]

    bins = turned[0].shape[1]
    for slot in range(4):
        across[:, slot * bins : (slot + 1) * bins] = turned[slot][...]
    for n, at in enumerate(tiles(grad.shape[2], 256)):
        parts = []
        for slot in range(4):
            ratio = []
            for row in (16 * slot + 2 * n, 16 * slot + 2 * n + 1):
                ratio.append(totals[row + 8 : row + 9] / totals[row : row + 1])
            ratio = jnp.concatenate(ratio, axis=1)
            part = factor * lins[slot][:, at] + (factor * (1.0 - total_weight) * ratio) * sigs[slot][:, at]
            part = part.astype(BF16)
            grad[slot, :, at] = part
            parts.append(part[:bins])
        total[...] = dot(across[...], jnp.concatenate(parts, axis=0))
        for j in range(0, X * Z, 2):
            to = slice(j * own, (j + 2) * own)
            mine[to, at] = jnp.concatenate([rows(core, j), rows(core, j + 1)], axis=0)
            away = jnp.concatenate([rows(1 - core, j), rows(1 - core, j + 1)], axis=0)
            other[to, at] = away.astype(BF16)


def weight_parts(factor, place, sigs, lins, turned, totals):
    bins, tracks = sigs[0].shape
    channels = turned[0].shape[0]
    half = channels // CORES
    outs = [
        jax.ShapeDtypeStruct((4, bins, tracks), BF16),
        struct(half, tracks),
        struct(half, tracks, BF16),
    ]
    return call(
        "weight_parts",
        functools.partial(weight_kernel, factor),
        (place, *sigs, *lins, *turned, totals),
        outs,
        8 * bins * channels * tracks,
        scalars=1,
        scratch=[pltpu.VMEM((channels, 256), F32), pltpu.VMEM((channels, 4 * turned[0].shape[1]), BF16)],
    )


def back(grad, weight):
    return lax.dot_general(grad, weight, (((1,), (1,)), ((), ())), preferred_element_type=F32)


def loss_terms(totals):
    total = -totals[64:]
    for slot in range(4):
        predicted, target = totals[16 * slot : 16 * slot + 8], totals[16 * slot + 8 : 16 * slot + 16]
        log_total = jnp.log(predicted)
        terms = total_weight * (predicted - target * log_total) + target * log_total
        total = total + terms
    return jnp.sum(total, keepdims=True)


def three_of(value, columns):
    one = value.astype(BF16).astype(F32)
    two = (value - one).astype(BF16).astype(F32)
    return [jnp.broadcast_to(v, (1, columns)) for v in (one, two, (value - one) - two)]


def loss_of(block):
    rows = block[:, :128].astype(F32)
    return rows[2:3] + (rows[3:4] + rows[4:5])


def across_kernel(grad, weight, totals, lo, hi, loss):
    half = lo.shape[0] - EDGE
    bins = 2 * half
    value = loss_terms(totals)
    loss[...] = jnp.broadcast_to(value, loss.shape)
    for at in tiles(weight.shape[0], 512):
        out = back(grad[3], weight[at])
        rows = three_of(value, 512)
        none = jnp.zeros_like(rows[0])
        lo[:half, at] = out[:half].astype(BF16)
        hi[:half, at] = out[half:bins].astype(BF16)
        lo[half:, at] = block_of(out[bins : bins + 1], none, *rows).astype(BF16)
        hi[half:, at] = block_of(none, out[bins + 1 : bins + 2], *rows).astype(BF16)


def across_part(grad, weight, totals):
    _, rows, tracks = grad.shape
    channels = weight.shape[0]
    outs = [struct(rows // 2 + EDGE // 2, channels, BF16)] * 2 + [struct(8, 128)]
    arrays = (grad, weight, totals)
    return call("across_part", across_kernel, arrays, outs, 2 * rows * channels * tracks)


def near_kernel(grad, weight, own, lo, hi, lo_sum, hi_sum, below_more, above_more):
    half = lo.shape[0]
    bins = 2 * half
    for at in tiles(weight.shape[0], 512):
        out = back(grad[2], weight[at])
        lo_sum[:, at] = out[:half]
        hi[:, at] = out[half:bins].astype(BF16)
        above_more[:, at] = out[bins:]
        out = back(grad[1], weight[at])
        lo[:, at] = out[:half].astype(BF16)
        hi_sum[:, at] = out[half:bins]
        below_more[:, at] = out[bins:]
        own[:, at] = back(grad[0], weight[at])


def near_parts(grad, weight):
    _, rows, tracks = grad.shape
    channels = weight.shape[0]
    half = (rows - EDGE) // 2
    outs = [struct(rows, channels)] + [struct(half, channels, BF16)] * 2
    outs += [struct(half, channels)] * 2 + [struct(EDGE, channels)] * 2
    return call("near_parts", near_kernel, (grad, weight), outs, 6 * rows * channels * tracks)


def join_kernel(lo_sum, hi_sum, below_more, above_more, up, down, to_up, to_down, loss):
    half = lo_sum.shape[0]
    row = lax.broadcasted_iota(jnp.int32, (EDGE, lo_sum.shape[1]), 0)
    block = up[half:].astype(F32)
    to_up[:half] = (lo_sum[...] + up[:half].astype(F32)).astype(BF16)
    to_up[half:] = jnp.where(row < 2, above_more[...] + block, block).astype(BF16)
    to_down[:half] = (hi_sum[...] + down[:half].astype(F32)).astype(BF16)
    to_down[half:] = jnp.where(row < 2, below_more[...] + down[half:].astype(F32), 0.0).astype(BF16)
    loss[...] = jnp.broadcast_to(loss_of(up[half:]) + loss_of(down[half:]), loss.shape)


def join(*arrays):
    rows, channels = arrays[-1].shape
    outs = [struct(rows, channels, BF16)] * 2 + [struct(8, 128)]
    return call("join", join_kernel, arrays, outs, rows * channels)


def core_sum_kernel(mine, other, keep, above, below, lo, hi):
    size, half = keep.shape[0], lo.shape[0]

    def part(start, count):
        return mine[start : start + count] + other[start : start + count].astype(F32)

    keep[...] = part(0, size)
    above[...] = part(size, size)
    lo[...] = part(2 * size, half).astype(BF16)
    hi[...] = part(2 * size + half, half).astype(BF16)
    below[...] = part(3 * size, size)


def core_sum(mine, other):
    rows, tracks = mine.shape
    size = rows // X
    outs = [struct(size, tracks)] * 3 + [struct(size // 2, tracks, BF16)] * 2
    return call("core_sum", core_sum_kernel, (mine, other), outs, rows * tracks)


def pass_kernel(above, below, up, down, to_up, to_down):
    half = up.shape[0]
    to_up[:half] = (above[:half] + up[...].astype(F32)).astype(BF16)
    to_up[half:] = above[half:].astype(BF16)
    to_down[:half] = below[:half].astype(BF16)
    to_down[half:] = (below[half:] + down[...].astype(F32)).astype(BF16)


def pass_on(above, below, up, down):
    outs = [struct(*above.shape, BF16)] * 2
    return call("pass_on", pass_kernel, (above, below, up, down), outs, 2 * math.prod(above.shape))


def slope_kernel(mixed, low, high, taps, out):
    row = lax.broadcasted_iota(jnp.int32, (EDGE, 256), 0)
    for at in tiles(mixed.shape[1], 256):
        below, above = low[:, at].astype(F32), high[:, at].astype(F32)
        below = jnp.where(row == EDGE - 1, below[0:1], jnp.where(row == EDGE - 2, below[1:2], 0.0))
        above = jnp.where(row < 2, above, 0.0)
        block = jnp.concatenate([below, mixed[:, at].astype(F32), above], axis=0)
        x = convolve(block, block[:1], block[:1], taps[:, at])
        square = x * x
        t = jnp.tanh(gelu_scale * (x + gelu_cube * (x * square)))
        slope = gelu_scale * (1.0 + 3.0 * gelu_cube * square)
        out[:, at] = 0.5 * (1.0 + t) + 0.5 * x * ((1.0 - t * t) * slope)


def slopes(mixed, low, high, taps):
    bins, channels = mixed.shape
    outs = [struct(bins + 2 * EDGE, channels)]
    flops = 40 * bins * channels
    return call("slopes", slope_kernel, (mixed, low, high, taps), outs, flops, transcendentals=bins * channels)[0]


def skip_kernel(denominator, place, own, up, down, hi, lo, slope, taps, own_loss, near_loss, out, loss):
    half = hi.shape[0]
    bins = 2 * half
    far = jnp.broadcast_to(loss_of(up[half:]), loss.shape)
    loss[...] = ((own_loss[...] + far) + near_loss[...]) / denominator
    index = (place[2] * Z + place[1]) * CORES + place[0]
    has_low = jnp.where(index == 0, 0.0, 1.0)
    has_high = jnp.where(index == X * Z * CORES - 1, 0.0, 1.0)
    row = lax.broadcasted_iota(jnp.int32, (EDGE, 256), 0)
    for at in tiles(own.shape[1], 256):
        tap = taps[:, at]
        first = own[:half, at] + (up[:half, at].astype(F32) + lo[:, at].astype(F32))
        second = own[half:bins, at] + (hi[:, at].astype(F32) + down[:half, at].astype(F32))
        more = own[bins:, at] + (up[half:, at].astype(F32) + down[half:, at].astype(F32))
        before = jnp.where(row == EDGE - 1, more[0:1] * has_low, 0.0)
        after_ = jnp.where(row == 0, more[1:2] * has_high, 0.0)
        pre = jnp.concatenate([before, first, second, after_], axis=0) * slope[:, at]
        turned = jnp.concatenate([tap[2:3], tap[1:2], tap[0:1]], axis=0)
        result = convolve(pre, pre[:1], pre[:1], turned)
        out[0, :, at] = result[EDGE : EDGE + bins].astype(BF16)


def skip_gradient(denominator, *arrays):
    bins, channels = 2 * arrays[4].shape[0], arrays[4].shape[1]
    outs = [jax.ShapeDtypeStruct((1, bins, channels), BF16), struct(8, 128)]
    kernel = functools.partial(skip_kernel, denominator)
    return call("skip_gradient", kernel, arrays, outs, 12 * bins * channels, scalars=1)


def after(value, *others):
    return lax.optimization_barrier((value, *others))[0]


def shards(coarse_input, skip_input, depth_kernel, head_weight, head_bias, coverage):
    rep_count, seq_count = REP, X * Z * CORES
    denominator = (
        coverage.shape[0] * (head_weight.shape[1] * rep_count) * (coverage.shape[1] * seq_count)
    )
    factor = loss_scale / denominator
    rep, seq = lax.axis_index("rep"), lax.axis_index("seq")
    tracks = head_weight.shape[1]
    bias = head_bias[None]
    sums = jnp.zeros((72, 128), F32)

    order = jnp.stack([rep, (rep + REP - 1) % REP, (rep + 1) % REP, (rep + 2) % REP]).astype(jnp.int32)
    place = jnp.stack([seq % CORES, (seq // CORES) % Z, seq // (CORES * Z)]).astype(jnp.int32)
    coarse, order, place, sums, bias = lax.optimization_barrier(
        (coarse_input[0], order, place, sums, bias)
    )

    def head_of(slot, parts, rows, sums):
        return head(slot, order, parts, rows, head_weight, bias, coverage, low, high, sums)

    mixed, up, down = mix(coarse, skip_input[0], depth_kernel)
    bins, most = mixed.shape[0], up.shape[0]
    half, more = bins // 2, SPARE + EDGE
    below_up, above_down = move_rep(up, 1), move_rep(down, -1)
    low, high = halo(*pack(mixed, coverage))
    edges, more_up, more_down = edge_rows(mixed, low, high, depth_kernel, up, down)
    below_more, above_more = move_rep(more_up, 1), move_rep(more_down, -1)
    rows = ((0, 0, half), (1, most - half, most), (2, 0, EDGE))
    own_head = head_of(0, (up, down, edges), rows, sums)
    ready = (own_head[2], below_more, above_more)
    across_a = move_rep(after(below_up, more_up)[:half], 1)
    across_b = move_rep(after(above_down, more_up)[most - half :], -1)
    across_e = move_rep(edges, 2)
    rows = ((0, 0, most), (1, 0, SPARE), (1, SPARE, more))
    below_head = head_of(1, (below_up, below_more), rows, after(*ready))
    rows = ((1, 0, SPARE), (0, 0, most), (1, SPARE, more))
    above_head = head_of(2, (above_down, above_more), rows, below_head[2])
    rows = ((0, 0, half), (1, 0, half), (2, 0, EDGE))
    across_head = head_of(3, (across_a, across_b, across_e), rows, above_head[2])
    heads = (own_head, below_head, above_head, across_head)
    totals = seq_sum(across_head[2])
    sigs, lins, _, turned = zip(*heads)
    grad, mine, other = weight_parts(factor, place, sigs, lins, turned, totals)
    other = move_core(other)
    part_lo, part_hi, own_loss = across_part(grad, head_weight, totals)
    up, down = move_rep(part_lo, 1), move_rep(part_hi, -1)
    keep, next_x, last_x, far_lo, far_hi = core_sum(mine, after(other, part_lo))
    far_lo, far_hi = move_x(far_lo, 1), move_x(far_hi, -1)
    own, lo, hi, *sums = near_parts(after(grad, keep), head_weight)
    hi, lo = move_rep(hi, 1), move_rep(lo, -1)
    next_x, last_x = pass_on(after(next_x, own), last_x, far_lo, far_hi)
    from_last, from_next = move_x(next_x, 1), move_x(last_x, -1)
    slope = slopes(after(mixed, next_x), low, high, depth_kernel)
    to_up, to_down, near_loss = join(after(sums[0], next_x), *sums[1:], up, down)
    up, down = move_rep(to_up, 1), move_rep(to_down, -1)
    keep = after(keep, to_up, hi, lo, slope)
    keep = keep + (from_last.astype(F32) + from_next.astype(F32))
    for bits in (1, 6, 2):
        half = keep.shape[0] // 2
        sent = keep[half:].astype(BF16)
        if bits == 2:
            sent = after(sent, up, down)
        keep = keep[:half] + flip_z(sent, bits).astype(F32)
    arrays = (up, down, hi, lo, slope, depth_kernel, own_loss, near_loss)
    skip_grad, loss = skip_gradient(denominator, place, after(own, sent), *arrays)
    return (loss[0, 0], keep, skip_grad)


def solution(mesh):
    return jax.shard_map(
        shards,
        mesh=mesh,
        in_specs=(
            P("rep", "seq", None),
            P("rep", "seq", None),
            P(),
            P(None, "rep"),
            P("rep"),
            P(None, "seq", "rep"),
        ),
        out_specs=(P(), P("seq", "rep"), P("rep", "seq", None)),
        check_vma=False,
    )
```

```python
import functools
import math

import jax
import jax.numpy as jnp
from jax import lax
from jax.experimental import pallas as pl
from jax.experimental.pallas import tpu as pltpu
from jax.sharding import PartitionSpec as P

loss_scale = 4194304.0
total_weight = 0.2
X, Z, CORES, REP = 4, 8, 2, 4


def seq_index(x, z, c):
    return (x * Z + z) * CORES + c


def seq_move(block, to):
    pairs = [
        (seq_index(x, z, c), seq_index(*to(x, z, c)))
        for x in range(X)
        for z in range(Z)
        for c in range(CORES)
    ]
    return lax.ppermute(block, "seq", pairs)


def move_x(block, step):
    return seq_move(block, lambda x, z, c: ((x + step) % X, z, c))


def flip_z(block, bits):
    return seq_move(block, lambda x, z, c: (x, z ^ bits, c))


def move_core(block):
    return seq_move(block, lambda x, z, c: (x, z, 1 - c))


def move_rep(block, step):
    return lax.ppermute(block, "rep", [(i, (i + step) % REP) for i in range(REP)])


def halo(low_row, high_row):
    count = X * Z * CORES
    up = [(i, i + 1) for i in range(count - 1)]
    down = [(target, source) for source, target in up]
    return lax.ppermute(high_row, "seq", up), lax.ppermute(low_row, "seq", down)


def seq_sum(block):
    rounds = (
        (
            lambda x, z, c: (x, z, 1 - c),
            lambda x, z, c: (x, z ^ 1, c),
            lambda x, z, c: (x, z ^ 1, 1 - c),
        ),
        tuple(lambda x, z, c, k=k: ((x + k) % X, z, c) for k in (1, 2, 3)),
    )
    for moves in rounds:
        parts = [seq_move(block, to) for to in moves]
        block = (block + parts[0]) + (parts[1] + parts[2])
    for bits in (6, 2):
        block = block + flip_z(block, bits)
    return block


F32, BF16 = jnp.float32, jnp.bfloat16
gelu_scale, gelu_cube = math.sqrt(2.0 / math.pi), 0.044715
EDGE, SPARE = 16, 64


def dot(a, b):
    return jnp.dot(a, b, preferred_element_type=F32)


def struct(rows, columns, dtype=F32):
    return jax.ShapeDtypeStruct((rows, columns), dtype)


def call(name, kernel, arrays, outs, flops, scalars=0, scratch=(), transcendentals=0):
    nbytes = sum(math.prod(a.shape) * a.dtype.itemsize for a in (*arrays, *outs))
    smem = pl.BlockSpec(memory_space=pltpu.SMEM)
    vmem = pl.BlockSpec(memory_space=pltpu.VMEM)
    return pl.pallas_call(
        kernel,
        in_specs=[smem] * scalars + [vmem] * (len(arrays) - scalars),
        out_specs=[vmem] * len(outs),
        out_shape=list(outs),
        scratch_shapes=list(scratch),
        compiler_params=pltpu.CompilerParams(vmem_limit_bytes=14 << 20),
        cost_estimate=pl.CostEstimate(
            flops=flops, bytes_accessed=nbytes, transcendentals=transcendentals
        ),
        name=name,
    )(*arrays)


def pinned(rows, columns, dtype=F32):
    return pltpu.VMEM((rows, columns), dtype)


def tiles(extent, width):
    return [slice(start, start + width) for start in range(0, extent, width)]


def previous(block, edge):
    rows = lax.broadcasted_iota(jnp.int32, block.shape, 0)
    return jnp.where(rows == 0, edge, pltpu.roll(block, 1, 0))


def following(block, edge):
    count = block.shape[0]
    rows = lax.broadcasted_iota(jnp.int32, block.shape, 0)
    return jnp.where(rows == count - 1, edge, pltpu.roll(block, count - 1, 0))


def convolve(block, low, high, taps):
    return taps[0:1] * previous(block, low) + taps[1:2] * block + taps[2:3] * following(block, high)


def mix_kernel(coarse_far, skip_far, taps, mixed, up, down, coarse, skip, arrived):
    copies = []
    for n, at in enumerate(tiles(skip.shape[1], 512)):
        for k, (far, near) in enumerate(((coarse_far, coarse), (skip_far, skip))):
            copies.append(pltpu.make_async_copy(far.at[:, at], near.at[:, at], arrived.at[n, k]))
            copies[-1].start()
    bins, fine = skip.shape[0], skip.shape[0] // 2
    row = lax.broadcasted_iota(jnp.int32, (bins, fine), 0)
    column = lax.broadcasted_iota(jnp.int32, (bins, fine), 1)
    twice = jnp.where((row == 2 * column) | (row == 2 * column + 1), 1.0, 0.0).astype(BF16)
    for n, at in enumerate(tiles(skip.shape[1], 512)):
        copies[2 * n].wait()
        copies[2 * n + 1].wait()
        out = (dot(twice, coarse[:, at]) + skip[:, at].astype(F32)).astype(BF16)
        mixed[:, at] = out
        block = out.astype(F32)
        hidden = jax.nn.gelu(convolve(block, block[:1], block[:1], taps[:, at])).astype(BF16)
        up[:, at] = hidden[: bins - SPARE]
        down[:, at] = hidden[SPARE:]


def mix(coarse, skip, taps):
    bins, channels = skip.shape
    most = struct(bins - SPARE, channels, BF16)
    outs = [struct(bins, channels, BF16), most, most]
    vmem, far = pl.BlockSpec(memory_space=pltpu.VMEM), pl.BlockSpec(memory_space=pltpu.HBM)
    return pl.pallas_call(
        mix_kernel,
        in_specs=[far, far, vmem],
        out_specs=[vmem] * 3,
        out_shape=outs,
        scratch_shapes=[
            pltpu.VMEM(coarse.shape, BF16),
            pltpu.VMEM(skip.shape, BF16),
            pltpu.SemaphoreType.DMA((3, 2)),
        ],
        compiler_params=pltpu.CompilerParams(vmem_limit_bytes=14 << 20),
        cost_estimate=pl.CostEstimate(
            flops=bins * bins * channels,
            bytes_accessed=7 * bins * channels,
            transcendentals=bins * channels,
        ),
        name="mix",
    )(*(pltpu.with_memory_space_constraint(x, pltpu.HBM) for x in (coarse, skip)), taps)


def block_of(*rows):
    row = lax.broadcasted_iota(jnp.int32, (EDGE, rows[0].shape[1]), 0)
    out = jnp.zeros(row.shape, F32)
    for n, value in enumerate(rows):
        out = jnp.where(row == n, value, out)
    return out


def pack_kernel(mixed, coverage, first, last):
    bins, channels = mixed.shape
    top, bottom = mixed[:EDGE].astype(F32), mixed[bins - EDGE :].astype(F32)
    pad = jnp.zeros((1, channels - coverage.shape[2]), F32)
    low, high = [top[0:1], top[1:2]], [bottom[EDGE - 1 :], bottom[EDGE - 2 : EDGE - 1]]
    for s in range(coverage.shape[0]):
        row = coverage[s, :EDGE].astype(F32)[:1]
        low.append(jnp.concatenate([row, pad], axis=1))
        row = coverage[s, bins - EDGE :].astype(F32)[EDGE - 1 :]
        high.append(jnp.concatenate([row, pad], axis=1))
    first[...] = block_of(*low).astype(BF16)
    last[...] = block_of(*high).astype(BF16)


def pack(mixed, coverage):
    outs = [struct(EDGE, mixed.shape[1], BF16)] * 2
    return call("pack", pack_kernel, (mixed, coverage), outs, 1000 * mixed.shape[1])


def edge_kernel(mixed, low, high, taps, up, down, edges, more_up, more_down):
    bins = mixed.shape[0]
    start, end = mixed[:EDGE].astype(F32), mixed[bins - EDGE :].astype(F32)
    below, above = low[...].astype(F32), high[...].astype(F32)
    near = [below[1:2], below[0:1], start[0:1], start[1:2]]
    far = [end[EDGE - 2 : EDGE - 1], end[EDGE - 1 :], above[0:1], above[1:2]]
    rows = [
        taps[0:1] * a + taps[1:2] * b + taps[2:3] * c
        for a, b, c in (near[1:], far[:3], near[:3], far[1:])
    ]
    block = jax.nn.gelu(block_of(*rows)).astype(BF16)
    edges[...] = block
    more_up[:SPARE] = down[down.shape[0] - SPARE :]
    more_up[SPARE:] = block
    more_down[:SPARE] = up[:SPARE]
    more_down[SPARE:] = block


def edge_rows(mixed, low, high, taps, up, down):
    channels = mixed.shape[1]
    more = struct(SPARE + EDGE, channels, BF16)
    outs = [struct(EDGE, channels, BF16), more, more]
    return call("edges", edge_kernel, (mixed, low, high, taps, up, down), outs, 1000 * channels)


def log1p(e):
    series = e * (1 + e * (-1 / 2 + e * (1 / 3 + e * (-1 / 4 + e * (1 / 5 - e / 6)))))
    return jnp.where(e < 0.05, series, jnp.log(1 + e))


def head_kernel(slot, count, rows, *refs):
    order, parts = refs[0], refs[1 : 1 + count]
    weight, bias, coverage, low, high, sums, sig, lin, totals, turned, held = refs[1 + count :]
    bins = coverage.shape[1]
    nth = lax.broadcasted_iota(jnp.int32, (EDGE, 256), 0)
    held[:bins] = jnp.concatenate([parts[n][start:stop] for n, start, stop in rows[:-1]], axis=0)
    n, start, stop = rows[-1]
    edges = parts[n][start:stop].astype(F32)
    line = lax.broadcasted_iota(jnp.int32, edges.shape, 0)
    top, bottom = held[:EDGE].astype(F32), held[bins - EDGE : bins].astype(F32)
    held[:EDGE] = jnp.where(line == 0, edges[0:1], top).astype(BF16)
    held[bins - EDGE : bins] = jnp.where(line == EDGE - 1, edges[1:2], bottom).astype(BF16)
    held[bins:] = block_of(edges[2:3], edges[3:4]).astype(BF16)
    turned[...] = held[:bins].T
    totals[...] = sums[...]
    sequence = order[slot]
    for n, at in enumerate(tiles(weight.shape[1], 256)):
        logits = dot(held[...], weight[:, at]) + bias[:, at]
        e = jnp.exp(-jnp.abs(logits))
        predicted = jnp.maximum(logits, 0.0) + log1p(e)
        beside = [
            jnp.sum(jnp.where(nth == 2 + sequence, side[:, at].astype(F32), 0.0), axis=0, keepdims=True)
            for side in (low, high)
        ]
        target = jnp.concatenate([coverage[sequence, :, at].astype(F32), block_of(*beside)], axis=0)
        common = jnp.where(logits >= 0, 1.0, e) / (predicted * (1.0 + e))
        sigmoid = predicted * common
        sig[:, at] = sigmoid
        lin[:, at] = total_weight * sigmoid - target * common
        values = (predicted, target, target * jnp.log(predicted))
        for where, value in zip((16 * slot, 16 * slot + 8, 64), values):
            total = jnp.sum(value[:bins], axis=0, keepdims=True)
            for half in range(2):
                row = slice(where + 2 * n + half, where + 2 * n + half + 1)
                totals[row] = sums[row] + total[:, 128 * half : 128 * (half + 1)]


def head(slot, order, parts, rows, weight, bias, coverage, low, high, sums):
    channels, tracks = weight.shape
    bins = coverage.shape[1]
    terms = pinned(bins + EDGE, tracks)
    outs = [terms, terms, struct(72, 128), pinned(channels, bins, BF16)]
    return call(
        "head",
        functools.partial(head_kernel, slot, len(parts), rows),
        (order, *parts, weight, bias, coverage, low, high, sums),
        outs,
        2 * bins * channels * tracks,
        scalars=1,
        scratch=[pltpu.VMEM((bins + EDGE, channels), BF16)],
        transcendentals=4 * bins * tracks,
    )


def weight_kernel(factor, place, *refs):
    sigs, lins, turned = refs[:4], refs[4:8], refs[8:12]
    totals, grad, mine, other, total, across = refs[12:]
    own = total.shape[0] // (X * Z * CORES)
    core, z, x = place[0], place[1], place[2]

    def rows(n, c, j):
        k, bits = j // 8, (0, 2, 6, 4, 1, 3, 7, 5)[j % 8]
        to_x = lax.rem(x + k, X)
        to_z = lax.bitwise_xor(z, bits)
        start = ((to_x * Z + to_z) * CORES + c) * own
        return total[pl.ds(pl.multiple_of(start, 8), own), :]

    bins = turned[0].shape[1]
    for slot in range(4):
        across[:, slot * bins : (slot + 1) * bins] = turned[slot][...]
    for n, at in enumerate(tiles(grad.shape[2], 256)):
        parts = []
        for slot in range(4):
            ratio = []
            for row in (16 * slot + 2 * n, 16 * slot + 2 * n + 1):
                ratio.append(totals[row + 8 : row + 9] / totals[row : row + 1])
            ratio = jnp.concatenate(ratio, axis=1)
            part = factor * lins[slot][:, at] + (factor * (1.0 - total_weight) * ratio) * sigs[slot][:, at]
            part = part.astype(BF16)
            grad[slot, :, at] = part
            parts.append(part[:bins])
        total[...] = dot(across[...], jnp.concatenate(parts, axis=0))
        for j in range(0, X * Z, 2):
            to = slice(j * own, (j + 2) * own)
            mine[to, at] = jnp.concatenate([rows(n, core, j), rows(n, core, j + 1)], axis=0)
            away = jnp.concatenate([rows(n, 1 - core, j), rows(n, 1 - core, j + 1)], axis=0)
            other[to, at] = away.astype(BF16)


def weight_parts(factor, place, sigs, lins, turned, totals):
    bins, tracks = sigs[0].shape
    channels = turned[0].shape[0]
    half = channels // CORES
    outs = [
        jax.ShapeDtypeStruct((4, bins, tracks), BF16),
        struct(half, tracks),
        struct(half, tracks, BF16),
    ]
    return call(
        "weight_parts",
        functools.partial(weight_kernel, factor),
        (place, *sigs, *lins, *turned, totals),
        outs,
        8 * bins * channels * tracks,
        scalars=1,
        scratch=[pltpu.VMEM((channels, 256), F32), pltpu.VMEM((channels, 4 * turned[0].shape[1]), BF16)],
    )


def back(grad, weight):
    return lax.dot_general(grad, weight, (((1,), (1,)), ((), ())), preferred_element_type=F32)


def loss_terms(totals):
    total = -totals[64:]
    for slot in range(4):
        predicted, target = totals[16 * slot : 16 * slot + 8], totals[16 * slot + 8 : 16 * slot + 16]
        log_total = jnp.log(predicted)
        terms = total_weight * (predicted - target * log_total) + target * log_total
        total = total + terms
    return jnp.sum(total, keepdims=True)


def three_of(value, columns):
    one = value.astype(BF16).astype(F32)
    two = (value - one).astype(BF16).astype(F32)
    return [jnp.broadcast_to(v, (1, columns)) for v in (one, two, (value - one) - two)]


def loss_of(block):
    rows = block[:, :128].astype(F32)
    return rows[2:3] + (rows[3:4] + rows[4:5])


def across_kernel(grad, weight, totals, lo, hi, loss):
    half = lo.shape[0] - EDGE
    bins = 2 * half
    value = loss_terms(totals)
    loss[...] = jnp.broadcast_to(value, loss.shape)
    for at in tiles(weight.shape[0], 512):
        out = back(grad[3], weight[at])
        rows = three_of(value, 512)
        none = jnp.zeros_like(rows[0])
        lo[:half, at] = out[:half].astype(BF16)
        hi[:half, at] = out[half:bins].astype(BF16)
        lo[half:, at] = block_of(out[bins : bins + 1], none, *rows).astype(BF16)
        hi[half:, at] = block_of(none, out[bins + 1 : bins + 2], *rows).astype(BF16)


def across_part(grad, weight, totals):
    _, rows, tracks = grad.shape
    channels = weight.shape[0]
    outs = [struct(rows // 2 + EDGE // 2, channels, BF16)] * 2 + [struct(8, 128)]
    arrays = (grad, weight, totals)
    return call("across_part", across_kernel, arrays, outs, 2 * rows * channels * tracks)


def near_kernel(grad, weight, own, lo, hi, lo_sum, hi_sum, below_more, above_more):
    half = lo.shape[0]
    bins = 2 * half
    for at in tiles(weight.shape[0], 512):
        out = back(grad[2], weight[at])
        lo_sum[:, at] = out[:half]
        hi[:, at] = out[half:bins].astype(BF16)
        above_more[:, at] = out[bins:]
        out = back(grad[1], weight[at])
        lo[:, at] = out[:half].astype(BF16)
        hi_sum[:, at] = out[half:bins]
        below_more[:, at] = out[bins:]
        own[:, at] = back(grad[0], weight[at])


def near_parts(grad, weight):
    _, rows, tracks = grad.shape
    channels = weight.shape[0]
    half = (rows - EDGE) // 2
    outs = [struct(rows, channels)] + [struct(half, channels, BF16)] * 2
    outs += [struct(half, channels)] * 2 + [struct(EDGE, channels)] * 2
    return call("near_parts", near_kernel, (grad, weight), outs, 6 * rows * channels * tracks)


def join_kernel(lo_sum, hi_sum, below_more, above_more, up, down, to_up, to_down, loss):
    half = lo_sum.shape[0]
    row = lax.broadcasted_iota(jnp.int32, (EDGE, lo_sum.shape[1]), 0)
    block = up[half:].astype(F32)
    to_up[:half] = (lo_sum[...] + up[:half].astype(F32)).astype(BF16)
    to_up[half:] = jnp.where(row < 2, above_more[...] + block, block).astype(BF16)
    to_down[:half] = (hi_sum[...] + down[:half].astype(F32)).astype(BF16)
    to_down[half:] = jnp.where(row < 2, below_more[...] + down[half:].astype(F32), 0.0).astype(BF16)
    loss[...] = jnp.broadcast_to(loss_of(up[half:]) + loss_of(down[half:]), loss.shape)


def join(*arrays):
    rows, channels = arrays[-1].shape
    outs = [struct(rows, channels, BF16)] * 2 + [struct(8, 128)]
    return call("join", join_kernel, arrays, outs, rows * channels)


def core_sum_kernel(mine, other, keep, above, below, lo, hi):
    size, half = keep.shape[0], lo.shape[0]

    def part(start, count):
        return mine[start : start + count] + other[start : start + count].astype(F32)

    keep[...] = part(0, size)
    above[...] = part(size, size)
    lo[...] = part(2 * size, half).astype(BF16)
    hi[...] = part(2 * size + half, half).astype(BF16)
    below[...] = part(3 * size, size)


def core_sum(mine, other):
    rows, tracks = mine.shape
    size = rows // X
    outs = [struct(size, tracks)] * 3 + [struct(size // 2, tracks, BF16)] * 2
    return call("core_sum", core_sum_kernel, (mine, other), outs, rows * tracks)


def pass_kernel(above, below, up, down, to_up, to_down):
    half = up.shape[0]
    to_up[:half] = (above[:half] + up[...].astype(F32)).astype(BF16)
    to_up[half:] = above[half:].astype(BF16)
    to_down[:half] = below[:half].astype(BF16)
    to_down[half:] = (below[half:] + down[...].astype(F32)).astype(BF16)


def pass_on(above, below, up, down):
    outs = [struct(*above.shape, BF16)] * 2
    return call("pass_on", pass_kernel, (above, below, up, down), outs, 2 * math.prod(above.shape))


def slope_kernel(mixed, low, high, taps, out):
    row = lax.broadcasted_iota(jnp.int32, (EDGE, 256), 0)
    for at in tiles(mixed.shape[1], 256):
        below, above = low[:, at].astype(F32), high[:, at].astype(F32)
        below = jnp.where(row == EDGE - 1, below[0:1], jnp.where(row == EDGE - 2, below[1:2], 0.0))
        above = jnp.where(row < 2, above, 0.0)
        block = jnp.concatenate([below, mixed[:, at].astype(F32), above], axis=0)
        x = convolve(block, block[:1], block[:1], taps[:, at])
        square = x * x
        t = jnp.tanh(gelu_scale * (x + gelu_cube * (x * square)))
        slope = gelu_scale * (1.0 + 3.0 * gelu_cube * square)
        out[:, at] = 0.5 * (1.0 + t) + 0.5 * x * ((1.0 - t * t) * slope)


def slopes(mixed, low, high, taps):
    bins, channels = mixed.shape
    outs = [struct(bins + 2 * EDGE, channels)]
    flops = 40 * bins * channels
    return call("slopes", slope_kernel, (mixed, low, high, taps), outs, flops, transcendentals=bins * channels)[0]


def skip_kernel(denominator, place, own, up, down, hi, lo, slope, taps, own_loss, near_loss, out, loss):
    half = hi.shape[0]
    bins = 2 * half
    far = jnp.broadcast_to(loss_of(up[half:]), loss.shape)
    loss[...] = ((own_loss[...] + far) + near_loss[...]) / denominator
    index = (place[2] * Z + place[1]) * CORES + place[0]
    has_low = jnp.where(index == 0, 0.0, 1.0)
    has_high = jnp.where(index == X * Z * CORES - 1, 0.0, 1.0)
    row = lax.broadcasted_iota(jnp.int32, (EDGE, 256), 0)
    for at in tiles(own.shape[1], 256):
        tap = taps[:, at]
        first = own[:half, at] + (up[:half, at].astype(F32) + lo[:, at].astype(F32))
        second = own[half:bins, at] + (hi[:, at].astype(F32) + down[:half, at].astype(F32))
        more = own[bins:, at] + (up[half:, at].astype(F32) + down[half:, at].astype(F32))
        before = jnp.where(row == EDGE - 1, more[0:1] * has_low, 0.0)
        after_ = jnp.where(row == 0, more[1:2] * has_high, 0.0)
        pre = jnp.concatenate([before, first, second, after_], axis=0) * slope[:, at]
        turned = jnp.concatenate([tap[2:3], tap[1:2], tap[0:1]], axis=0)
        result = convolve(pre, pre[:1], pre[:1], turned)
        out[0, :, at] = result[EDGE : EDGE + bins].astype(BF16)


def skip_gradient(denominator, *arrays):
    bins, channels = 2 * arrays[4].shape[0], arrays[4].shape[1]
    outs = [jax.ShapeDtypeStruct((1, bins, channels), BF16), struct(8, 128)]
    kernel = functools.partial(skip_kernel, denominator)
    return call("skip_gradient", kernel, arrays, outs, 12 * bins * channels, scalars=1)


def after(value, *others):
    return lax.optimization_barrier((value, *others))[0]


def shards(coarse_input, skip_input, depth_kernel, head_weight, head_bias, coverage):
    rep_count, seq_count = REP, X * Z * CORES
    denominator = (
        coverage.shape[0] * (head_weight.shape[1] * rep_count) * (coverage.shape[1] * seq_count)
    )
    factor = loss_scale / denominator
    rep, seq = lax.axis_index("rep"), lax.axis_index("seq")
    tracks = head_weight.shape[1]
    bias = head_bias[None]
    sums = jnp.zeros((72, 128), F32)

    order = jnp.stack([rep, (rep + REP - 1) % REP, (rep + 1) % REP, (rep + 2) % REP]).astype(jnp.int32)
    place = jnp.stack([seq % CORES, (seq // CORES) % Z, seq // (CORES * Z)]).astype(jnp.int32)
    coarse, order, place, sums, bias = lax.optimization_barrier(
        (coarse_input[0], order, place, sums, bias)
    )

    def head_of(slot, parts, rows, sums):
        return head(slot, order, parts, rows, head_weight, bias, coverage, low, high, sums)

    mixed, up, down = mix(coarse, skip_input[0], depth_kernel)
    bins, most = mixed.shape[0], up.shape[0]
    half, more = bins // 2, SPARE + EDGE
    below_up, above_down = move_rep(up, 1), move_rep(down, -1)
    low, high = halo(*pack(mixed, coverage))
    edges, more_up, more_down = edge_rows(mixed, low, high, depth_kernel, up, down)
    below_more, above_more = move_rep(more_up, 1), move_rep(more_down, -1)
    rows = ((0, 0, half), (1, most - half, most), (2, 0, EDGE))
    own_head = head_of(0, (up, down, edges), rows, sums)
    ready = (own_head[2], below_more, above_more)
    across_a = move_rep(after(below_up, more_up)[:half], 1)
    across_b = move_rep(after(above_down, more_up)[most - half :], -1)
    across_e = move_rep(edges, 2)
    rows = ((0, 0, most), (1, 0, SPARE), (1, SPARE, more))
    below_head = head_of(1, (below_up, below_more), rows, after(*ready))
    rows = ((1, 0, SPARE), (0, 0, most), (1, SPARE, more))
    above_head = head_of(2, (above_down, above_more), rows, below_head[2])
    rows = ((0, 0, half), (1, 0, half), (2, 0, EDGE))
    across_head = head_of(3, (across_a, across_b, across_e), rows, above_head[2])
    heads = (own_head, below_head, above_head, across_head)
    totals = seq_sum(across_head[2])
    sigs, lins, _, turned = zip(*heads)
    grad, mine, other = weight_parts(factor, place, sigs, lins, turned, totals)
    other = move_core(other)
    part_lo, part_hi, own_loss = across_part(grad, head_weight, totals)
    up, down = move_rep(part_lo, 1), move_rep(part_hi, -1)
    keep, next_x, last_x, far_lo, far_hi = core_sum(mine, after(other, part_lo))
    far_lo, far_hi = move_x(far_lo, 1), move_x(far_hi, -1)
    own, lo, hi, *sums = near_parts(after(grad, keep), head_weight)
    hi, lo = move_rep(hi, 1), move_rep(lo, -1)
    next_x, last_x = pass_on(after(next_x, own), last_x, far_lo, far_hi)
    from_last, from_next = move_x(next_x, 1), move_x(last_x, -1)
    slope = slopes(after(mixed, next_x), low, high, depth_kernel)
    to_up, to_down, near_loss = join(after(sums[0], next_x), *sums[1:], up, down)
    up, down = move_rep(to_up, 1), move_rep(to_down, -1)
    keep = after(keep, to_up, hi, lo, slope)
    keep = keep + (from_last.astype(F32) + from_next.astype(F32))
    for bits in (1, 6, 2):
        half = keep.shape[0] // 2
        sent = keep[half:].astype(BF16)
        if bits == 2:
            sent = after(sent, up, down)
        keep = keep[:half] + flip_z(sent, bits).astype(F32)
    arrays = (up, down, hi, lo, slope, depth_kernel, own_loss, near_loss)
    skip_grad, loss = skip_gradient(denominator, place, after(own, sent), *arrays)
    return (loss[0, 0], keep, skip_grad)


def solution(mesh):
    return jax.shard_map(
        shards,
        mesh=mesh,
        in_specs=(
            P("rep", "seq", None),
            P("rep", "seq", None),
            P(),
            P(None, "rep"),
            P("rep"),
            P(None, "seq", "rep"),
        ),
        out_specs=(P(), P("seq", "rep"), P("rep", "seq", None)),
        check_vma=False,
    )
```

```python
import functools
import math

import jax
import jax.numpy as jnp
from jax import lax
from jax.experimental import pallas as pl
from jax.experimental.pallas import tpu as pltpu
from jax.sharding import PartitionSpec as P

loss_scale = 4194304.0
total_weight = 0.2
X, Z, CORES, REP = 4, 8, 2, 4


def seq_index(x, z, c):
    return (x * Z + z) * CORES + c


def seq_move(block, to, cores=CORES):
    pairs = [
        (seq_index(x, z, c), seq_index(*to(x, z, c)))
        for x in range(X)
        for z in range(Z)
        for c in range(cores)
    ]
    return lax.ppermute(block, "seq", pairs)


def move_x(block, step):
    return seq_move(block, lambda x, z, c: ((x + step) % X, z, c))


def flip_z(block, bits):
    return seq_move(block, lambda x, z, c: (x, z ^ bits, c))


def move_core(block):
    return seq_move(block, lambda x, z, c: (x, z, 1 - c))


def move_rep(block, step):
    return lax.ppermute(block, "rep", [(i, (i + step) % REP) for i in range(REP)])


def halo(low_row, high_row):
    count = X * Z * CORES
    up = [(i, i + 1) for i in range(count - 1)]
    down = [(target, source) for source, target in up]
    return lax.ppermute(high_row, "seq", up), lax.ppermute(low_row, "seq", down)


def seq_sum(block, first_core):
    rounds = (
        (
            lambda x, z, c: (x, z, 1 - c),
            lambda x, z, c: (x, z ^ 1, c),
            lambda x, z, c: (x, z ^ 1, 1 - c),
        ),
        tuple(lambda x, z, c, k=k: ((x + k) % X, z, c) for k in (1, 2, 3)),
    )
    for n, moves in enumerate(rounds):
        parts = [seq_move(block, to, CORES - n) for to in moves]
        block = (block + parts[0]) + (parts[1] + parts[2])
    for bits in (6, 2):
        block = block + seq_move(block, lambda x, z, c: (x, z ^ bits, c), 1)
    return block * first_core + seq_move(block, lambda x, z, c: (x, z, 1), 1)


F32, BF16 = jnp.float32, jnp.bfloat16
gelu_scale, gelu_cube = math.sqrt(2.0 / math.pi), 0.044715
EDGE, SPARE = 16, 64


def dot(a, b):
    return jnp.dot(a, b, preferred_element_type=F32)


def struct(rows, columns, dtype=F32):
    return jax.ShapeDtypeStruct((rows, columns), dtype)


def call(name, kernel, arrays, outs, flops, scalars=0, scratch=(), transcendentals=0):
    nbytes = sum(math.prod(a.shape) * a.dtype.itemsize for a in (*arrays, *outs))
    smem = pl.BlockSpec(memory_space=pltpu.SMEM)
    vmem = pl.BlockSpec(memory_space=pltpu.VMEM)
    return pl.pallas_call(
        kernel,
        in_specs=[smem] * scalars + [vmem] * (len(arrays) - scalars),
        out_specs=[vmem] * len(outs),
        out_shape=list(outs),
        scratch_shapes=list(scratch),
        compiler_params=pltpu.CompilerParams(vmem_limit_bytes=14 << 20),
        cost_estimate=pl.CostEstimate(
            flops=flops, bytes_accessed=nbytes, transcendentals=transcendentals
        ),
        name=name,
    )(*arrays)


def pinned(rows, columns, dtype=F32):
    return pltpu.VMEM((rows, columns), dtype)


def tiles(extent, width):
    return [slice(start, start + width) for start in range(0, extent, width)]


def previous(block, edge):
    rows = lax.broadcasted_iota(jnp.int32, block.shape, 0)
    return jnp.where(rows == 0, edge, pltpu.roll(block, 1, 0))


def following(block, edge):
    count = block.shape[0]
    rows = lax.broadcasted_iota(jnp.int32, block.shape, 0)
    return jnp.where(rows == count - 1, edge, pltpu.roll(block, count - 1, 0))


def convolve(block, low, high, taps):
    return taps[0:1] * previous(block, low) + taps[1:2] * block + taps[2:3] * following(block, high)


def mix_kernel(coarse_far, skip_far, taps, mixed, up, down, coarse, skip, arrived):
    copies = []
    for n, at in enumerate(tiles(skip.shape[1], 512)):
        for k, (far, near) in enumerate(((coarse_far, coarse), (skip_far, skip))):
            copies.append(pltpu.make_async_copy(far.at[:, at], near.at[:, at], arrived.at[n, k]))
            copies[-1].start()
    bins, fine = skip.shape[0], skip.shape[0] // 2
    row = lax.broadcasted_iota(jnp.int32, (bins, fine), 0)
    column = lax.broadcasted_iota(jnp.int32, (bins, fine), 1)
    twice = jnp.where((row == 2 * column) | (row == 2 * column + 1), 1.0, 0.0).astype(BF16)
    for n, at in enumerate(tiles(skip.shape[1], 512)):
        copies[2 * n].wait()
        copies[2 * n + 1].wait()
        out = (dot(twice, coarse[:, at]) + skip[:, at].astype(F32)).astype(BF16)
        mixed[:, at] = out
        block = out.astype(F32)
        hidden = jax.nn.gelu(convolve(block, block[:1], block[:1], taps[:, at])).astype(BF16)
        up[:, at] = hidden[: bins - SPARE]
        down[:, at] = hidden[SPARE:]


def mix(coarse, skip, taps):
    bins, channels = skip.shape
    most = struct(bins - SPARE, channels, BF16)
    outs = [struct(bins, channels, BF16), most, most]
    vmem, far = pl.BlockSpec(memory_space=pltpu.VMEM), pl.BlockSpec(memory_space=pltpu.HBM)
    return pl.pallas_call(
        mix_kernel,
        in_specs=[far, far, vmem],
        out_specs=[vmem] * 3,
        out_shape=outs,
        scratch_shapes=[
            pltpu.VMEM(coarse.shape, BF16),
            pltpu.VMEM(skip.shape, BF16),
            pltpu.SemaphoreType.DMA((3, 2)),
        ],
        compiler_params=pltpu.CompilerParams(vmem_limit_bytes=14 << 20),
        cost_estimate=pl.CostEstimate(
            flops=bins * bins * channels,
            bytes_accessed=7 * bins * channels,
            transcendentals=bins * channels,
        ),
        name="mix",
    )(*(pltpu.with_memory_space_constraint(x, pltpu.HBM) for x in (coarse, skip)), taps)


def block_of(*rows):
    row = lax.broadcasted_iota(jnp.int32, (EDGE, rows[0].shape[1]), 0)
    out = jnp.zeros(row.shape, F32)
    for n, value in enumerate(rows):
        out = jnp.where(row == n, value, out)
    return out


def pack_kernel(mixed, coverage, first, last):
    bins, channels = mixed.shape
    top, bottom = mixed[:EDGE].astype(F32), mixed[bins - EDGE :].astype(F32)
    pad = jnp.zeros((1, channels - coverage.shape[2]), F32)
    low, high = [top[0:1], top[1:2]], [bottom[EDGE - 1 :], bottom[EDGE - 2 : EDGE - 1]]
    for s in range(coverage.shape[0]):
        row = coverage[s, :EDGE].astype(F32)[:1]
        low.append(jnp.concatenate([row, pad], axis=1))
        row = coverage[s, bins - EDGE :].astype(F32)[EDGE - 1 :]
        high.append(jnp.concatenate([row, pad], axis=1))
    first[...] = block_of(*low).astype(BF16)
    last[...] = block_of(*high).astype(BF16)


def pack(mixed, coverage):
    outs = [struct(EDGE, mixed.shape[1], BF16)] * 2
    return call("pack", pack_kernel, (mixed, coverage), outs, 1000 * mixed.shape[1])


def edge_kernel(mixed, low, high, taps, up, down, edges, more_up, more_down):
    bins = mixed.shape[0]
    start, end = mixed[:EDGE].astype(F32), mixed[bins - EDGE :].astype(F32)
    below, above = low[...].astype(F32), high[...].astype(F32)
    near = [below[1:2], below[0:1], start[0:1], start[1:2]]
    far = [end[EDGE - 2 : EDGE - 1], end[EDGE - 1 :], above[0:1], above[1:2]]
    rows = [
        taps[0:1] * a + taps[1:2] * b + taps[2:3] * c
        for a, b, c in (near[1:], far[:3], near[:3], far[1:])
    ]
    block = jax.nn.gelu(block_of(*rows)).astype(BF16)
    edges[...] = block
    more_up[:SPARE] = down[down.shape[0] - SPARE :]
    more_up[SPARE:] = block
    more_down[:SPARE] = up[:SPARE]
    more_down[SPARE:] = block


def edge_rows(mixed, low, high, taps, up, down):
    channels = mixed.shape[1]
    more = struct(SPARE + EDGE, channels, BF16)
    outs = [struct(EDGE, channels, BF16), more, more]
    return call("edges", edge_kernel, (mixed, low, high, taps, up, down), outs, 1000 * channels)


def log1p(e):
    series = e * (1 + e * (-1 / 2 + e * (1 / 3 + e * (-1 / 4 + e * (1 / 5 - e / 6)))))
    return jnp.where(e < 0.05, series, jnp.log(1 + e))


def head_kernel(slot, count, rows, *refs):
    order, parts = refs[0], refs[1 : 1 + count]
    weight, bias, coverage, low, high, sums, sig, lin, totals, turned, held = refs[1 + count :]
    bins = coverage.shape[1]
    nth = lax.broadcasted_iota(jnp.int32, (EDGE, 256), 0)
    held[:bins] = jnp.concatenate([parts[n][start:stop] for n, start, stop in rows[:-1]], axis=0)
    n, start, stop = rows[-1]
    edges = parts[n][start:stop].astype(F32)
    line = lax.broadcasted_iota(jnp.int32, edges.shape, 0)
    top, bottom = held[:EDGE].astype(F32), held[bins - EDGE : bins].astype(F32)
    held[:EDGE] = jnp.where(line == 0, edges[0:1], top).astype(BF16)
    held[bins - EDGE : bins] = jnp.where(line == EDGE - 1, edges[1:2], bottom).astype(BF16)
    held[bins:] = block_of(edges[2:3], edges[3:4]).astype(BF16)
    turned[...] = held[:bins].T
    totals[...] = sums[...]
    sequence = order[slot]
    for n, at in enumerate(tiles(weight.shape[1], 256)):
        logits = dot(held[...], weight[:, at]) + bias[:, at]
        e = jnp.exp(-jnp.abs(logits))
        predicted = jnp.maximum(logits, 0.0) + log1p(e)
        beside = [
            jnp.sum(jnp.where(nth == 2 + sequence, side[:, at].astype(F32), 0.0), axis=0, keepdims=True)
            for side in (low, high)
        ]
        target = jnp.concatenate([coverage[sequence, :, at].astype(F32), block_of(*beside)], axis=0)
        common = jnp.where(logits >= 0, 1.0, e) / (predicted * (1.0 + e))
        sigmoid = predicted * common
        sig[:, at] = sigmoid
        lin[:, at] = total_weight * sigmoid - target * common
        values = (predicted, target, target * jnp.log(predicted))
        for where, value in zip((16 * slot, 16 * slot + 8, 64), values):
            total = jnp.sum(value[:bins], axis=0, keepdims=True)
            for half in range(2):
                row = slice(where + 2 * n + half, where + 2 * n + half + 1)
                totals[row] = sums[row] + total[:, 128 * half : 128 * (half + 1)]


def head(slot, order, parts, rows, weight, bias, coverage, low, high, sums):
    channels, tracks = weight.shape
    bins = coverage.shape[1]
    terms = pinned(bins + EDGE, tracks)
    outs = [terms, terms, struct(72, 128), pinned(channels, bins, BF16)]
    return call(
        "head",
        functools.partial(head_kernel, slot, len(parts), rows),
        (order, *parts, weight, bias, coverage, low, high, sums),
        outs,
        2 * bins * channels * tracks,
        scalars=1,
        scratch=[pltpu.VMEM((bins + EDGE, channels), BF16)],
        transcendentals=4 * bins * tracks,
    )


def weight_kernel(factor, place, *refs):
    sigs, lins, turned = refs[:4], refs[4:8], refs[8:12]
    totals, grad, mine, other, total, across = refs[12:]
    own = total.shape[0] // (X * Z * CORES)
    core, z, x = place[0], place[1], place[2]

    def rows(n, c, j):
        k, bits = j // 8, (0, 2, 6, 4, 1, 3, 7, 5)[j % 8]
        to_x = lax.rem(x + k, X)
        to_z = lax.bitwise_xor(z, bits)
        start = ((to_x * Z + to_z) * CORES + c) * own
        return total[pl.ds(pl.multiple_of(start, 8), own), :]

    bins = turned[0].shape[1]
    for slot in range(4):
        across[:, slot * bins : (slot + 1) * bins] = turned[slot][...]
    for n, at in enumerate(tiles(grad.shape[2], 256)):
        parts = []
        for slot in range(4):
            ratio = []
            for row in (16 * slot + 2 * n, 16 * slot + 2 * n + 1):
                ratio.append(totals[row + 8 : row + 9] / totals[row : row + 1])
            ratio = jnp.concatenate(ratio, axis=1)
            part = factor * lins[slot][:, at] + (factor * (1.0 - total_weight) * ratio) * sigs[slot][:, at]
            part = part.astype(BF16)
            grad[slot, :, at] = part
            parts.append(part[:bins])
        total[...] = dot(across[...], jnp.concatenate(parts, axis=0))
        for j in range(0, X * Z, 2):
            to = slice(j * own, (j + 2) * own)
            mine[to, at] = jnp.concatenate([rows(n, core, j), rows(n, core, j + 1)], axis=0)
            away = jnp.concatenate([rows(n, 1 - core, j), rows(n, 1 - core, j + 1)], axis=0)
            other[to, at] = away.astype(BF16)


def weight_parts(factor, place, sigs, lins, turned, totals):
    bins, tracks = sigs[0].shape
    channels = turned[0].shape[0]
    half = channels // CORES
    outs = [
        jax.ShapeDtypeStruct((4, bins, tracks), BF16),
        struct(half, tracks),
        struct(half, tracks, BF16),
    ]
    return call(
        "weight_parts",
        functools.partial(weight_kernel, factor),
        (place, *sigs, *lins, *turned, totals),
        outs,
        8 * bins * channels * tracks,
        scalars=1,
        scratch=[pltpu.VMEM((channels, 256), F32), pltpu.VMEM((channels, 4 * turned[0].shape[1]), BF16)],
    )


def back(grad, weight):
    return lax.dot_general(grad, weight, (((1,), (1,)), ((), ())), preferred_element_type=F32)


def loss_terms(totals):
    total = -totals[64:]
    for slot in range(4):
        predicted, target = totals[16 * slot : 16 * slot + 8], totals[16 * slot + 8 : 16 * slot + 16]
        log_total = jnp.log(predicted)
        terms = total_weight * (predicted - target * log_total) + target * log_total
        total = total + terms
    return jnp.sum(total, keepdims=True)


def three_of(value, columns):
    one = value.astype(BF16).astype(F32)
    two = (value - one).astype(BF16).astype(F32)
    return [jnp.broadcast_to(v, (1, columns)) for v in (one, two, (value - one) - two)]


def loss_of(block):
    rows = block[:, :128].astype(F32)
    return rows[2:3] + (rows[3:4] + rows[4:5])


def across_kernel(grad, weight, totals, lo, hi, loss):
    half = lo.shape[0] - EDGE
    bins = 2 * half
    value = loss_terms(totals)
    loss[...] = jnp.broadcast_to(value, loss.shape)
    for at in tiles(weight.shape[0], 512):
        out = back(grad[3], weight[at])
        rows = three_of(value, 512)
        none = jnp.zeros_like(rows[0])
        lo[:half, at] = out[:half].astype(BF16)
        hi[:half, at] = out[half:bins].astype(BF16)
        lo[half:, at] = block_of(out[bins : bins + 1], none, *rows).astype(BF16)
        hi[half:, at] = block_of(none, out[bins + 1 : bins + 2], *rows).astype(BF16)


def across_part(grad, weight, totals):
    _, rows, tracks = grad.shape
    channels = weight.shape[0]
    outs = [struct(rows // 2 + EDGE // 2, channels, BF16)] * 2 + [struct(8, 128)]
    arrays = (grad, weight, totals)
    return call("across_part", across_kernel, arrays, outs, 2 * rows * channels * tracks)


def near_kernel(grad, weight, own, lo, hi, lo_sum, hi_sum, below_more, above_more):
    half = lo.shape[0]
    bins = 2 * half
    for at in tiles(weight.shape[0], 512):
        out = back(grad[2], weight[at])
        lo_sum[:, at] = out[:half]
        hi[:, at] = out[half:bins].astype(BF16)
        above_more[:, at] = out[bins:]
        out = back(grad[1], weight[at])
        lo[:, at] = out[:half].astype(BF16)
        hi_sum[:, at] = out[half:bins]
        below_more[:, at] = out[bins:]
        own[:, at] = back(grad[0], weight[at])


def near_parts(grad, weight):
    _, rows, tracks = grad.shape
    channels = weight.shape[0]
    half = (rows - EDGE) // 2
    outs = [struct(rows, channels)] + [struct(half, channels, BF16)] * 2
    outs += [struct(half, channels)] * 2 + [struct(EDGE, channels)] * 2
    return call("near_parts", near_kernel, (grad, weight), outs, 6 * rows * channels * tracks)


def join_kernel(lo_sum, hi_sum, below_more, above_more, up, down, to_up, to_down, loss):
    half = lo_sum.shape[0]
    row = lax.broadcasted_iota(jnp.int32, (EDGE, lo_sum.shape[1]), 0)
    block = up[half:].astype(F32)
    to_up[:half] = (lo_sum[...] + up[:half].astype(F32)).astype(BF16)
    to_up[half:] = jnp.where(row < 2, above_more[...] + block, block).astype(BF16)
    to_down[:half] = (hi_sum[...] + down[:half].astype(F32)).astype(BF16)
    to_down[half:] = jnp.where(row < 2, below_more[...] + down[half:].astype(F32), 0.0).astype(BF16)
    loss[...] = jnp.broadcast_to(loss_of(up[half:]) + loss_of(down[half:]), loss.shape)


def join(*arrays):
    rows, channels = arrays[-1].shape
    outs = [struct(rows, channels, BF16)] * 2 + [struct(8, 128)]
    return call("join", join_kernel, arrays, outs, rows * channels)


def core_sum_kernel(mine, other, keep, above, below, lo, hi):
    size, half = keep.shape[0], lo.shape[0]

    def part(start, count):
        return mine[start : start + count] + other[start : start + count].astype(F32)

    keep[...] = part(0, size)
    above[...] = part(size, size)
    lo[...] = part(2 * size, half).astype(BF16)
    hi[...] = part(2 * size + half, half).astype(BF16)
    below[...] = part(3 * size, size)


def core_sum(mine, other):
    rows, tracks = mine.shape
    size = rows // X
    outs = [struct(size, tracks)] * 3 + [struct(size // 2, tracks, BF16)] * 2
    return call("core_sum", core_sum_kernel, (mine, other), outs, rows * tracks)


def pass_kernel(above, below, up, down, to_up, to_down):
    half = up.shape[0]
    to_up[:half] = (above[:half] + up[...].astype(F32)).astype(BF16)
    to_up[half:] = above[half:].astype(BF16)
    to_down[:half] = below[:half].astype(BF16)
    to_down[half:] = (below[half:] + down[...].astype(F32)).astype(BF16)


def pass_on(above, below, up, down):
    outs = [struct(*above.shape, BF16)] * 2
    return call("pass_on", pass_kernel, (above, below, up, down), outs, 2 * math.prod(above.shape))


def slope_kernel(mixed, low, high, taps, out):
    row = lax.broadcasted_iota(jnp.int32, (EDGE, 256), 0)
    for at in tiles(mixed.shape[1], 256):
        below, above = low[:, at].astype(F32), high[:, at].astype(F32)
        below = jnp.where(row == EDGE - 1, below[0:1], jnp.where(row == EDGE - 2, below[1:2], 0.0))
        above = jnp.where(row < 2, above, 0.0)
        block = jnp.concatenate([below, mixed[:, at].astype(F32), above], axis=0)
        x = convolve(block, block[:1], block[:1], taps[:, at])
        square = x * x
        t = jnp.tanh(gelu_scale * (x + gelu_cube * (x * square)))
        slope = gelu_scale * (1.0 + 3.0 * gelu_cube * square)
        out[:, at] = 0.5 * (1.0 + t) + 0.5 * x * ((1.0 - t * t) * slope)


def slopes(mixed, low, high, taps):
    bins, channels = mixed.shape
    outs = [struct(bins + 2 * EDGE, channels)]
    flops = 40 * bins * channels
    return call("slopes", slope_kernel, (mixed, low, high, taps), outs, flops, transcendentals=bins * channels)[0]


def skip_kernel(denominator, place, own, up, down, hi, lo, slope, taps, own_loss, near_loss, out, loss):
    half = hi.shape[0]
    bins = 2 * half
    far = jnp.broadcast_to(loss_of(up[half:]), loss.shape)
    loss[...] = ((own_loss[...] + far) + near_loss[...]) / denominator
    index = (place[2] * Z + place[1]) * CORES + place[0]
    has_low = jnp.where(index == 0, 0.0, 1.0)
    has_high = jnp.where(index == X * Z * CORES - 1, 0.0, 1.0)
    row = lax.broadcasted_iota(jnp.int32, (EDGE, 256), 0)
    for at in tiles(own.shape[1], 256):
        tap = taps[:, at]
        first = own[:half, at] + (up[:half, at].astype(F32) + lo[:, at].astype(F32))
        second = own[half:bins, at] + (hi[:, at].astype(F32) + down[:half, at].astype(F32))
        more = own[bins:, at] + (up[half:, at].astype(F32) + down[half:, at].astype(F32))
        before = jnp.where(row == EDGE - 1, more[0:1] * has_low, 0.0)
        after_ = jnp.where(row == 0, more[1:2] * has_high, 0.0)
        pre = jnp.concatenate([before, first, second, after_], axis=0) * slope[:, at]
        turned = jnp.concatenate([tap[2:3], tap[1:2], tap[0:1]], axis=0)
        result = convolve(pre, pre[:1], pre[:1], turned)
        out[0, :, at] = result[EDGE : EDGE + bins].astype(BF16)


def skip_gradient(denominator, *arrays):
    bins, channels = 2 * arrays[4].shape[0], arrays[4].shape[1]
    outs = [jax.ShapeDtypeStruct((1, bins, channels), BF16), struct(8, 128)]
    kernel = functools.partial(skip_kernel, denominator)
    return call("skip_gradient", kernel, arrays, outs, 12 * bins * channels, scalars=1)


def after(value, *others):
    return lax.optimization_barrier((value, *others))[0]


def shards(coarse_input, skip_input, depth_kernel, head_weight, head_bias, coverage):
    rep_count, seq_count = REP, X * Z * CORES
    denominator = (
        coverage.shape[0] * (head_weight.shape[1] * rep_count) * (coverage.shape[1] * seq_count)
    )
    factor = loss_scale / denominator
    rep, seq = lax.axis_index("rep"), lax.axis_index("seq")
    tracks = head_weight.shape[1]
    bias = head_bias[None]
    sums = jnp.zeros((72, 128), F32)

    order = jnp.stack([rep, (rep + REP - 1) % REP, (rep + 1) % REP, (rep + 2) % REP]).astype(jnp.int32)
    place = jnp.stack([seq % CORES, (seq // CORES) % Z, seq // (CORES * Z)]).astype(jnp.int32)
    first_core = jnp.broadcast_to((1 - place[0]).astype(F32), sums.shape)
    coarse, order, place, sums, bias, first_core = lax.optimization_barrier(
        (coarse_input[0], order, place, sums, bias, first_core)
    )

    def head_of(slot, parts, rows, sums):
        return head(slot, order, parts, rows, head_weight, bias, coverage, low, high, sums)

    mixed, up, down = mix(coarse, skip_input[0], depth_kernel)
    bins, most = mixed.shape[0], up.shape[0]
    half, more = bins // 2, SPARE + EDGE
    below_up, above_down = move_rep(up, 1), move_rep(down, -1)
    low, high = halo(*pack(mixed, coverage))
    edges, more_up, more_down = edge_rows(mixed, low, high, depth_kernel, up, down)
    below_more, above_more = move_rep(more_up, 1), move_rep(more_down, -1)
    rows = ((0, 0, half), (1, most - half, most), (2, 0, EDGE))
    own_head = head_of(0, (up, down, edges), rows, sums)
    ready = (own_head[2], below_more, above_more)
    across_a = move_rep(after(below_up, more_up)[:half], 1)
    across_b = move_rep(after(above_down, more_up)[most - half :], -1)
    across_e = move_rep(edges, 2)
    rows = ((0, 0, most), (1, 0, SPARE), (1, SPARE, more))
    below_head = head_of(1, (below_up, below_more), rows, after(*ready))
    rows = ((1, 0, SPARE), (0, 0, most), (1, SPARE, more))
    above_head = head_of(2, (above_down, above_more), rows, below_head[2])
    rows = ((0, 0, half), (1, 0, half), (2, 0, EDGE))
    across_head = head_of(3, (across_a, across_b, across_e), rows, above_head[2])
    heads = (own_head, below_head, above_head, across_head)
    totals = seq_sum(across_head[2], first_core)
    sigs, lins, _, turned = zip(*heads)
    grad, mine, other = weight_parts(factor, place, sigs, lins, turned, totals)
    other = move_core(other)
    part_lo, part_hi, own_loss = across_part(grad, head_weight, totals)
    up, down = move_rep(part_lo, 1), move_rep(part_hi, -1)
    keep, next_x, last_x, far_lo, far_hi = core_sum(mine, after(other, part_lo))
    far_lo, far_hi = move_x(far_lo, 1), move_x(far_hi, -1)
    own, lo, hi, *sums = near_parts(after(grad, keep), head_weight)
    hi, lo = move_rep(hi, 1), move_rep(lo, -1)
    next_x, last_x = pass_on(after(next_x, own), last_x, far_lo, far_hi)
    from_last, from_next = move_x(next_x, 1), move_x(last_x, -1)
    slope = slopes(after(mixed, next_x), low, high, depth_kernel)
    to_up, to_down, near_loss = join(after(sums[0], next_x), *sums[1:], up, down)
    up, down = move_rep(to_up, 1), move_rep(to_down, -1)
    keep = after(keep, to_up, hi, lo, slope)
    keep = keep + (from_last.astype(F32) + from_next.astype(F32))
    for bits in (1, 6, 2):
        half = keep.shape[0] // 2
        sent = keep[half:].astype(BF16)
        if bits == 2:
            sent = after(sent, up, down)
        keep = keep[:half] + flip_z(sent, bits).astype(F32)
    arrays = (up, down, hi, lo, slope, depth_kernel, own_loss, near_loss)
    skip_grad, loss = skip_gradient(denominator, place, after(own, sent), *arrays)
    return (loss[0, 0], keep, skip_grad)


def solution(mesh):
    return jax.shard_map(
        shards,
        mesh=mesh,
        in_specs=(
            P("rep", "seq", None),
            P("rep", "seq", None),
            P(),
            P(None, "rep"),
            P("rep"),
            P(None, "seq", "rep"),
        ),
        out_specs=(P(), P("seq", "rep"), P("rep", "seq", None)),
        check_vma=False,
    )
```
